32 devices in a mesh: head: 4 (over y, x), batch: 8 (over z, core).
Axes of the slice: x: 2, y: 2, z: 4, core: 2. Of those that a mesh axis runs over, the one named last changes fastest.
Arguments:
- tokens: bfloat16 [384, 196, 256], P('batch'), may hold values from -6 to 6
- image_count: int32 [8], P('batch'), may hold values from 16 to 48, as said below
- token_place: int32 [196], replicated, may hold values from 0 to 195, each once
- qkv_weight: float32 [4, 128, 256], P('head'), may hold values from -0.375 to 0.375
- bias_table: float32 [4, 196], P('head'), may hold values from -4 to 4
- proj_weight: float32 [256, 256], replicated, may hold values from -0.375 to 0.375
- attention_gain: float32 [256], replicated, may hold values from 0.5 to 1.5
- attention_shift: float32 [256], replicated, may hold values from -3 to 3
- up_weight: float32 [256, 512], P(None, 'head'), may hold values from -0.375 to 0.375
- hidden_gain: float32 [512], P('head'), may hold values from 0.5 to 1.5
- hidden_shift: float32 [512], P('head'), may hold values from -3 to 3
- down_weight: float32 [512, 256], P('head'), may hold values from -0.25 to 0.25
- output_gain: float32 [256], replicated, may hold values from 0.5 to 1.5
- output_shift: float32 [256], replicated, may hold values from -3 to 3
- cotangent: bfloat16 [384, 196, 256], P('batch', 'head'), may hold values from -6 to 6
Outputs:
- output: float32 [384, 196, 256], P('batch', 'head')
- tokens_grad: float32 [384, 196, 256], P('batch', 'head')
- qkv_grad: float32 [4, 128, 256], P('head')
- bias_grad: float32 [4, 196], P('head')
- proj_grad: float32 [256, 256], P('head')
- attention_gain_grad: float32 [256], replicated
- attention_shift_grad: float32 [256], replicated
- up_grad: float32 [256, 512], P(None, 'head')
- hidden_gain_grad: float32 [512], P('head')
- hidden_shift_grad: float32 [512], P('head')
- down_grad: float32 [512, 256], P('head')
- output_gain_grad: float32 [256], replicated
- output_shift_grad: float32 [256], replicated
The draws below stay inside these ranges and needn't reach their ends.
Inputs may be any that keep to these rules, and one draw needn't show every extreme that they name: Index b of batch holds image_count[b] real images in its first slots of 48; the other slots are padding that no statistic reads.
All inputs are finite; a program needn't handle non-finite values.
Results may differ from the reference program's by a relative error of at most 0.019.
The reference program's roundings to bfloat16 on the way count: a program that leaves them out, or rounds other values in their place, can miss the bound.
Values may be sent and summed in bfloat16 or wider, within the bound.
A program may use at most 192 MiB of HBM per device.

```python
import jax
import jax.numpy as jnp
from jax import lax

D = 256
HEADS = 4
KEY = 32
VAL = 64
HID = 512
SIDE = 14
IMG_DEV = 48
TOK = 196
OFFS = 196
IMGS = 384
N_BATCH = 8


def draw_image_count(key, part):
    key = jax.random.fold_in(key, 11)
    least = max(1, IMG_DEV // 3)
    places = jnp.arange(N_BATCH, dtype=jnp.int32)
    ramp = least + (IMG_DEV - least) * places // max(N_BATCH - 1, 1)
    jitter = jax.random.randint(key, (N_BATCH,), 0, max(2, (IMG_DEV - least) // 4 + 1))
    counts = jnp.clip(ramp - jitter, least, IMG_DEV)
    counts = counts.at[0].set(least).at[N_BATCH - 1].set(IMG_DEV)
    return counts.astype(jnp.int32)


def levels(own_key, extent, split, low, top_value):
    level = 1.0
    for axis_at, shards_of in split:
        heights = jax.random.uniform(jax.random.fold_in(jax.random.fold_in(own_key, 6), axis_at), (shards_of,), jnp.float32, low / len(split), top_value / len(split))
        level = level * jnp.repeat(jnp.exp(heights), extent[axis_at] // shards_of).reshape((-1,) + (1,) * (len(extent) - 1 - axis_at))
    return level


def normal_values(stream_key, extent, deviation, reach, pieces=(), held_as=jnp.bfloat16):
    drawn = jax.random.normal(stream_key, extent, jnp.float32) * deviation
    if len(pieces) > 0:
        drawn = levels(stream_key, extent, pieces, -0.22, 0.18) * drawn
    return jnp.clip(drawn, min=-reach, max=reach).astype(held_as)


def setup_inputs(seed: int = 0) -> dict:
    streams_of = jax.random.split(jax.random.key(seed), 16)
    tokens = normal_values(streams_of[0], (IMGS, TOK, D), 1.0, 6.0, ((0, 8),))
    image_count = draw_image_count(jax.random.fold_in(streams_of[15], 71), 0)
    token_place = jax.random.permutation(streams_of[2], TOK).astype(jnp.int32)
    qkv_weight = normal_values(streams_of[3], (HEADS, 2 * KEY + VAL, D), D ** -0.5, 0.375, ((0, 4),), jnp.float32)
    bias_table = normal_values(streams_of[4], (HEADS, OFFS), 1.0, 4.0, ((0, 4),), jnp.float32)
    proj_weight = normal_values(streams_of[5], (HEADS * VAL, D), (HEADS * VAL) ** -0.5, 0.375, (), jnp.float32)
    attention_gain = jnp.clip(1.0 + 0.1 * jax.random.normal(streams_of[6], (D,), jnp.float32), 0.5, 1.5)
    attention_shift = normal_values(streams_of[7], (D,), 0.5, 3.0, (), jnp.float32)
    up_weight = normal_values(streams_of[8], (D, HID), D ** -0.5, 0.375, ((1, 4),), jnp.float32)
    hidden_gain = jnp.clip(1.0 + 0.1 * jax.random.normal(streams_of[9], (HID,), jnp.float32), 0.5, 1.5)
    hidden_shift = normal_values(streams_of[10], (HID,), 0.5, 3.0, ((0, 4),), jnp.float32)
    down_weight = normal_values(streams_of[11], (HID, D), HID ** -0.5, 0.25, ((0, 4),), jnp.float32)
    output_gain = jnp.clip(1.0 + 0.1 * jax.random.normal(streams_of[12], (D,), jnp.float32), 0.5, 1.5)
    output_shift = normal_values(streams_of[13], (D,), 0.5, 3.0, (), jnp.float32)
    cotangent = normal_values(streams_of[14], (IMGS, TOK, D), 1.0, 6.0, ((0, 8), (1, 4)))
    return {"tokens": tokens, "image_count": image_count, "token_place": token_place, "qkv_weight": qkv_weight, "bias_table": bias_table, "proj_weight": proj_weight, "attention_gain": attention_gain, "attention_shift": attention_shift, "up_weight": up_weight, "hidden_gain": hidden_gain, "hidden_shift": hidden_shift, "down_weight": down_weight, "output_gain": output_gain, "output_shift": output_shift, "cotangent": cotangent}


@jax.custom_vjp
def low(v):
    return lax.optimization_barrier(v.astype(jnp.bfloat16)).astype(jnp.float32)

@jax.custom_vjp
def low_back(v):
    return v

def low_keep(v):
    return (low(v), None)

def low_pass(kept, grad):
    return (grad,)

def back_keep(v):
    return (v, None)

def back_low(kept, grad):
    return (low(grad),)
low.defvjp(low_keep, low_pass)
low_back.defvjp(back_keep, back_low)
epsilon = 1e-05
images_per_block = 16
highest = lax.Precision.HIGHEST

def silu(value):
    return value * jax.nn.sigmoid(value)

def reference(tokens, image_count, token_place, qkv_weight, bias_table, proj_weight, attention_gain, attention_shift, up_weight, hidden_gain, hidden_shift, down_weight, output_gain, output_shift, cotangent):
    images = IMG_DEV * N_BATCH
    slots = jnp.arange(images, dtype=jnp.int32)
    owners = (slots // IMG_DEV).astype(jnp.int32)
    valid = (slots % IMG_DEV < image_count[owners]).astype(jnp.float32)
    rows_valid = valid[:, None, None]
    seen = jnp.sum(valid) * TOK
    scaling = KEY ** (-0.5)
    grid_rows = (token_place // SIDE).astype(jnp.int32)
    grid_cols = (token_place % SIDE).astype(jnp.int32)
    offset_index = (jnp.abs(grid_rows[:, None] - grid_rows[None, :]) * SIDE + jnp.abs(grid_cols[:, None] - grid_cols[None, :])).astype(jnp.int32)

    def normalize(values, gain, shift):
        mean = lax.optimization_barrier(jnp.sum(values * rows_valid, axis=(0, 1))) / seen
        square = lax.optimization_barrier(jnp.sum(values * values * rows_valid, axis=(0, 1))) / seen
        inverse = lax.rsqrt(square - mean * mean + epsilon)
        return gain * ((values - mean) * inverse) + shift

    def forward(tokens_f, qkv_w, table, proj_w, gain_one, shift_one, up_w, gain_two, shift_two, down_w, gain_three, shift_three):
        qkv_low = low(qkv_w)
        proj_low = low(proj_w)
        up_low = low(up_w)
        down_low = low(down_w)
        position_bias = table[:, offset_index]

        def attend(block):
            mixed = jnp.einsum('itd,hcd->ithc', block, qkv_low, precision=highest)
            mixed = low_back(low(mixed))
            query = mixed[..., :KEY]
            key_part = mixed[..., KEY:2 * KEY]
            value_part = mixed[..., 2 * KEY:]
            scores = jnp.einsum('ithc,ishc->ihts', query, key_part, precision=highest) * scaling + position_bias[None]
            scores = low_back(scores)
            weights = jax.nn.softmax(scores, axis=-1)
            attended = jnp.einsum('ihts,ishc->ithc', low(weights), value_part, precision=highest)
            attended = low_back(attended)
            active = low(silu(attended)).reshape(block.shape[0], TOK, HEADS * VAL)
            return jnp.einsum('itc,cd->itd', active, proj_low, precision=highest)
        blocks = tokens_f.reshape(images // images_per_block, images_per_block, TOK, D)
        projected = lax.map(jax.checkpoint(attend), blocks).reshape(images, TOK, D)
        projected = low_back(projected)
        residual = tokens_f + normalize(projected, gain_one, shift_one)
        hidden = low_back(jnp.einsum('itd,df->itf', low(residual), up_low, precision=highest))
        active_two = low(silu(normalize(hidden, gain_two, shift_two)))
        outgoing = low_back(jnp.einsum('itf,fd->itd', active_two, down_low, precision=highest))
        return rows_valid * (residual + normalize(outgoing, gain_three, shift_three))
    tokens_f = tokens.astype(jnp.float32)
    output, pullback = jax.vjp(forward, tokens_f, qkv_weight, bias_table, proj_weight, attention_gain, attention_shift, up_weight, hidden_gain, hidden_shift, down_weight, output_gain, output_shift)
    grads = pullback(cotangent.astype(jnp.float32))
    return (output, grads[0], grads[1], grads[2], grads[3], grads[4], grads[5], grads[6], grads[7], grads[8], grads[9], grads[10], grads[11])
```

```python
import functools
import types

import jax
import jax.numpy as jnp
from jax import lax
from jax.experimental import pallas as pl
from jax.experimental.pallas import tpu as pltpu
from jax.sharding import PartitionSpec as P

KEY = 32
VAL = 64
SIDE = 14
EPSILON = 1e-05
LOG2E = 1.4426950408889634
MESH = pl.DeviceIdType.MESH
f32 = jnp.float32
bf16 = jnp.bfloat16


def nn(left, right):
    return lax.dot_general(left, right, (((1,), (0,)), ((), ())), preferred_element_type=f32)


def nt(left, right):
    return lax.dot_general(left, right, (((1,), (1,)), ((), ())), preferred_element_type=f32)


def round_up(value, step):
    return -(-value // step) * step


def sigmoid(value):
    return 0.5 * jnp.tanh(0.5 * value) + 0.5


def fold(value):
    rows, columns = value.shape
    return jnp.sum(value.reshape(rows // 8, 8, columns), axis=0)


def total(value):
    return jnp.sum(value, axis=0, keepdims=True)


def lookup(table, index):
    rows = index.shape[0]
    low = jnp.broadcast_to(table[:, 0:128], (rows, 128))
    high = jnp.broadcast_to(table[:, 128:256], (rows, 128))
    return take(low, high, index)


def take(low, high, index):
    parts = []
    for half in range(2):
        at = index[:, half * 128 : (half + 1) * 128]
        inside = lax.bitwise_and(at, 127)
        first = jnp.take_along_axis(low, inside, axis=1, mode="promise_in_bounds")
        second = jnp.take_along_axis(high, inside, axis=1, mode="promise_in_bounds")
        parts.append(jnp.where(at < 128, first, second))
    return jnp.concatenate(parts, axis=1)


def layout(z):
    n, T, L, D, F, H, B, C = z.n, z.T, z.L, z.D, z.F, z.H, z.B, z.C
    dma = pltpu.SemaphoreType.DMA
    vmem = pltpu.VMEM
    return {
        "qkv32": vmem((C, D), f32),
        "up32": vmem((D, F // H), f32),
        "down32": vmem((F // H, D), f32),
        "proj32": vmem((D, D), f32),
        "xraw": vmem((n, z.length, D), bf16),
        "qkvg": vmem((H, C, D), bf16),
        "upg": vmem((H, D, F // H), bf16),
        "downg": vmem((H, F // H, D), bf16),
        "smallg": vmem((H, 4, 128), f32),
        "ct": vmem((H, n, z.share, D), bf16),
        "w2": vmem((H * C, D), bf16),
        "w2t": vmem((D, H * C), bf16),
        "upcat": vmem((D, F), bf16),
        "projw": vmem((D, D), bf16),
        "bias": vmem((H, T, L), f32),
        "dbias": vmem((H, T, L), f32),
        "rowmask": vmem((T, D), f32),
        "eye": vmem((D, D), bf16),
        "eyet": vmem((T, L), bf16),
        "onehot": vmem((L, L), bf16),
        "xpad": vmem((n, L, D), bf16),
        "mt": vmem((n, H * C, L), bf16),
        "vnat": vmem((n, T, H * VAL), bf16),
        "qbd": vmem((H * KEY, H * L), bf16),
        "dabd": vmem((H * VAL, H * L), bf16),
        "p": vmem((n, H, T, L), bf16),
        "linv": vmem((n, H, 1, L), f32),
        "att": vmem((n, H * VAL, L), f32),
        "act": vmem((n, H * VAL, L), bf16),
        "proj": vmem((n, T, D), f32),
        "res": vmem((n, T, D), bf16),
        "hid": vmem((n, T, F), f32),
        "slope": vmem((n, T, F), f32),
        "act2": vmem((n, T, F), bf16),
        "out": vmem((n, T, D), f32),
        "u": vmem((n, T, D), f32),
        "gproj": vmem((n, L, D), bf16),
        "tmp": vmem((T, D), f32),
        "osend": vmem((H, n, z.share, D), bf16),
        "dmt": vmem((H * C, L), bf16),
        "gdown": vmem((D, F), f32),
        "gup": vmem((D, F), f32),
        "gpr": vmem((D, D), f32),
        "gqkv": vmem((H * C, D), f32),
        "srow": vmem((2, F), f32),
        "ar0h": vmem((H, 4, D), f32),
        "ar0b": vmem((B, 4, D), f32),
        "ar1h": vmem((H, 2, F), f32),
        "ar1b": vmem((B, 2, F), f32),
        "ar2h": vmem((H, 4, D), f32),
        "ar2b": vmem((B, 4, D), f32),
        "ar3h": vmem((H, 2, F), f32),
        "ar3b": vmem((B, 2, F), f32),
        "ar4h": vmem((H, 2, D), f32),
        "ar4b": vmem((B, 2, D), f32),
        "ar5h": vmem((H, H, L), f32),
        "ar5b": vmem((B, H, L), f32),
        "ge1": vmem((H, z.re, 128), bf16),
        "ge1r": vmem((H, z.re, 128), bf16),
        "ge2": vmem((B, z.re // B, 128), f32),
        "ge2r": vmem((B, z.re // B, 128), f32),
        "ge3": vmem((B, z.re // B, 128), f32),
        "gl1": vmem((H, z.rl, 128), bf16),
        "gl1r": vmem((H, z.rl, 128), bf16),
        "gl2": vmem((B, z.rl // B, 128), f32),
        "gl2r": vmem((B, z.rl // B, 128), f32),
        "gl3": vmem((B, z.rl // B, 128), f32),
        "loc": dma((8,)),
        "hs": dma((9, H)),
        "hr": dma((9, H)),
        "ahs": dma((6, H)),
        "ahr": dma((6, H)),
        "abs": dma((6, B)),
        "abr": dma((6, B)),
        "gbs": dma((4, B)),
        "gbr": dma((4, B)),
    }


def block_kernel(z, names, *refs):
    (tokens, count, place, qkv_w, table, proj_w, gain_1, shift_1, up_w, gain_2, shift_2, down_w,
     gain_3, shift_3, cot, out_o, tg_o, early_o, late_o, small_o) = refs[:20]
    s = types.SimpleNamespace(**dict(zip(names, refs[20:], strict=True)))
    n, T, L, D, F, H, B, C = z.n, z.T, z.L, z.D, z.F, z.H, z.B, z.C
    share, length = z.share, z.length
    me_h = lax.axis_index("head")
    me_b = lax.axis_index("batch")

    def local(src, dst, k):
        copy = pltpu.make_async_copy(src, dst, s.loc.at[k])
        copy.start()
        return copy

    def to_head(src, dst, k, j):
        return pltpu.make_async_remote_copy(
            src_ref=src, dst_ref=dst, send_sem=s.hs.at[k, j], recv_sem=s.hr.at[k, j],
            device_id={"head": lax.rem(me_h + j, H)}, device_id_type=MESH)

    def to_batch(src, dst, send, recv, j):
        return pltpu.make_async_remote_copy(
            src_ref=src, dst_ref=dst, send_sem=send, recv_sem=recv,
            device_id={"batch": lax.rem(me_b + j, B)}, device_id_type=MESH)

    def around(size, step):
        if size <= 8:
            for j in range(1, size):
                step(j)
        else:
            lax.fori_loop(1, size, lambda j, c: (step(j), c)[1], 0)

    c_qkv = local(qkv_w.at[0], s.qkv32, 0)
    c_up = local(up_w, s.up32, 1)
    c_down = local(down_w, s.down32, 2)
    c_tok = local(tokens.at[pl.ds(me_h * n, n)], s.xraw, 3)
    c_proj = local(proj_w, s.proj32, 4)

    barrier = pltpu.get_barrier_semaphore()
    around(H, lambda j: pl.semaphore_signal(
        barrier, inc=1, device_id={"head": lax.rem(me_h + j, H)}, device_id_type=MESH))
    around(B, lambda j: pl.semaphore_signal(
        barrier, inc=1, device_id={"batch": lax.rem(me_b + j, B)}, device_id_type=MESH))

    s.smallg[me_h] = jnp.concatenate(
        [gain_2[...], shift_2[...], table[:, 0:128], jnp.concatenate(
            [table[:, 128:length], jnp.zeros((1, 256 - length), f32)], axis=1)], axis=0)
    c_qkv.wait()
    s.qkvg[me_h] = s.qkv32[...].astype(bf16)
    c_up.wait()
    s.upg[me_h] = s.up32[...].astype(bf16)
    c_down.wait()
    s.downg[me_h] = s.down32[...].astype(bf16)

    pl.semaphore_wait(barrier, H - 1 + B - 1)

    weights = (s.qkvg, s.smallg, s.upg, s.downg)
    for k in range(2):
        for j in range(1, H):
            to_head(weights[k].at[me_h], weights[k].at[me_h], k, j).start()
    for k in range(2, 4):
        for j in range(1, H):
            to_head(weights[k].at[me_h], weights[k].at[me_h], k, j).start()
    for j in range(1, H):
        to_head(cot.at[pl.ds(lax.rem(me_h + j, H) * n, n)], s.ct.at[me_h], 4, j).start()
    c_cot = local(cot.at[pl.ds(me_h * n, n)], s.ct.at[me_h], 5)

    row_at = lax.broadcasted_iota(jnp.int32, (L, L), 0)
    lane_at = lax.broadcasted_iota(jnp.int32, (L, L), 1)
    s.eye[...] = jnp.where(row_at == lane_at, 1.0, 0.0).astype(bf16)
    s.eyet[...] = jnp.where((row_at == lane_at) & (row_at < length), 1.0, 0.0)[0:T].astype(bf16)
    s.rowmask[...] = jnp.where(row_at < length, 1.0, 0.0)[0:T]
    place_lane = jnp.broadcast_to(
        jnp.concatenate([place[...].astype(f32), jnp.zeros((1, L - length), f32)], axis=1), (L, L))
    place_row = place_lane.T
    s.onehot[...] = jnp.where((place_row == lane_at.astype(f32)) & (row_at < length), 1.0, 0.0).astype(bf16)

    def grid_of(at):
        at = at.astype(jnp.int32)
        row = lax.shift_right_logical(at * 4682, 16)
        return row, at - row * SIDE

    rows_t, cols_t = grid_of(place_lane[0:T])
    rows_s, cols_s = grid_of(place_row[0:T])
    offsets = jnp.abs(rows_s - rows_t) * SIDE + jnp.abs(cols_s - cols_t)
    for h in range(H):
        s.dbias[h] = jnp.zeros((T, L), f32)
    s.qbd[...] = jnp.zeros(s.qbd.shape, bf16)
    s.dabd[...] = jnp.zeros(s.dabd.shape, bf16)
    s.dmt[...] = jnp.zeros(s.dmt.shape, bf16)
    s.gdown[...] = jnp.zeros(s.gdown.shape, f32)
    s.gup[...] = jnp.zeros(s.gup.shape, f32)
    s.gpr[...] = jnp.zeros(s.gpr.shape, f32)
    s.gqkv[...] = jnp.zeros(s.gqkv.shape, f32)

    def valid_of(i):
        return jnp.where(me_h * n + i < count[0], 1.0, 0.0)

    c_proj.wait()
    s.projw[...] = s.proj32[...].astype(bf16)
    c_tok.wait()

    def pad(i, carry):
        s.xpad[i] = jnp.zeros((L, D), bf16)
        s.xpad[i, 0:length, :] = (s.xraw[i].astype(f32) * valid_of(i)).astype(bf16)
        s.gproj[i, T:L, :] = jnp.zeros((L - T, D), bf16)
        return carry

    lax.fori_loop(0, n, pad, 0)

    for k in range(2):
        for j in range(1, H):
            to_head(weights[k].at[me_h], weights[k].at[me_h], k, j).wait()
    for h in range(H):
        s.w2[h * KEY : (h + 1) * KEY] = s.qkvg[h, 0:KEY]
        s.w2[(H + h) * KEY : (H + h + 1) * KEY] = s.qkvg[h, KEY : 2 * KEY]
        at = 2 * H * KEY + h * VAL
        s.w2[at : at + VAL] = s.qkvg[h, 2 * KEY : C]
        line = jnp.concatenate([s.smallg[h, 2:3, :], s.smallg[h, 3:4, :]], axis=1)
        s.bias[h] = jnp.where(row_at[0:T] < length, lookup(line, offsets) * LOG2E, -1e30)

    scale = KEY**-0.5
    KH, VH = H * KEY, H * VAL

    def attend(i, carry):
        first, second = carry
        x = s.xpad[i]
        mixed = nt(s.w2[...], x).astype(bf16)
        s.mt[i] = mixed
        natural = nt(x[0:T], s.w2[KH : H * C]).astype(bf16)
        s.vnat[i] = natural[:, KH:]
        keys = natural[:, 0:KH]
        for h in range(H):
            s.qbd[h * KEY : (h + 1) * KEY, h * L : (h + 1) * L] = mixed[h * KEY : (h + 1) * KEY]
        for h in range(H):
            scores = nn(keys, s.qbd[:, h * L : (h + 1) * L]) * (scale * LOG2E) + s.bias[h]
            raised = jnp.exp2(scores - jnp.max(scores, axis=0, keepdims=True))
            inverse = 1.0 / total(raised)
            s.linv[i, h] = inverse
            low = raised.astype(bf16)
            s.p[i, h] = low
            values = mixed[2 * KH + h * VAL : 2 * KH + (h + 1) * VAL, 0:T]
            attended = nn(values, low) * inverse
            s.att[i, h * VAL : (h + 1) * VAL] = attended
            s.act[i, h * VAL : (h + 1) * VAL] = (attended * sigmoid(attended)).astype(bf16)
        active = nt(s.eyet[...], s.act[i]).astype(bf16)
        projected = nn(active, s.projw[...])
        s.proj[i] = projected
        return first + fold(projected), second + fold(projected * projected)

    def zeros(width):
        return jnp.zeros((8, width), f32)

    def all_reduce(k, rows, hbuf, bbuf):
        for r, row in enumerate(rows):
            hbuf[me_h, r : r + 1, :] = row
        for j in range(1, H):
            pltpu.make_async_remote_copy(
                src_ref=hbuf.at[me_h], dst_ref=hbuf.at[me_h], send_sem=s.ahs.at[k, j], recv_sem=s.ahr.at[k, j],
                device_id={"head": lax.rem(me_h + j, H)}, device_id_type=MESH).start()
        for j in range(1, H):
            pltpu.make_async_remote_copy(
                src_ref=hbuf.at[me_h], dst_ref=hbuf.at[me_h], send_sem=s.ahs.at[k, j], recv_sem=s.ahr.at[k, j],
                device_id={"head": lax.rem(me_h + j, H)}, device_id_type=MESH).wait()
        part = hbuf[0]
        for h in range(1, H):
            part = part + hbuf[h]
        bbuf[me_b] = part
        around(B, lambda j: to_batch(bbuf.at[me_b], bbuf.at[me_b], s.abs.at[k, j], s.abr.at[k, j], j).start())
        around(B, lambda j: to_batch(bbuf.at[me_b], bbuf.at[me_b], s.abs.at[k, j], s.abr.at[k, j], j).wait())
        if B <= 8:
            whole = bbuf[0]
            for b in range(1, B):
                whole = whole + bbuf[b]
            return whole
        return lax.fori_loop(1, B, lambda b, c: c + bbuf[b], bbuf[0])

    first, second = lax.fori_loop(0, n, attend, (zeros(D), zeros(D)))
    mine = jnp.clip(count[0] - me_h * n, 0, n).astype(f32) * float(length)
    sums = all_reduce(
        0, [total(first), total(second), jnp.full((1, D), mine), jnp.zeros((1, D), f32)], s.ar0h, s.ar0b)
    seen_row = sums[2:3, :]
    seen_wide = jnp.concatenate([seen_row] * (F // D), axis=1)

    def moments(first, second, seen):
        mean = first / seen
        return mean, lax.rsqrt(second / seen - mean * mean + EPSILON)

    mean_1, inverse_1 = moments(sums[0:1], sums[1:2], seen_row)
    a_1 = gain_1[...] * inverse_1
    b_1 = shift_1[...] - mean_1 * a_1

    for k in range(2, 4):
        for j in range(1, H):
            to_head(weights[k].at[me_h], weights[k].at[me_h], k, j).wait()
    for h in range(H):
        s.upcat[:, h * (F // H) : (h + 1) * (F // H)] = s.upg[h]
    down = s.downg[...].reshape(F, D)

    def residual_of(i):
        return s.xpad[i, 0:T].astype(f32) + (s.proj[i] * a_1 + (b_1 * valid_of(i)) * s.rowmask[...])

    def enter(i, carry):
        first, second = carry
        residual = residual_of(i).astype(bf16)
        s.res[i] = residual
        hidden = nn(residual, s.upcat[...])
        s.hid[i] = hidden
        return first + fold(hidden), second + fold(hidden * hidden)

    first, second = lax.fori_loop(0, n, enter, (zeros(F), zeros(F)))
    sums = all_reduce(1, [total(first), total(second)], s.ar1h, s.ar1b)
    mean_2, inverse_2 = moments(sums[0:1], sums[1:2], seen_wide)
    gain_2w = jnp.concatenate([s.smallg[h, 0:1, :] for h in range(H)], axis=1)
    shift_2w = jnp.concatenate([s.smallg[h, 1:2, :] for h in range(H)], axis=1)
    a_2 = gain_2w * inverse_2
    b_2 = shift_2w - mean_2 * a_2

    for j in range(1, H):
        to_head(cot.at[pl.ds(lax.rem(me_h + j, H) * n, n)], s.ct.at[me_h], 4, j).wait()
    c_cot.wait()

    def leave(i, carry):
        one, two, three, four = carry
        shaped = s.hid[i] * a_2 + b_2
        gate = sigmoid(shaped)
        active = shaped * gate
        s.slope[i] = gate + active * (1.0 - gate)
        low = active.astype(bf16)
        s.act2[i] = low
        outgoing = nn(low, down)
        s.out[i] = outgoing
        valid = valid_of(i)
        s.u[i, T - 16 : T, :] = jnp.zeros((16, D), f32)
        for q in range(H):
            s.u[i, q * share : (q + 1) * share, :] = s.ct[q, i].astype(f32) * valid
        upstream = s.u[i]
        masked = outgoing * (s.rowmask[...] * valid)
        return (one + fold(masked), two + fold(masked * outgoing), three + fold(upstream),
                four + fold(upstream * outgoing))

    sums = lax.fori_loop(0, n, leave, (zeros(D), zeros(D), zeros(D), zeros(D)))
    sums = all_reduce(2, [total(v) for v in sums], s.ar2h, s.ar2b)
    mean_3, inverse_3 = moments(sums[0:1], sums[1:2], seen_row)
    a_3 = gain_3[...] * inverse_3
    b_3 = shift_3[...] - mean_3 * a_3
    sum_shift_3 = sums[2:3]
    sum_gain_3 = inverse_3 * (sums[3:4] - mean_3 * sum_shift_3)

    def back(gain, mean, inverse, sum_shift, sum_gain, seen):
        scaled = gain * inverse
        slope = -scaled * inverse * (sum_gain / seen)
        return scaled, slope, -scaled * (sum_shift / seen) - slope * mean

    s_3, v_3, r_3 = back(gain_3[...], mean_3, inverse_3, sum_shift_3, sum_gain_3, seen_row)

    def back_leave(i, carry):
        one, two = carry
        valid = valid_of(i)
        outgoing = s.out[i]
        s.tmp[...] = (residual_of(i) + (outgoing * a_3 + b_3)) * valid
        for q in range(H):
            s.osend[q, i] = s.tmp[q * share : (q + 1) * share, :].astype(bf16)
        grad = (s.u[i] * s_3 + (outgoing * v_3 + r_3) * (s.rowmask[...] * valid)).astype(bf16)
        shaped = nt(grad, down) * s.slope[i]
        s.slope[i] = shaped
        turned = nt(s.eye[...], grad).astype(bf16)
        s.gdown[...] += nn(turned, s.act2[i])
        return one + fold(shaped), two + fold(shaped * s.hid[i])

    first, second = lax.fori_loop(0, n, back_leave, (zeros(F), zeros(F)))
    sums = all_reduce(3, [total(first), total(second)], s.ar3h, s.ar3b)

    for j in range(1, H):
        to_head(s.osend.at[lax.rem(me_h + j, H)], out_o.at[pl.ds(me_h * n, n)], 5, j).start()
    c_out = local(s.osend.at[me_h], out_o.at[pl.ds(me_h * n, n)], 6)

    sum_shift_2 = sums[0:1]
    sum_gain_2 = inverse_2 * (sums[1:2] - mean_2 * sum_shift_2)
    s_2, v_2, r_2 = back(gain_2w, mean_2, inverse_2, sum_shift_2, sum_gain_2, seen_wide)
    s.srow[0:1, :] = sum_gain_2
    s.srow[1:2, :] = sum_shift_2

    def back_enter(i, carry):
        one, two = carry
        mask = s.rowmask[...] * valid_of(i)
        grad = (s.slope[i] * s_2 + s.hid[i] * v_2 + r_2 * jnp.concatenate([mask] * (F // D), axis=1)).astype(bf16)
        turned = nt(s.eye[...], s.res[i]).astype(bf16)
        s.gup[...] += nn(turned, grad)
        upstream = s.u[i] + nt(grad, s.upcat[...])
        s.u[i] = upstream
        return one + fold(upstream), two + fold(upstream * s.proj[i])

    first, second = lax.fori_loop(0, n, back_enter, (zeros(D), zeros(D)))
    sums = all_reduce(4, [total(first), total(second)], s.ar4h, s.ar4b)
    sum_shift_1 = sums[0:1]
    sum_gain_1 = inverse_1 * (sums[1:2] - mean_1 * sum_shift_1)
    s_1, v_1, r_1 = back(gain_1[...], mean_1, inverse_1, sum_shift_1, sum_gain_1, seen_row)

    def back_project(i, carry):
        mask = s.rowmask[...] * valid_of(i)
        grad = (s.u[i] * s_1 + s.proj[i] * v_1 + r_1 * mask).astype(bf16)
        s.gproj[i, 0:T, :] = grad
        s.gpr[...] += nn(s.act[i], s.gproj[i])
        return carry

    lax.fori_loop(0, n, back_project, 0)

    def shares(buffer, k):
        for j in range(1, H):
            yield to_head(buffer[0].at[lax.rem(me_h + j, H)], buffer[1].at[me_h], k, j)

    def head_sum(buffer):
        whole = buffer[0][me_h].astype(f32)
        for j in range(1, H):
            whole = whole + buffer[1][lax.rem(me_h + j, H)].astype(f32)
        return whole

    def spread(src, dst, k, act):
        around(B, lambda j: act(to_batch(src(lax.rem(me_b + j, B)), dst, s.gbs.at[k, j], s.gbr.at[k, j], j)))

    def batch_sum(own, received):
        if B <= 8:
            whole = own
            for j in range(1, B):
                whole = whole + received[lax.rem(me_b + j, B)]
            return whole
        return lax.fori_loop(1, B, lambda j, c: c + received[lax.rem(me_b + j, B)], own)

    FH = F // H
    PH = D // H
    for h in range(H):
        s.ge1[h, 0:D, :] = s.gup[:, h * FH : (h + 1) * FH].astype(bf16)
        s.ge1[h, D : 2 * D, :] = s.gdown[:, h * FH : (h + 1) * FH].astype(bf16)
        for half in range(D // 128):
            at = 2 * D + half * PH
            s.ge1[h, at : at + PH, :] = s.gpr[h * PH : (h + 1) * PH, half * 128 : (half + 1) * 128].astype(bf16)
        if z.re > 2 * D + PH * (D // 128):
            s.ge1[h, 2 * D + PH * (D // 128) :, :] = jnp.zeros((z.re - 2 * D - PH * (D // 128), 128), bf16)
    for copy in shares((s.ge1, s.ge1r), 7):
        copy.start()

    for j in range(1, H):
        to_head(s.osend.at[lax.rem(me_h + j, H)], out_o.at[pl.ds(me_h * n, n)], 5, j).wait()
    c_out.wait()

    def back_attend(i, carry):
        slope_gate = sigmoid(s.att[i])
        att = s.att[i]
        active = att * slope_gate
        gact = nt(s.projw[...], s.gproj[i]) * (slope_gate + active * (1.0 - slope_gate))
        for h in range(H):
            rows = slice(h * VAL, (h + 1) * VAL)
            grad = gact[rows] * s.linv[i, h]
            low = grad.astype(bf16)
            s.dabd[rows, h * L : (h + 1) * L] = low
            delta = total(grad * att[rows])
            weights_low = s.p[i, h]
            gscores = weights_low.astype(f32) * (nn(s.vnat[i], s.dabd[:, h * L : (h + 1) * L]) - delta)
            s.dbias[h] += gscores
            glow = gscores.astype(bf16)
            q_rows = slice(h * KEY, (h + 1) * KEY)
            k_rows = slice(KH + h * KEY, KH + (h + 1) * KEY)
            v_rows = slice(2 * KH + h * VAL, 2 * KH + (h + 1) * VAL)
            s.dmt[q_rows, :] = (nn(s.mt[i, k_rows, 0:T], glow) * scale).astype(bf16)
            s.dmt[k_rows, 0:T] = (nt(s.mt[i, q_rows, :], glow) * scale).astype(bf16)
            s.dmt[v_rows, 0:T] = nt(low, weights_low).astype(bf16)
        s.gqkv[...] += nn(s.dmt[...], s.xpad[i])
        turned = nn(s.w2t[...], s.dmt[...]).astype(bf16)
        s.tmp[...] = s.u[i] + nt(s.eyet[...], turned)
        for q in range(H):
            s.osend[q, i] = s.tmp[q * share : (q + 1) * share, :].astype(bf16)
        for j in range(1, H):
            to_head(s.osend.at[lax.rem(me_h + j, H), i], tg_o.at[me_h * n + i], 6, j).start()
        pltpu.make_async_copy(s.osend.at[me_h, i], tg_o.at[me_h * n + i], s.loc.at[7]).start()
        return carry

    s.w2t[...] = nt(s.eye[...], s.w2[...]).astype(bf16)
    lax.fori_loop(0, n // 2, back_attend, 0)

    for copy in shares((s.ge1, s.ge1r), 7):
        copy.wait()
    s.ge2[...] = head_sum((s.ge1, s.ge1r)).reshape(B, z.re // B, 128)
    spread(lambda peer: s.ge2.at[peer], s.ge2r.at[me_b], 0, lambda c: c.start())

    lax.fori_loop(n // 2, n, back_attend, 0)

    spread(lambda peer: s.ge2.at[peer], s.ge2r.at[me_b], 0, lambda c: c.wait())
    s.ge3[me_b] = batch_sum(s.ge2[me_b], s.ge2r)
    spread(lambda peer: s.ge3.at[me_b], s.ge3.at[me_b], 1, lambda c: c.start())

    for h in range(H):
        for half in range(D // 128):
            lanes = slice(half * 128, (half + 1) * 128)
            at = half * C
            s.gl1[h, at : at + KEY, :] = s.gqkv[h * KEY : (h + 1) * KEY, lanes].astype(bf16)
            s.gl1[h, at + KEY : at + 2 * KEY, :] = s.gqkv[KH + h * KEY : KH + (h + 1) * KEY, lanes].astype(bf16)
            s.gl1[h, at + 2 * KEY : at + C, :] = s.gqkv[2 * KH + h * VAL : 2 * KH + (h + 1) * VAL, lanes].astype(bf16)
        if z.rl > C * (D // 128):
            s.gl1[h, C * (D // 128) :, :] = jnp.zeros((z.rl - C * (D // 128), 128), bf16)
    for copy in shares((s.gl1, s.gl1r), 8):
        copy.start()

    slot = lax.broadcasted_iota(jnp.int32, (T, L), 1)
    d_row, d_col = grid_of(slot)
    picks = []
    for down_sign in (1, -1):
        for right_sign in (1, -1):
            r = rows_s + down_sign * d_row
            c = cols_s + right_sign * d_col
            good = (r >= 0) & (r < SIDE) & (c >= 0) & (c < SIDE) & (slot < length)
            if down_sign < 0:
                good = good & (d_row > 0)
            if right_sign < 0:
                good = good & (d_col > 0)
            picks.append((jnp.where(good, r * SIDE + c, 0), good))
    bias_rows = []
    for h in range(H):
        whole = s.dbias[h]
        high = whole.astype(bf16)
        rest = (whole - high.astype(f32)).astype(bf16)
        ordered = nn(high, s.onehot[...]) + nn(rest, s.onehot[...])
        line = jnp.zeros((T, L), f32)
        for index, good in picks:
            line = line + jnp.where(good, take(ordered[:, 0:128], ordered[:, 128:256], index), 0.0)
        bias_rows.append(total(line * s.rowmask[...]))
    bias_sums = all_reduce(5, bias_rows, s.ar5h, s.ar5b)
    s.ar5h[0] = bias_sums

    for copy in shares((s.gl1, s.gl1r), 8):
        copy.wait()
    s.gl2[...] = head_sum((s.gl1, s.gl1r)).reshape(B, z.rl // B, 128)
    spread(lambda peer: s.gl2.at[peer], s.gl2r.at[me_b], 2, lambda c: c.start())
    spread(lambda peer: s.gl2.at[peer], s.gl2r.at[me_b], 2, lambda c: c.wait())
    s.gl3[me_b] = batch_sum(s.gl2[me_b], s.gl2r)
    spread(lambda peer: s.gl3.at[me_b], s.gl3.at[me_b], 3, lambda c: c.start())

    own = pl.ds(pl.multiple_of(me_h * FH, FH), FH)
    small_o[...] = jnp.zeros(small_o.shape, f32)
    small_o[0:1, :] = sum_gain_1
    small_o[1:2, :] = sum_shift_1
    small_o[2:3, :] = sum_gain_3
    small_o[3:4, :] = sum_shift_3
    small_o[4:5, 0:FH] = s.srow[0:1, own]
    small_o[5:6, 0:FH] = s.srow[1:2, own]
    small_o[6:7, :] = s.ar5h[0, pl.ds(me_h, 1), :]

    spread(lambda peer: s.ge3.at[me_b], s.ge3.at[me_b], 1, lambda c: c.wait())
    early_o[...] = s.ge3[...].reshape(z.re, 128)
    spread(lambda peer: s.gl3.at[me_b], s.gl3.at[me_b], 3, lambda c: c.wait())
    late_o[...] = s.gl3[...].reshape(z.rl, 128)

    for j in range(1, H):
        to_head(s.osend.at[lax.rem(me_h + j, H)], tg_o.at[pl.ds(me_h * n, n)], 6, j).wait()
    pltpu.make_async_copy(s.osend.at[me_h], tg_o.at[pl.ds(me_h * n, n)], s.loc.at[7]).wait()


def finish_kernel(z, out_i, tg_i, early, late, small, out, tg, qkv, bias, proj, g1, s1, up, g2, s2, down, g3, s3):
    out[...] = out_i[...].astype(f32)
    tg[...] = tg_i[...].astype(f32)

    @pl.when(pl.program_id(0) == 0)
    def _():
        D, C, PH = z.D, z.C, z.D // z.H
        up[...] = early[0:D, :]
        down[...] = early[D : 2 * D, :].T
        for half in range(D // 128):
            lanes = slice(half * 128, (half + 1) * 128)
            proj[:, lanes] = early[2 * D + half * PH : 2 * D + (half + 1) * PH, :]
            qkv[0, :, lanes] = late[half * C : (half + 1) * C, :]
        g1[...] = small[0:1, :]
        s1[...] = small[1:2, :]
        g3[...] = small[2:3, :]
        s3[...] = small[3:4, :]
        g2[...] = small[4:5, 0 : z.F // z.H]
        s2[...] = small[5:6, 0 : z.F // z.H]
        bias[...] = small[6:7, 0 : z.length]


def on_device(H, B, tokens, image_count, token_place, qkv_weight, bias_table, proj_weight, attention_gain,
              attention_shift, up_weight, hidden_gain, hidden_shift, down_weight, output_gain, output_shift,
              cotangent):
    images, length, width = tokens.shape
    z = types.SimpleNamespace(
        n=images // H, T=round_up(length, 16), L=round_up(length, 128), D=width, F=up_weight.shape[1] * H,
        H=H, B=B, C=qkv_weight.shape[1], share=cotangent.shape[1], length=length)
    z.re = round_up(2 * z.D + z.D // H * (z.D // 128), 8 * max(B, 2))
    z.rl = round_up(z.C * (z.D // 128), 8 * max(B, 2))
    scratch = layout(z)
    hbm = pl.BlockSpec(memory_space=pl.ANY)
    vmem = pl.BlockSpec(memory_space=pltpu.VMEM)
    smem = pl.BlockSpec(memory_space=pltpu.SMEM)
    outs = pl.pallas_call(
        functools.partial(block_kernel, z, tuple(scratch)),
        out_shape=(
            jax.ShapeDtypeStruct((images, z.share, width), bf16),
            jax.ShapeDtypeStruct((images, z.share, width), bf16),
            jax.ShapeDtypeStruct((z.re, 128), f32),
            jax.ShapeDtypeStruct((z.rl, 128), f32),
            jax.ShapeDtypeStruct((8, width), f32),
        ),
        in_specs=[hbm, smem, vmem, hbm, vmem, hbm, vmem, vmem, hbm, vmem, vmem, hbm, vmem, vmem, hbm],
        out_specs=(hbm, hbm, vmem, vmem, vmem),
        scratch_shapes=list(scratch.values()),
        compiler_params=pltpu.CompilerParams(
            collective_id=0, has_side_effects=True, vmem_limit_bytes=63 * 1024 * 1024
        ),
    )(
        tokens, image_count, token_place.reshape(1, -1), qkv_weight, bias_table, proj_weight,
        attention_gain.reshape(1, -1), attention_shift.reshape(1, -1), up_weight, hidden_gain.reshape(1, -1),
        hidden_shift.reshape(1, -1), down_weight, output_gain.reshape(1, -1), output_shift.reshape(1, -1), cotangent,
    )

    steps = 4
    block = pl.BlockSpec((images // steps, z.share, width), lambda i: (i, 0, 0))

    def whole(*shape):
        return jax.ShapeDtypeStruct(shape, f32), pl.BlockSpec(shape, lambda i: (0,) * len(shape))

    fh = z.F // H
    small = [
        whole(1, z.C, width), whole(1, length), whole(width // H, width), whole(1, width), whole(1, width),
        whole(width, fh), whole(1, fh), whole(1, fh), whole(fh, width), whole(1, width), whole(1, width)]
    big = jax.ShapeDtypeStruct((images, z.share, width), f32)
    res = pl.pallas_call(
        functools.partial(finish_kernel, z),
        grid=(steps,),
        out_shape=[big, big] + [a for a, _ in small],
        in_specs=[block, block, whole(z.re, 128)[1], whole(z.rl, 128)[1], whole(8, width)[1]],
        out_specs=[block, block] + [b for _, b in small],
    )(*outs)
    res = list(res)
    for k in (5, 6, 8, 9, 11, 12):
        res[k] = res[k].reshape(-1)
    return tuple(res)


def solution(mesh):
    H, B = mesh.shape["head"], mesh.shape["batch"]
    placed = (
        P("batch", None, None),
        P("batch"),
        P(),
        P("head", None, None),
        P("head", None),
        P(),
        P(),
        P(),
        P(None, "head"),
        P("head"),
        P("head"),
        P("head", None),
        P(),
        P(),
        P("batch", "head", None),
    )
    return jax.shard_map(
        functools.partial(on_device, H, B),
        mesh=mesh,
        in_specs=placed,
        out_specs=(
            P("batch", "head", None),
            P("batch", "head", None),
            P("head", None, None),
            P("head", None),
            P("head", None),
            P(),
            P(),
            P(None, "head"),
            P("head"),
            P("head"),
            P("head", None),
            P(),
            P(),
        ),
        check_vma=False,
    )
```

```python
import functools
import types

import jax
import jax.numpy as jnp
from jax import lax
from jax.experimental import pallas as pl
from jax.experimental.pallas import tpu as pltpu
from jax.sharding import PartitionSpec as P

KEY = 32
VAL = 64
SIDE = 14
EPSILON = 1e-05
LOG2E = 1.4426950408889634
MESH = pl.DeviceIdType.MESH
f32 = jnp.float32
bf16 = jnp.bfloat16


def nn(left, right):
    return lax.dot_general(left, right, (((1,), (0,)), ((), ())), preferred_element_type=f32)


def nt(left, right):
    return lax.dot_general(left, right, (((1,), (1,)), ((), ())), preferred_element_type=f32)


def round_up(value, step):
    return -(-value // step) * step


def sigmoid(value):
    return 0.5 * jnp.tanh(0.5 * value) + 0.5


def fold(value):
    rows, columns = value.shape
    return jnp.sum(value.reshape(rows // 8, 8, columns), axis=0)


def total(value):
    return jnp.sum(value, axis=0, keepdims=True)


def lookup(table, index):
    rows = index.shape[0]
    low = jnp.broadcast_to(table[:, 0:128], (rows, 128))
    high = jnp.broadcast_to(table[:, 128:256], (rows, 128))
    return take(low, high, index)


def take(low, high, index):
    parts = []
    for half in range(2):
        at = index[:, half * 128 : (half + 1) * 128]
        inside = lax.bitwise_and(at, 127)
        first = jnp.take_along_axis(low, inside, axis=1, mode="promise_in_bounds")
        second = jnp.take_along_axis(high, inside, axis=1, mode="promise_in_bounds")
        parts.append(jnp.where(at < 128, first, second))
    return jnp.concatenate(parts, axis=1)


def layout(z):
    n, T, L, D, F, H, B, C = z.n, z.T, z.L, z.D, z.F, z.H, z.B, z.C
    dma = pltpu.SemaphoreType.DMA
    vmem = pltpu.VMEM
    return {
        "xt": vmem((T, 16, D), bf16),
        "ct": vmem((T, 16, D), bf16),
        "mix": vmem((n * 16, 256), bf16),
        "qkvg": vmem((H, C, D), bf16),
        "downg": vmem((H, F // H, D), bf16),
        "smallg": vmem((H, 4, 128), f32),
        "w2": vmem((H * C, D), bf16),
        "w2t": vmem((D, H * C), bf16),
        "upcat": vmem((D, F), bf16),
        "projw": vmem((D, D), bf16),
        "bias": vmem((H, T, L), f32),
        "dbias": vmem((H, T, L), f32),
        "rowmask": vmem((T, D), f32),
        "eye": vmem((D, D), bf16),
        "eyet": vmem((T, L), bf16),
        "onehot": vmem((L, L), bf16),
        "xpad": vmem((n, L, D), bf16),
        "mt": vmem((n, H * C, L), bf16),
        "vnat": vmem((n, T, H * VAL), bf16),
        "qbd": vmem((H * KEY, H * L), bf16),
        "dabd": vmem((H * VAL, H * L), bf16),
        "p": vmem((n, H, T, L), bf16),
        "linv": vmem((n, H, 1, L), f32),
        "att": vmem((n, H * VAL, L), f32),
        "act": vmem((n, H * VAL, L), bf16),
        "proj": vmem((n, T, D), f32),
        "res": vmem((n, T, D), bf16),
        "hid": vmem((n, T, F), f32),
        "slope": vmem((n, T, F), f32),
        "act2": vmem((n, T, F), bf16),
        "out": vmem((n, T, D), f32),
        "u": vmem((n, T, D), f32),
        "gproj": vmem((n, L, D), bf16),
        "tmp": vmem((T, D), f32),
        "osend": vmem((H, n, z.share, D), bf16),
        "tsend": vmem((H, n, z.share, D), bf16),
        "dmt": vmem((H * C, L), bf16),
        "gdown": vmem((D, F), f32),
        "gup": vmem((D, F), f32),
        "gpr": vmem((D, D), f32),
        "gqkv": vmem((H * C, D), f32),
        "srow": vmem((2, F), f32),
        "brow": vmem((H, 1, L), f32),
        **z.sums,
        "cnt": vmem((B, 1, 128), f32),
        "ge1": vmem((H, z.re, 128), bf16),
        "ge1r": vmem((H, z.re, 128), bf16),
        "ge2": vmem((B, z.re // B, 128), f32),
        "ge2r": vmem((B, z.re // B, 128), f32),
        "ge3": vmem((B, z.re // B, 128), f32),
        "gl1": vmem((H, z.rl, 128), bf16),
        "gl1r": vmem((H, z.rl, 128), bf16),
        "gl2": vmem((B, z.rl // B, 128), f32),
        "gl2r": vmem((B, z.rl // B, 128), f32),
        "gl3": vmem((B, z.rl // B, 128), f32),
        "loc": dma((8,)),
        "hs": dma((9, H)),
        "hr": dma((9, H)),
        "ass": dma((6, z.ports)),
        "asr": dma((6, z.ports)),
        "cns": dma((B,)),
        "cnr": dma((B,)),
        "gbs": dma((4, B)),
        "gbr": dma((4, B)),
    }


def block_kernel(z, names, *refs):
    (tokens, count, place, qkv_w, table, proj_w, gain_1, shift_1, up_w, gain_2, shift_2, down_w,
     gain_3, shift_3, cot, out_o, tg_o, early_o, late_o, small_o) = refs[:20]
    s = types.SimpleNamespace(**dict(zip(names, refs[20:], strict=True)))
    n, T, L, D, F, H, B, C = z.n, z.T, z.L, z.D, z.F, z.H, z.B, z.C
    share, length = z.share, z.length
    me_h = lax.axis_index("head")
    me_b = lax.axis_index("batch")

    def local(src, dst, k):
        copy = pltpu.make_async_copy(src, dst, s.loc.at[k])
        copy.start()
        return copy

    def to_head(src, dst, k, j):
        return pltpu.make_async_remote_copy(
            src_ref=src, dst_ref=dst, send_sem=s.hs.at[k, j], recv_sem=s.hr.at[k, j],
            device_id={"head": lax.rem(me_h + j, H)}, device_id_type=MESH)

    def to_batch(src, dst, send, recv, j):
        return pltpu.make_async_remote_copy(
            src_ref=src, dst_ref=dst, send_sem=send, recv_sem=recv,
            device_id={"batch": lax.rem(me_b + j, B)}, device_id_type=MESH)

    def around(size, step):
        if size <= 8:
            for j in range(1, size):
                step(j)
        else:
            lax.fori_loop(1, size, lambda j, c: (step(j), c)[1], 0)

    FH = F // H
    PH = D // H
    own = pl.ds(pl.multiple_of(me_h * FH, FH), FH)
    qkv_32, up_32, down_32 = s.gqkv.at[0:C], s.gup.at[:, 0:FH], s.gdown.at[0:FH, 0:D]
    c_qkv = local(qkv_w.at[0], qkv_32, 0)
    c_up = local(up_w, up_32, 1)
    c_down = local(down_w, down_32, 2)
    def window(slot):
        return pl.multiple_of(slot * n // 8 * 8, 8)

    c_tok = local(tokens.at[:, pl.ds(window(me_h), 16)], s.xt.at[pl.ds(0, length)], 3)
    c_proj = local(proj_w, s.gpr, 4)

    def everyone():
        pairs = [(a, b) for a in range(H) for b in range(B) if a or b]
        return sorted(pairs, key=lambda p: -(p[0] % 2 + p[0] // 2 + (2 if p[1] > 1 else p[1] / 4)))

    def at_offset(offset):
        a, b = offset
        x, y = lax.rem(me_h, 2), lax.div(me_h, 2)
        other = (y + a // 2 - 2 * y * (a // 2)) * 2 + x + a % 2 - 2 * x * (a % 2)
        return {"head": other, "batch": lax.rem(me_b + b, B)}

    barrier = pltpu.get_barrier_semaphore()
    if z.direct:
        for offset in everyone():
            pl.semaphore_signal(barrier, inc=1, device_id=at_offset(offset), device_id_type=MESH)
    else:
        around(H, lambda j: pl.semaphore_signal(
            barrier, inc=1, device_id={"head": lax.rem(me_h + j, H)}, device_id_type=MESH))
        around(B, lambda j: pl.semaphore_signal(
            barrier, inc=1, device_id={"batch": lax.rem(me_b + j, B)}, device_id_type=MESH))

    s.smallg[me_h] = jnp.concatenate(
        [gain_2[...], shift_2[...], table[:, 0:128], jnp.concatenate(
            [table[:, 128:length], jnp.zeros((1, 256 - length), f32)], axis=1)], axis=0)
    c_qkv.wait()
    s.qkvg[me_h] = qkv_32[...].astype(bf16)
    c_up.wait()
    s.upcat[:, own] = up_32[...].astype(bf16)
    c_down.wait()
    s.downg[me_h] = down_32[...].astype(bf16)

    s.cnt[me_b] = jnp.full((1, 128), count[0]).astype(f32)
    pl.semaphore_wait(barrier, H * B - 1 if z.direct else H - 1 + B - 1)

    shared = (s.qkvg.at[me_h], s.smallg.at[me_h], s.upcat.at[:, own], s.downg.at[me_h])

    def weight_copy(k, j):
        return to_head(shared[k], shared[k], k, j)

    for k in range(4):
        for j in range(1, H):
            weight_copy(k, j).start()
    def cot_copy(j):
        peer = lax.rem(me_h + j, H)
        return to_head(cot.at[:, pl.ds(window(peer), 16)], s.ct.at[pl.ds(me_h * share, share)], 4, j)

    def count_copy(j):
        return to_batch(s.cnt.at[me_b], s.cnt.at[me_b], s.cns.at[j], s.cnr.at[j], j)

    around(B, lambda j: count_copy(j).start())
    for j in range(1, H):
        cot_copy(j).start()
    c_cot = local(cot.at[:, pl.ds(window(me_h), 16)], s.ct.at[pl.ds(me_h * share, share)], 5)

    row_at = lax.broadcasted_iota(jnp.int32, (L, L), 0)
    lane_at = lax.broadcasted_iota(jnp.int32, (L, L), 1)
    s.eye[...] = jnp.where(row_at == lane_at, 1.0, 0.0).astype(bf16)
    s.eyet[...] = jnp.where((row_at == lane_at) & (row_at < length), 1.0, 0.0)[0:T].astype(bf16)
    s.rowmask[...] = jnp.where(row_at < length, 1.0, 0.0)[0:T]
    place_lane = jnp.broadcast_to(
        jnp.concatenate([place[...].astype(f32), jnp.zeros((1, L - length), f32)], axis=1), (L, L))
    place_row = place_lane.T
    s.onehot[...] = jnp.where((place_row == lane_at.astype(f32)) & (row_at < length), 1.0, 0.0).astype(bf16)

    def grid_of(at):
        at = at.astype(jnp.int32)
        row = lax.shift_right_logical(at * 4682, 16)
        return row, at - row * SIDE

    rows_t, cols_t = grid_of(place_lane[0:T])
    rows_s, cols_s = grid_of(place_row[0:T])
    offsets = jnp.abs(rows_s - rows_t) * SIDE + jnp.abs(cols_s - cols_t)
    for h in range(H):
        s.dbias[h] = jnp.zeros((T, L), f32)
    s.qbd[...] = jnp.zeros(s.qbd.shape, bf16)
    s.dabd[...] = jnp.zeros(s.dabd.shape, bf16)
    s.dmt[...] = jnp.zeros(s.dmt.shape, bf16)
    s.gdown[...] = jnp.zeros(s.gdown.shape, f32)
    s.gup[...] = jnp.zeros(s.gup.shape, f32)
    s.gqkv[...] = jnp.zeros(s.gqkv.shape, f32)

    def valid_of(i):
        return jnp.where(me_h * n + i < count[0], 1.0, 0.0)

    c_proj.wait()
    s.projw[...] = s.gpr[...].astype(bf16)
    s.gpr[...] = jnp.zeros(s.gpr.shape, f32)
    line_at = lax.broadcasted_iota(jnp.int32, (n * 16, 256), 0)
    pick_at = lax.broadcasted_iota(jnp.int32, (n * 16, 256), 1)
    image_at = lax.shift_right_logical(line_at, 4)
    s.mix[...] = jnp.where(
        (lax.bitwise_and(line_at, 15) == lax.shift_right_logical(pick_at, 4))
        & (lax.bitwise_and(pick_at, 15) == image_at + (me_h * n - window(me_h)))
        & (image_at + me_h * n < count[0]),
        1.0, 0.0).astype(bf16)
    s.xt[length:T] = jnp.zeros((T - length, 16, D), bf16)
    s.ct[length:T] = jnp.zeros((T - length, 16, D), bf16)
    s.xpad[:, T:L, :] = jnp.zeros((n, L - T, D), bf16)
    s.gproj[:, T:L, :] = jnp.zeros((n, L - T, D), bf16)
    c_tok.wait()

    def enter_tokens(k, carry):
        at = pl.ds(pl.multiple_of(k * 16, 16), 16)
        s.xpad[:, at, :] = nn(s.mix[...], s.xt[at].reshape(256, D)).astype(bf16).reshape(n, 16, D)
        return carry

    def enter_cotangent(k, carry):
        at = pl.ds(pl.multiple_of(k * 16, 16), 16)
        s.u[:, at, :] = nn(s.mix[...], s.ct[at].reshape(256, D)).reshape(n, 16, D)
        return carry

    lax.fori_loop(0, T // 16, enter_tokens, 0)

    for k in range(2):
        for j in range(1, H):
            weight_copy(k, j).wait()
    for h in range(H):
        s.w2[h * KEY : (h + 1) * KEY] = s.qkvg[h, 0:KEY]
        s.w2[(H + h) * KEY : (H + h + 1) * KEY] = s.qkvg[h, KEY : 2 * KEY]
        at = 2 * H * KEY + h * VAL
        s.w2[at : at + VAL] = s.qkvg[h, 2 * KEY : C]
        line = jnp.concatenate([s.smallg[h, 2:3, :], s.smallg[h, 3:4, :]], axis=1)
        s.bias[h] = jnp.where(row_at[0:T] < length, lookup(line, offsets) * LOG2E, -1e30)

    scale = KEY**-0.5
    KH, VH = H * KEY, H * VAL

    def attend(i, carry):
        first, second = carry
        x = s.xpad[i]
        mixed = nt(s.w2[...], x).astype(bf16)
        s.mt[i] = mixed
        natural = nt(x[0:T], s.w2[KH : H * C]).astype(bf16)
        s.vnat[i] = natural[:, KH:]
        keys = natural[:, 0:KH]
        for h in range(H):
            s.qbd[h * KEY : (h + 1) * KEY, h * L : (h + 1) * L] = mixed[h * KEY : (h + 1) * KEY]
        for h in range(H):
            scores = nn(keys, s.qbd[:, h * L : (h + 1) * L]) * (scale * LOG2E) + s.bias[h]
            raised = jnp.exp2(scores - jnp.max(scores, axis=0, keepdims=True))
            inverse = 1.0 / total(raised)
            s.linv[i, h] = inverse
            low = raised.astype(bf16)
            s.p[i, h] = low
            values = mixed[2 * KH + h * VAL : 2 * KH + (h + 1) * VAL, 0:T]
            attended = nn(values, low) * inverse
            s.att[i, h * VAL : (h + 1) * VAL] = attended
            s.act[i, h * VAL : (h + 1) * VAL] = (attended * sigmoid(attended)).astype(bf16)
        active = nt(s.eyet[...], s.act[i]).astype(bf16)
        projected = nn(active, s.projw[...])
        s.proj[i] = projected
        return first + fold(projected), second + fold(projected * projected)

    def zeros(width):
        return jnp.zeros((8, width), f32)

    def port(k, src, slot, offset, j):
        return pltpu.make_async_remote_copy(
            src_ref=src, dst_ref=slot, send_sem=s.ass.at[k, j], recv_sem=s.asr.at[k, j],
            device_id=offset, device_id_type=MESH)

    def sum_slots(buf, size):
        if size <= 32:
            whole = buf[0]
            for b in range(1, size):
                whole = whole + buf[b]
            return whole
        return lax.fori_loop(1, size, lambda b, c: c + buf[b], buf[0])

    def sum_copies(k):
        buf = z.bufs(s, k)[0]
        if z.direct:
            me = me_h * B + me_b
            return [port(k, buf.at[me], buf.at[me], at_offset(o), j) for j, o in enumerate(everyone())]
        return [port(k, buf.at[me_h], buf.at[me_h], {"head": lax.rem(me_h + j, H)}, j) for j in range(1, H)]

    def start_sum(k, rows):
        buf = z.bufs(s, k)[0]
        me = me_h * B + me_b if z.direct else me_h
        r = 0
        for row in rows:
            for c in range(row.shape[1] // 128):
                buf[me, r : r + 1, :] = row[:, c * 128 : (c + 1) * 128]
                r += 1
        for copy in sum_copies(k):
            copy.start()

    def finish_sum(k, width):
        for copy in sum_copies(k):
            copy.wait()
        bufs = z.bufs(s, k)
        if z.direct:
            whole = sum_slots(bufs[0], H * B)
        else:
            bufs[1][me_b] = sum_slots(bufs[0], H)
            around(B, lambda j: port(
                k, bufs[1].at[me_b], bufs[1].at[me_b], {"batch": lax.rem(me_b + j, B)}, H + j).start())
            around(B, lambda j: port(
                k, bufs[1].at[me_b], bufs[1].at[me_b], {"batch": lax.rem(me_b + j, B)}, H + j).wait())
            whole = sum_slots(bufs[1], B)
        step = width // 128
        return [
            jnp.concatenate([whole[r + c : r + c + 1] for c in range(step)], axis=1)
            for r in range(0, whole.shape[0], step)
        ]

    first, second = lax.fori_loop(0, n, attend, (zeros(D), zeros(D)))
    start_sum(0, [total(first), total(second)])
    for j in range(1, H):
        cot_copy(j).wait()
    c_cot.wait()
    lax.fori_loop(0, T // 16, enter_cotangent, 0)
    for k in range(2, 4):
        for j in range(1, H):
            weight_copy(k, j).wait()
    down = s.downg[...].reshape(F, D)
    s.w2t[...] = nt(s.eye[...], s.w2[...]).astype(bf16)
    gain_2w = jnp.concatenate([s.smallg[h, 0:1, :] for h in range(H)], axis=1)
    shift_2w = jnp.concatenate([s.smallg[h, 1:2, :] for h in range(H)], axis=1)
    around(B, lambda j: count_copy(j).wait())
    seen_part = sum_slots(s.cnt, B) * float(length)
    seen_row = jnp.concatenate([seen_part] * (D // 128), axis=1)
    sums = finish_sum(0, D)
    seen_wide = jnp.concatenate([seen_row] * (F // D), axis=1)

    def moments(first, second, seen):
        mean = first / seen
        return mean, lax.rsqrt(second / seen - mean * mean + EPSILON)

    mean_1, inverse_1 = moments(sums[0], sums[1], seen_row)
    a_1 = gain_1[...] * inverse_1
    b_1 = shift_1[...] - mean_1 * a_1

    def residual_of(i):
        return s.xpad[i, 0:T].astype(f32) + (s.proj[i] * a_1 + (b_1 * valid_of(i)) * s.rowmask[...])

    def enter(i, carry):
        first, second = carry
        residual = residual_of(i).astype(bf16)
        s.res[i] = residual
        hidden = nn(residual, s.upcat[...])
        s.hid[i] = hidden
        return first + fold(hidden), second + fold(hidden * hidden)

    first, second = lax.fori_loop(0, n, enter, (zeros(F), zeros(F)))
    start_sum(1, [total(first), total(second)])
    sums = finish_sum(1, F)
    mean_2, inverse_2 = moments(sums[0], sums[1], seen_wide)
    a_2 = gain_2w * inverse_2
    b_2 = shift_2w - mean_2 * a_2

    def leave(i, carry):
        one, two, three, four = carry
        shaped = s.hid[i] * a_2 + b_2
        gate = sigmoid(shaped)
        active = shaped * gate
        s.slope[i] = gate + active * (1.0 - gate)
        low = active.astype(bf16)
        s.act2[i] = low
        outgoing = nn(low, down)
        s.out[i] = outgoing
        valid = valid_of(i)
        upstream = s.u[i]
        masked = outgoing * (s.rowmask[...] * valid)
        return (one + fold(masked), two + fold(masked * outgoing), three + fold(upstream),
                four + fold(upstream * outgoing))

    sums = lax.fori_loop(0, n, leave, (zeros(D), zeros(D), zeros(D), zeros(D)))
    start_sum(2, [total(v) for v in sums])
    sums = finish_sum(2, D)
    mean_3, inverse_3 = moments(sums[0], sums[1], seen_row)
    a_3 = gain_3[...] * inverse_3
    b_3 = shift_3[...] - mean_3 * a_3
    sum_shift_3 = sums[2]
    sum_gain_3 = inverse_3 * (sums[3] - mean_3 * sum_shift_3)

    def back(gain, mean, inverse, sum_shift, sum_gain, seen):
        scaled = gain * inverse
        slope = -scaled * inverse * (sum_gain / seen)
        return scaled, slope, -scaled * (sum_shift / seen) - slope * mean

    s_3, v_3, r_3 = back(gain_3[...], mean_3, inverse_3, sum_shift_3, sum_gain_3, seen_row)

    def back_leave(i, carry):
        one, two = carry
        mask = s.rowmask[...] * valid_of(i)
        grad = (s.u[i] * s_3 + (s.out[i] * v_3 + r_3) * mask).astype(bf16)
        s.gproj[i, 0:T, :] = grad
        shaped = nt(grad, down) * s.slope[i]
        s.slope[i] = shaped
        return one + fold(shaped), two + fold(shaped * s.hid[i])

    def down_gradient(i, carry):
        turned = nt(s.eye[...], s.gproj[i, 0:T, :]).astype(bf16)
        s.gdown[...] += nn(turned, s.act2[i])
        s.tmp[...] = (residual_of(i) + (s.out[i] * a_3 + b_3)) * valid_of(i)
        for q in range(H):
            s.osend[q, i] = s.tmp[q * share : (q + 1) * share, :].astype(bf16)
        return carry

    first, second = lax.fori_loop(0, n, back_leave, (zeros(F), zeros(F)))
    start_sum(3, [total(first), total(second)])
    lax.fori_loop(0, n, down_gradient, 0)
    sums = finish_sum(3, F)

    sum_shift_2 = sums[0]
    sum_gain_2 = inverse_2 * (sums[1] - mean_2 * sum_shift_2)
    s_2, v_2, r_2 = back(gain_2w, mean_2, inverse_2, sum_shift_2, sum_gain_2, seen_wide)
    s.srow[0:1, :] = sum_gain_2
    s.srow[1:2, :] = sum_shift_2

    def back_enter(i, carry):
        one, two = carry
        mask = s.rowmask[...] * valid_of(i)
        grad = (s.slope[i] * s_2 + s.hid[i] * v_2 + r_2 * jnp.concatenate([mask] * (F // D), axis=1)).astype(bf16)
        s.act2[i] = grad
        upstream = s.u[i] + nt(grad, s.upcat[...])
        s.u[i] = upstream
        return one + fold(upstream), two + fold(upstream * s.proj[i])

    first, second = lax.fori_loop(0, n, back_enter, (zeros(D), zeros(D)))
    start_sum(4, [total(first), total(second)])

    def up_gradient(i, carry):
        turned = nt(s.eye[...], s.res[i]).astype(bf16)
        s.gup[...] += nn(turned, s.act2[i])
        return carry

    lax.fori_loop(0, n, up_gradient, 0)
    sums = finish_sum(4, D)
    for j in range(1, H):
        to_head(s.osend.at[lax.rem(me_h + j, H)], out_o.at[pl.ds(me_h * n, n)], 5, j).start()
    c_out = local(s.osend.at[me_h], out_o.at[pl.ds(me_h * n, n)], 6)
    sum_shift_1 = sums[0]
    sum_gain_1 = inverse_1 * (sums[1] - mean_1 * sum_shift_1)
    s_1, v_1, r_1 = back(gain_1[...], mean_1, inverse_1, sum_shift_1, sum_gain_1, seen_row)

    def back_project(i, carry):
        mask = s.rowmask[...] * valid_of(i)
        grad = (s.u[i] * s_1 + s.proj[i] * v_1 + r_1 * mask).astype(bf16)
        s.gproj[i, 0:T, :] = grad
        s.gpr[...] += nn(s.act[i], s.gproj[i])
        return carry

    lax.fori_loop(0, n, back_project, 0)

    def shares(buffer, k):
        for j in range(1, H):
            yield to_head(buffer[0].at[lax.rem(me_h + j, H)], buffer[1].at[me_h], k, j)

    def head_sum(buffer):
        whole = buffer[0][me_h].astype(f32)
        for j in range(1, H):
            whole = whole + buffer[1][lax.rem(me_h + j, H)].astype(f32)
        return whole

    def spread(src, dst, k, act):
        around(B, lambda j: act(to_batch(src(lax.rem(me_b + j, B)), dst, s.gbs.at[k, j], s.gbr.at[k, j], j)))

    def batch_sum(own, received):
        if B <= 8:
            whole = own
            for j in range(1, B):
                whole = whole + received[lax.rem(me_b + j, B)]
            return whole
        return lax.fori_loop(1, B, lambda j, c: c + received[lax.rem(me_b + j, B)], own)

    for h in range(H):
        s.ge1[h, 0:D, :] = s.gup[:, h * FH : (h + 1) * FH].astype(bf16)
        s.ge1[h, D : 2 * D, :] = s.gdown[:, h * FH : (h + 1) * FH].astype(bf16)
        for half in range(D // 128):
            at = 2 * D + half * PH
            s.ge1[h, at : at + PH, :] = s.gpr[h * PH : (h + 1) * PH, half * 128 : (half + 1) * 128].astype(bf16)
        if z.re > 2 * D + PH * (D // 128):
            s.ge1[h, 2 * D + PH * (D // 128) :, :] = jnp.zeros((z.re - 2 * D - PH * (D // 128), 128), bf16)
    for copy in shares((s.ge1, s.ge1r), 7):
        copy.start()

    def back_attend(i, carry):
        slope_gate = sigmoid(s.att[i])
        att = s.att[i]
        active = att * slope_gate
        gact = nt(s.projw[...], s.gproj[i]) * (slope_gate + active * (1.0 - slope_gate))
        for h in range(H):
            rows = slice(h * VAL, (h + 1) * VAL)
            grad = gact[rows] * s.linv[i, h]
            low = grad.astype(bf16)
            s.dabd[rows, h * L : (h + 1) * L] = low
            delta = total(grad * att[rows])
            weights_low = s.p[i, h]
            gscores = weights_low.astype(f32) * (nn(s.vnat[i], s.dabd[:, h * L : (h + 1) * L]) - delta)
            s.dbias[h] += gscores
            glow = gscores.astype(bf16)
            q_rows = slice(h * KEY, (h + 1) * KEY)
            k_rows = slice(KH + h * KEY, KH + (h + 1) * KEY)
            v_rows = slice(2 * KH + h * VAL, 2 * KH + (h + 1) * VAL)
            s.dmt[q_rows, :] = (nn(s.mt[i, k_rows, 0:T], glow) * scale).astype(bf16)
            s.dmt[k_rows, 0:T] = (nt(s.mt[i, q_rows, :], glow) * scale).astype(bf16)
            s.dmt[v_rows, 0:T] = nt(low, weights_low).astype(bf16)
        s.gqkv[...] += nn(s.dmt[...], s.xpad[i])
        turned = nn(s.w2t[...], s.dmt[...]).astype(bf16)
        s.tmp[...] = s.u[i] + nt(s.eyet[...], turned)
        for q in range(H):
            s.tsend[q, i] = s.tmp[q * share : (q + 1) * share, :].astype(bf16)
        for j in range(1, H):
            to_head(s.tsend.at[lax.rem(me_h + j, H), i], tg_o.at[me_h * n + i], 6, j).start()
        pltpu.make_async_copy(s.tsend.at[me_h, i], tg_o.at[me_h * n + i], s.loc.at[7]).start()
        return carry

    lax.fori_loop(0, n // 2, back_attend, 0)

    for copy in shares((s.ge1, s.ge1r), 7):
        copy.wait()
    s.ge2[...] = head_sum((s.ge1, s.ge1r)).reshape(B, z.re // B, 128)
    spread(lambda peer: s.ge2.at[peer], s.ge2r.at[me_b], 0, lambda c: c.start())

    lax.fori_loop(n // 2, n, back_attend, 0)

    spread(lambda peer: s.ge2.at[peer], s.ge2r.at[me_b], 0, lambda c: c.wait())
    s.ge3[me_b] = batch_sum(s.ge2[me_b], s.ge2r)
    spread(lambda peer: s.ge3.at[me_b], s.ge3.at[me_b], 1, lambda c: c.start())

    for h in range(H):
        for half in range(D // 128):
            lanes = slice(half * 128, (half + 1) * 128)
            at = half * C
            s.gl1[h, at : at + KEY, :] = s.gqkv[h * KEY : (h + 1) * KEY, lanes].astype(bf16)
            s.gl1[h, at + KEY : at + 2 * KEY, :] = s.gqkv[KH + h * KEY : KH + (h + 1) * KEY, lanes].astype(bf16)
            s.gl1[h, at + 2 * KEY : at + C, :] = s.gqkv[2 * KH + h * VAL : 2 * KH + (h + 1) * VAL, lanes].astype(bf16)
        if z.rl > C * (D // 128):
            s.gl1[h, C * (D // 128) :, :] = jnp.zeros((z.rl - C * (D // 128), 128), bf16)
    for copy in shares((s.gl1, s.gl1r), 8):
        copy.start()

    slot = lax.broadcasted_iota(jnp.int32, (T, L), 1)
    d_row, d_col = grid_of(slot)
    picks = []
    for down_sign in (1, -1):
        for right_sign in (1, -1):
            r = rows_s + down_sign * d_row
            c = cols_s + right_sign * d_col
            good = (r >= 0) & (r < SIDE) & (c >= 0) & (c < SIDE) & (slot < length)
            if down_sign < 0:
                good = good & (d_row > 0)
            if right_sign < 0:
                good = good & (d_col > 0)
            picks.append((jnp.where(good, r * SIDE + c, 0), good))
    bias_rows = []
    for h in range(H):
        whole = s.dbias[h]
        high = whole.astype(bf16)
        rest = (whole - high.astype(f32)).astype(bf16)
        ordered = nn(high, s.onehot[...]) + nn(rest, s.onehot[...])
        line = jnp.zeros((T, L), f32)
        for index, good in picks:
            line = line + jnp.where(good, take(ordered[:, 0:128], ordered[:, 128:256], index), 0.0)
        bias_rows.append(total(line * s.rowmask[...]))
    start_sum(5, bias_rows)

    for copy in shares((s.gl1, s.gl1r), 8):
        copy.wait()
    s.gl2[...] = head_sum((s.gl1, s.gl1r)).reshape(B, z.rl // B, 128)
    spread(lambda peer: s.gl2.at[peer], s.gl2r.at[me_b], 2, lambda c: c.start())
    for h, row in enumerate(finish_sum(5, L)):
        s.brow[h] = row
    spread(lambda peer: s.gl2.at[peer], s.gl2r.at[me_b], 2, lambda c: c.wait())
    s.gl3[me_b] = batch_sum(s.gl2[me_b], s.gl2r)
    spread(lambda peer: s.gl3.at[me_b], s.gl3.at[me_b], 3, lambda c: c.start())

    small_o[...] = jnp.zeros(small_o.shape, f32)
    small_o[0:1, :] = sum_gain_1
    small_o[1:2, :] = sum_shift_1
    small_o[2:3, :] = sum_gain_3
    small_o[3:4, :] = sum_shift_3
    small_o[4:5, 0:FH] = s.srow[0:1, own]
    small_o[5:6, 0:FH] = s.srow[1:2, own]
    small_o[6:7, :] = s.brow[me_h]

    spread(lambda peer: s.ge3.at[me_b], s.ge3.at[me_b], 1, lambda c: c.wait())
    early_o[...] = s.ge3[...].reshape(z.re, 128)
    spread(lambda peer: s.gl3.at[me_b], s.gl3.at[me_b], 3, lambda c: c.wait())
    late_o[...] = s.gl3[...].reshape(z.rl, 128)

    for j in range(1, H):
        to_head(s.osend.at[lax.rem(me_h + j, H)], out_o.at[pl.ds(me_h * n, n)], 5, j).wait()
        to_head(s.tsend.at[lax.rem(me_h + j, H)], tg_o.at[pl.ds(me_h * n, n)], 6, j).wait()
    c_out.wait()
    pltpu.make_async_copy(s.tsend.at[me_h], tg_o.at[pl.ds(me_h * n, n)], s.loc.at[7]).wait()


def finish_kernel(z, out_i, tg_i, early, late, small, out, tg, qkv, bias, proj, g1, s1, up, g2, s2, down, g3, s3):
    at = lax.broadcasted_iota(jnp.int32, (128, 128), 0)
    to = lax.broadcasted_iota(jnp.int32, (128, 128), 1)
    turn = jnp.where(lax.bitwise_and(at, 7) * 16 + lax.shift_right_logical(at, 3) == to, 1.0, 0.0).astype(bf16)
    for src, dst in ((out_i, out), (tg_i, tg)):
        rows = z.share // 16 * 16
        for k in range(0, rows, 16):
            dst[k : k + 16] = nn(turn, src[:, k : k + 16, :].reshape(128, z.D)).reshape(16, 8, z.D)
        for k in range(rows, z.share):
            dst[k] = src[:, k, :].astype(f32)

    @pl.when(pl.program_id(0) == 0)
    def _():
        D, C, PH = z.D, z.C, z.D // z.H
        up[...] = early[0:D, :]
        down[...] = early[D : 2 * D, :].T
        for half in range(D // 128):
            lanes = slice(half * 128, (half + 1) * 128)
            proj[:, lanes] = early[2 * D + half * PH : 2 * D + (half + 1) * PH, :]
            qkv[0, :, lanes] = late[half * C : (half + 1) * C, :]
        g1[...] = small[0:1, :]
        s1[...] = small[1:2, :]
        g3[...] = small[2:3, :]
        s3[...] = small[3:4, :]
        g2[...] = small[4:5, 0 : z.F // z.H]
        s2[...] = small[5:6, 0 : z.F // z.H]
        bias[...] = small[6:7, 0 : z.length]


def on_device(H, B, tokens, image_count, token_place, qkv_weight, bias_table, proj_weight, attention_gain,
              attention_shift, up_weight, hidden_gain, hidden_shift, down_weight, output_gain, output_shift,
              cotangent):
    images, length, width = tokens.shape
    z = types.SimpleNamespace(
        n=images // H, T=round_up(length, 16), L=round_up(length, 128), D=width, F=up_weight.shape[1] * H,
        H=H, B=B, C=qkv_weight.shape[1], share=cotangent.shape[1], length=length)
    z.re = round_up(2 * z.D + z.D // H * (z.D // 128), 8 * max(B, 2))
    z.rl = round_up(z.C * (z.D // 128), 8 * max(B, 2))
    z.direct = H == 4 and B <= 8
    z.ports = H * B if z.direct else H + B
    z.sums = {}
    for k, r in enumerate((2 * z.D, 2 * z.F, 4 * z.D, 2 * z.F, 2 * z.D, H * z.L)):
        z.sums["sum%d" % k] = pltpu.VMEM((H * B if z.direct else H, r // 128, 128), f32)
        if not z.direct:
            z.sums["part%d" % (k % 2)] = pltpu.VMEM((B, 8, 128), f32)

    def bufs(s, k):
        first = getattr(s, "sum%d" % k)
        return first, None if z.direct else getattr(s, "part%d" % (k % 2)).at[:, 0 : first.shape[1]]

    z.bufs = bufs
    scratch = layout(z)
    hbm = pl.BlockSpec(memory_space=pl.ANY)
    vmem = pl.BlockSpec(memory_space=pltpu.VMEM)
    smem = pl.BlockSpec(memory_space=pltpu.SMEM)
    outs = pl.pallas_call(
        functools.partial(block_kernel, z, tuple(scratch)),
        out_shape=(
            jax.ShapeDtypeStruct((images, z.share, width), bf16),
            jax.ShapeDtypeStruct((images, z.share, width), bf16),
            jax.ShapeDtypeStruct((z.re, 128), f32),
            jax.ShapeDtypeStruct((z.rl, 128), f32),
            jax.ShapeDtypeStruct((8, width), f32),
        ),
        in_specs=[hbm, smem, vmem, hbm, vmem, hbm, vmem, vmem, hbm, vmem, vmem, hbm, vmem, vmem, hbm],
        out_specs=(hbm, hbm, vmem, vmem, vmem),
        scratch_shapes=list(scratch.values()),
        compiler_params=pltpu.CompilerParams(
            collective_id=0, has_side_effects=True, vmem_limit_bytes=127 * 512 * 1024
        ),
    )(
        tokens.transpose(1, 0, 2), image_count, token_place.reshape(1, -1), qkv_weight, bias_table, proj_weight,
        attention_gain.reshape(1, -1), attention_shift.reshape(1, -1), up_weight, hidden_gain.reshape(1, -1),
        hidden_shift.reshape(1, -1), down_weight, output_gain.reshape(1, -1), output_shift.reshape(1, -1),
        cotangent.transpose(1, 0, 2),
    )

    steps = images // 8
    block = pl.BlockSpec((8, z.share, width), lambda i: (i, 0, 0))
    turned = pl.BlockSpec((z.share, 8, width), lambda i: (0, i, 0))

    def whole(*shape):
        return jax.ShapeDtypeStruct(shape, f32), pl.BlockSpec(shape, lambda i: (0,) * len(shape))

    fh = z.F // H
    small = [
        whole(1, z.C, width), whole(1, length), whole(width // H, width), whole(1, width), whole(1, width),
        whole(width, fh), whole(1, fh), whole(1, fh), whole(fh, width), whole(1, width), whole(1, width)]
    big = jax.ShapeDtypeStruct((z.share, images, width), f32)
    res = pl.pallas_call(
        functools.partial(finish_kernel, z),
        grid=(steps,),
        out_shape=[big, big] + [a for a, _ in small],
        in_specs=[block, block, whole(z.re, 128)[1], whole(z.rl, 128)[1], whole(8, width)[1]],
        out_specs=[turned, turned] + [b for _, b in small],
    )(*outs)
    res = [res[0].transpose(1, 0, 2), res[1].transpose(1, 0, 2), *res[2:]]
    for k in (5, 6, 8, 9, 11, 12):
        res[k] = res[k].reshape(-1)
    return tuple(res)


def solution(mesh):
    H, B = mesh.shape["head"], mesh.shape["batch"]
    placed = (
        P("batch", None, None),
        P("batch"),
        P(),
        P("head", None, None),
        P("head", None),
        P(),
        P(),
        P(),
        P(None, "head"),
        P("head"),
        P("head"),
        P("head", None),
        P(),
        P(),
        P("batch", "head", None),
    )
    return jax.shard_map(
        functools.partial(on_device, H, B),
        mesh=mesh,
        in_specs=placed,
        out_specs=(
            P("batch", "head", None),
            P("batch", "head", None),
            P("head", None, None),
            P("head", None),
            P("head", None),
            P(),
            P(),
            P(None, "head"),
            P("head"),
            P("head"),
            P("head", None),
            P(),
            P(),
        ),
        check_vma=False,
    )
```

```python
import functools
import types

import jax
import jax.numpy as jnp
from jax import lax
from jax.experimental import pallas as pl
from jax.experimental.pallas import tpu as pltpu
from jax.sharding import PartitionSpec as P

KEY = 32
VAL = 64
SIDE = 14
EPSILON = 1e-05
LOG2E = 1.4426950408889634
MESH = pl.DeviceIdType.MESH
f32 = jnp.float32
bf16 = jnp.bfloat16


def nn(left, right):
    return lax.dot_general(left, right, (((1,), (0,)), ((), ())), preferred_element_type=f32)


def nt(left, right):
    return lax.dot_general(left, right, (((1,), (1,)), ((), ())), preferred_element_type=f32)


def tn(left, right):
    return lax.dot_general(left, right, (((0,), (0,)), ((), ())), preferred_element_type=f32)


def among(block, at, total_rows):
    parts = []
    if at > 0:
        parts.append(jnp.zeros((at, block.shape[1]), block.dtype))
    parts.append(block)
    if at + block.shape[0] < total_rows:
        parts.append(jnp.zeros((total_rows - at - block.shape[0], block.shape[1]), block.dtype))
    return jnp.concatenate(parts, axis=0)


def spaced(value, heads):
    rows, columns = value.shape
    each = columns // heads
    lane = lax.broadcasted_iota(jnp.int32, (rows, columns), 1)
    return jnp.concatenate(
        [jnp.where((lane >= h * each) & (lane < (h + 1) * each), value, jnp.zeros_like(value)) for h in range(heads)],
        axis=0)


def round_up(value, step):
    return -(-value // step) * step


def sigmoid(value):
    return 0.5 * jnp.tanh(0.5 * value) + 0.5


def fold(value):
    rows, columns = value.shape
    return jnp.sum(value.reshape(rows // 8, 8, columns), axis=0)


def total(value):
    return jnp.sum(value, axis=0, keepdims=True)


def lookup(table, index):
    rows = index.shape[0]
    low = jnp.broadcast_to(table[:, 0:128], (rows, 128))
    high = jnp.broadcast_to(table[:, 128:256], (rows, 128))
    return take(low, high, index)


def take(low, high, index):
    parts = []
    for half in range(2):
        at = index[:, half * 128 : (half + 1) * 128]
        inside = lax.bitwise_and(at, 127)
        first = jnp.take_along_axis(low, inside, axis=1, mode="promise_in_bounds")
        second = jnp.take_along_axis(high, inside, axis=1, mode="promise_in_bounds")
        parts.append(jnp.where(at < 128, first, second))
    return jnp.concatenate(parts, axis=1)


def layout(z):
    n, T, L, D, F, H, B, C = z.n, z.T, z.L, z.D, z.F, z.H, z.B, z.C
    dma = pltpu.SemaphoreType.DMA
    vmem = pltpu.VMEM
    return {
        "xt": vmem((T, 16, D), bf16),
        "ct": vmem((T, 16, D), bf16),
        "mix": vmem((n * 16, 256), bf16),
        "qkvg": vmem((H, C, D), bf16),
        "downg": vmem((H, F // H, D), bf16),
        "smallg": vmem((H, 4, 128), f32),
        "w2": vmem((H * C, D), bf16),
        "upcat": vmem((D, F), bf16),
        "projw": vmem((D, D), bf16),
        "bias": vmem((H, T, L), f32),
        "dbias": vmem((H, T, L), f32),
        "rowmask": vmem((T, D), f32),
        "onehot": vmem((L, L), bf16),
        "xpad": vmem((n, L, D), bf16),
        "qt": vmem((n, H * KEY, L), bf16),
        "knat": vmem((n, T, H * KEY), bf16),
        "vnat": vmem((n, T, H * VAL), bf16),
        "tmp": vmem((z.group, T, D), f32),
        "p": vmem((n, H, T, L), bf16),
        "linv": vmem((n, H, 1, L), f32),
        "att": vmem((n, H * VAL, L), f32),
        "act": vmem((n, H * VAL, L), bf16),
        "proj": vmem((n, T, D), f32),
        "hid": vmem((n, T, F), f32),
        "slope": vmem((n, T, F), f32),
        "act2": vmem((n, T, F), bf16),
        "out": vmem((n, T, D), f32),
        "u": vmem((n, T, D), f32),
        "gproj": vmem((n, L, D), bf16),
        "osend": vmem((H, n, z.share, D), bf16),
        "tsend": vmem((H, n, z.share, D), bf16),
        "gdown": vmem((D, F), f32),
        "gup": vmem((D, F), f32),
        "gpr": vmem((D, D), f32),
        "gqkv": vmem((H * C, D), f32),
        "srow": vmem((2, F), f32),
        "brow": vmem((H, 1, L), f32),
        **z.sums,
        "cnt": vmem((B, 1, 128), f32),
        "ge1": vmem((H, z.re, 128), bf16),
        "ge1r": vmem((H, z.re, 128), bf16),
        "ge2": vmem((B, z.re // B, 128), f32),
        "ge2r": vmem((B, z.re // B, 128), f32),
        "ge3": vmem((B, z.re // B, 128), f32),
        "gl1": vmem((H, z.rl, 128), bf16),
        "gl1r": vmem((H, z.rl, 128), bf16),
        "gl2": vmem((B, z.rl // B, 128), f32),
        "gl2r": vmem((B, z.rl // B, 128), f32),
        "gl3": vmem((B, z.rl // B, 128), f32),
        "loc": dma((8,)),
        "hs": dma((9,)),
        "hr": dma((9,)),
        "ass": dma((12,)),
        "asr": dma((12,)),
        "bs": dma((7,)),
        "br": dma((7,)),
        "ready": pltpu.SemaphoreType.REGULAR,
    }


def block_kernel(z, names, *refs):
    (tokens, count, place, qkv_w, table, proj_w, gain_1, shift_1, up_w, gain_2, shift_2, down_w,
     gain_3, shift_3, cot, out_o, tg_o, early_o, late_o, small_o) = refs[:20]
    s = types.SimpleNamespace(**dict(zip(names, refs[20:], strict=True)))
    n, T, L, D, F, H, B, C = z.n, z.T, z.L, z.D, z.F, z.H, z.B, z.C
    share, length = z.share, z.length
    me_h = lax.axis_index("head")
    me_b = lax.axis_index("batch")

    def local(src, dst, k):
        copy = pltpu.make_async_copy(src, dst, s.loc.at[k])
        copy.start()
        return copy

    def to_head(src, dst, k, j):
        return pltpu.make_async_remote_copy(
            src_ref=src, dst_ref=dst, send_sem=s.hs.at[k], recv_sem=s.hr.at[k],
            device_id={"head": head_peers[j]}, device_id_type=MESH)

    def to_batch(src, dst, k, peer):
        return pltpu.make_async_remote_copy(
            src_ref=src, dst_ref=dst, send_sem=s.bs.at[k], recv_sem=s.br.at[k],
            device_id={"batch": peer}, device_id_type=MESH)

    head_peers = [lax.rem(me_h + j, H) for j in range(H)]
    core = lax.rem(me_b, 2)
    sibling = me_b + 1 - 2 * core

    def done(copies):
        copies.wait()

    def around(size, step):
        if size <= 8:
            for j in range(1, size):
                step(j)
        else:
            lax.fori_loop(1, size, lambda j, c: (step(j), c)[1], 0)

    FH = F // H
    PH = D // H
    own = pl.ds(pl.multiple_of(me_h * FH, FH), FH)
    qkv_32, up_32, down_32 = s.gqkv.at[0:C], s.gup.at[:, 0:FH], s.gdown.at[0:FH, 0:D]
    c_qkv = local(qkv_w.at[0], qkv_32, 0)
    c_up = local(up_w, up_32, 1)
    c_down = local(down_w, down_32, 2)
    def window(slot):
        return pl.multiple_of(slot * n // 8 * 8, 8)

    c_tok = local(tokens.at[:, pl.ds(window(me_h), 16)], s.xt.at[pl.ds(0, length)], 3)
    c_proj = local(proj_w, s.gpr, 4)

    def everyone():
        pairs = [(a, b) for a in range(H) for b in range(B) if a or b]
        return sorted(pairs, key=lambda p: -(p[0] % 2 + p[0] // 2 + (2 if p[1] > 1 else p[1] / 4)))

    def at_offset(a, b):
        x, y = lax.rem(me_h, 2), lax.div(me_h, 2)
        other = (y + a // 2 - 2 * y * (a // 2)) * 2 + x + a % 2 - 2 * x * (a % 2)
        return {"head": other, "batch": lax.rem(me_b + b, B)}

    barrier = pltpu.get_barrier_semaphore()
    for j in range(1, H):
        pl.semaphore_signal(barrier, inc=1, device_id={"head": head_peers[j]}, device_id_type=MESH)

    def greet(semaphore):
        around(B, lambda j: pl.semaphore_signal(
            semaphore, inc=1, device_id={"batch": lax.rem(me_b + j, B)}, device_id_type=MESH))

    greet(barrier)
    targets = [at_offset(*pair) for pair in everyone()] if z.direct else []

    s.smallg[me_h] = jnp.concatenate(
        [gain_2[...], shift_2[...], table[:, 0:128], jnp.concatenate(
            [table[:, 128:length], jnp.zeros((1, 256 - length), f32)], axis=1)], axis=0)
    c_qkv.wait()
    s.qkvg[me_h] = qkv_32[...].astype(bf16)
    up_rows = pl.ds(pl.multiple_of(core * (D // 2), D // 2), D // 2)
    down_rows = pl.ds(pl.multiple_of(core * (FH // 2), FH // 2), FH // 2)
    c_up.wait()
    s.upcat[up_rows, own] = s.gup[up_rows, 0:FH].astype(bf16)
    c_down.wait()
    s.downg[me_h, down_rows] = s.gdown[down_rows, 0:D].astype(bf16)

    s.cnt[me_b] = jnp.full((1, 128), count[0]).astype(f32)
    pl.semaphore_wait(barrier, H - 1 + B - 1)

    shared = (s.qkvg.at[me_h], s.smallg.at[me_h], s.upcat.at[up_rows, own], s.downg.at[me_h, down_rows])
    for k in (1, 0, 2, 3):
        for j in range(1, H):
            to_head(shared[k], shared[k], k, j).start()
    greet(s.ready)

    cuts = (0, share // 2, share * 5 // 6, share)

    def send_cotangent(piece):
        low, high = cuts[piece], cuts[piece + 1]
        for j in range(1, H):
            to_head(cot.at[pl.ds(low, high - low), pl.ds(window(head_peers[j]), 16)],
                    s.ct.at[pl.ds(me_h * share + low, high - low)], 4, j).start()

    around(B, lambda j: to_batch(s.cnt.at[me_b], s.cnt.at[me_b], 0, lax.rem(me_b + j, B)).start())
    send_cotangent(0)
    c_cot = local(cot.at[:, pl.ds(window(me_h), 16)], s.ct.at[pl.ds(me_h * share, share)], 5)

    row_at = lax.broadcasted_iota(jnp.int32, (L, L), 0)
    lane_at = lax.broadcasted_iota(jnp.int32, (L, L), 1)
    s.rowmask[...] = jnp.where(row_at < length, 1.0, 0.0)[0:T]
    place_lane = jnp.broadcast_to(
        jnp.concatenate([place[...].astype(f32), jnp.zeros((1, L - length), f32)], axis=1), (L, L))
    place_row = place_lane.T
    s.onehot[...] = jnp.where((place_row == lane_at.astype(f32)) & (row_at < length), 1.0, 0.0).astype(bf16)

    def grid_of(at):
        at = at.astype(jnp.int32)
        row = lax.shift_right_logical(at * 4682, 16)
        return row, at - row * SIDE

    rows_t, cols_t = grid_of(place_lane[0:T])
    rows_s, cols_s = grid_of(place_row[0:T])
    offsets = jnp.abs(rows_s - rows_t) * SIDE + jnp.abs(cols_s - cols_t)
    for h in range(H):
        s.dbias[h] = jnp.zeros((T, L), f32)
    s.gdown[...] = jnp.zeros(s.gdown.shape, f32)
    s.gup[...] = jnp.zeros(s.gup.shape, f32)
    s.gqkv[...] = jnp.zeros(s.gqkv.shape, f32)

    def valid_of(i):
        return jnp.where(me_h * n + i < count[0], 1.0, 0.0)

    c_proj.wait()
    s.projw[...] = s.gpr[...].astype(bf16)
    s.gpr[...] = jnp.zeros(s.gpr.shape, f32)
    line_at = lax.broadcasted_iota(jnp.int32, (n * 16, 256), 0)
    pick_at = lax.broadcasted_iota(jnp.int32, (n * 16, 256), 1)
    image_at = lax.shift_right_logical(line_at, 4)
    s.mix[...] = jnp.where(
        (lax.bitwise_and(line_at, 15) == lax.shift_right_logical(pick_at, 4))
        & (lax.bitwise_and(pick_at, 15) == image_at + (me_h * n - window(me_h)))
        & (image_at + me_h * n < count[0]),
        1.0, 0.0).astype(bf16)
    s.xt[length:T] = jnp.zeros((T - length, 16, D), bf16)
    s.ct[length:T] = jnp.zeros((T - length, 16, D), bf16)
    s.xpad[:, T:L, :] = jnp.zeros((n, L - T, D), bf16)
    s.gproj[:, T:L, :] = jnp.zeros((n, L - T, D), bf16)
    c_tok.wait()

    def enter_tokens(k, carry):
        at = pl.ds(pl.multiple_of(k * 16, 16), 16)
        s.xpad[:, at, :] = nn(s.mix[...], s.xt[at].reshape(256, D)).astype(bf16).reshape(n, 16, D)
        return carry

    def enter_cotangent(k, carry):
        at = pl.ds(pl.multiple_of(k * 16, 16), 16)
        s.u[:, at, :] = nn(s.mix[...], s.ct[at].reshape(256, D)).reshape(n, 16, D)
        return carry

    lax.fori_loop(0, T // 16, enter_tokens, 0)

    some = pl.ds(0, H - 1)
    done(to_head(s.smallg.at[some], s.smallg.at[some], 1, 1))
    for h in range(H):
        line = jnp.concatenate([s.smallg[h, 2:3, :], s.smallg[h, 3:4, :]], axis=1)
        s.bias[h] = jnp.where(row_at[0:T] < length, lookup(line, offsets) * LOG2E, -1e30)
    done(to_head(s.qkvg.at[some], s.qkvg.at[some], 0, 1))
    for h in range(H):
        s.w2[h * KEY : (h + 1) * KEY] = s.qkvg[h, 0:KEY]
        s.w2[(H + h) * KEY : (H + h + 1) * KEY] = s.qkvg[h, KEY : 2 * KEY]
        at = 2 * H * KEY + h * VAL
        s.w2[at : at + VAL] = s.qkvg[h, 2 * KEY : C]

    scale = KEY**-0.5
    KH, VH = H * KEY, H * VAL

    def attend(i, carry):
        first, second = carry
        at = [i * z.group + u for u in range(z.group)]
        mixed, scores = [], []
        for j in at:
            x = s.xpad[j]
            mixed.append(nt(s.w2[...], x).astype(bf16))
            s.qt[j] = mixed[-1][0:KH]
            natural = nt(x[0:T], s.w2[KH : H * C]).astype(bf16)
            s.knat[j] = natural[:, 0:KH]
            s.vnat[j] = natural[:, KH:]
            scores.append(natural[:, 0:KH])
        for u in range(z.group):
            scores[u] = nn(spaced(scores[u], H), mixed[u][0:KH])
        for h in range(H):
            for u, j in enumerate(at):
                logits = scores[u][h * T : (h + 1) * T] * (scale * LOG2E) + s.bias[h]
                raised = jnp.exp2(logits - jnp.max(logits, axis=0, keepdims=True))
                inverse = 1.0 / total(raised)
                s.linv[j, h] = inverse
                low = raised.astype(bf16)
                s.p[j, h] = low
                values = mixed[u][2 * KH + h * VAL : 2 * KH + (h + 1) * VAL, 0:T]
                attended = nn(values, low) * inverse
                s.att[j, h * VAL : (h + 1) * VAL] = attended
                s.act[j, h * VAL : (h + 1) * VAL] = (attended * sigmoid(attended)).astype(bf16)
        for j in at:
            projected = tn(s.act[j], s.projw[...])[0:T] * s.rowmask[...]
            s.proj[j] = projected
            first, second = first + fold(projected), second + fold(projected * projected)
        return first, second

    def zeros(width):
        return jnp.zeros((8, width), f32)

    def port(k, src, dst, device):
        return pltpu.make_async_remote_copy(
            src_ref=src, dst_ref=dst, send_sem=s.ass.at[k], recv_sem=s.asr.at[k],
            device_id=device, device_id_type=MESH)

    def sum_slots(buf, size):
        if size <= 32:
            whole = buf[0]
            for b in range(1, size):
                whole = whole + buf[b]
            return whole
        return lax.fori_loop(1, size, lambda b, c: c + buf[b], buf[0])

    def start_sum(k, rows):
        buf = z.bufs(s, k)[0]
        me = me_h * B + me_b if z.direct else me_h
        r = 0
        for row in rows:
            for c in range(row.shape[1] // 128):
                buf[me, r : r + 1, :] = row[:, c * 128 : (c + 1) * 128]
                r += 1
        for target in targets if z.direct else [{"head": p} for p in head_peers[1:]]:
            port(k, buf.at[me], buf.at[me], target).start()

    def finish_sum(k, width):
        others = z.bufs(s, k)[0].at[pl.ds(0, H * B - 1 if z.direct else H - 1)]
        done(port(k, others, others, {"head": head_peers[1]}))
        bufs = z.bufs(s, k)
        if z.direct:
            whole = sum_slots(bufs[0], H * B)
        else:
            bufs[1][me_b] = sum_slots(bufs[0], H)
            mine = bufs[1].at[me_b]
            around(B, lambda j: port(k + 6, mine, mine, {"batch": lax.rem(me_b + j, B)}).start())
            others = bufs[1].at[pl.ds(0, B - 1)]
            done(port(k + 6, others, others, {"batch": lax.rem(me_b + 1, B)}))
            whole = sum_slots(bufs[1], B)
        step = width // 128
        return [
            jnp.concatenate([whole[r + c : r + c + 1] for c in range(step)], axis=1)
            for r in range(0, whole.shape[0], step)
        ]

    first, second = lax.fori_loop(0, n // z.group, attend, (zeros(D), zeros(D)))
    pl.semaphore_wait(s.ready, B - 1)
    some_rows = pl.ds(0, D // 2)
    done(to_head(s.upcat.at[some_rows, pl.ds(0, FH * (H - 1))], s.upcat.at[some_rows, pl.ds(0, FH * (H - 1))], 2, 1))
    down_some = s.downg.at[some, pl.ds(0, FH // 2)]
    done(to_head(down_some, down_some, 3, 1))
    halves = (s.upcat.at[up_rows, :], s.downg.at[:, down_rows])
    for k in range(2):
        to_batch(halves[k], halves[k], k + 1, sibling).start()
    start_sum(0, [total(first), total(second)])
    send_cotangent(1)
    for k in range(2):
        to_batch(halves[k], halves[k], k + 1, sibling).wait()
    down = s.downg[...].reshape(F, D)
    gain_2w = jnp.concatenate([s.smallg[h, 0:1, :] for h in range(H)], axis=1)
    shift_2w = jnp.concatenate([s.smallg[h, 1:2, :] for h in range(H)], axis=1)
    others = s.cnt.at[pl.ds(0, B - 1)]
    done(to_batch(others, others, 0, sibling))
    seen_part = sum_slots(s.cnt, B) * float(length)
    seen_row = jnp.concatenate([seen_part] * (D // 128), axis=1)
    sums = finish_sum(0, D)
    seen_wide = jnp.concatenate([seen_row] * (F // D), axis=1)

    def moments(first, second, seen):
        mean = first / seen
        return mean, lax.rsqrt(second / seen - mean * mean + EPSILON)

    mean_1, inverse_1 = moments(sums[0], sums[1], seen_row)
    a_1 = gain_1[...] * inverse_1
    b_1 = shift_1[...] - mean_1 * a_1

    G = z.group
    GT = G * T

    def group(ref, i):
        return ref[pl.ds(i * G, G), 0:T].reshape(GT, ref.shape[2])

    def put(ref, i, value):
        ref[pl.ds(i * G, G), 0:T] = value.reshape(G, T, value.shape[1])

    def mask_of(i):
        return jnp.concatenate([s.rowmask[...] * valid_of(i * G + u) for u in range(G)], axis=0)

    def residual_of(i):
        return group(s.xpad, i).astype(f32) + (group(s.proj, i) * a_1 + b_1 * mask_of(i))

    def enter(i, carry):
        first, second = carry
        residual = residual_of(i).astype(bf16)
        hidden = nn(residual, s.upcat[...])
        put(s.hid, i, hidden)
        return first + fold(hidden), second + fold(hidden * hidden)

    first, second = lax.fori_loop(0, n // G, enter, (zeros(F), zeros(F)))
    start_sum(1, [total(first), total(second)])
    send_cotangent(2)
    others = s.ct.at[pl.ds(0, share * (H - 1))]
    done(to_head(others, others, 4, 1))
    c_cot.wait()
    lax.fori_loop(0, T // 16, enter_cotangent, 0)
    sums = finish_sum(1, F)
    mean_2, inverse_2 = moments(sums[0], sums[1], seen_wide)
    a_2 = gain_2w * inverse_2
    b_2 = shift_2w - mean_2 * a_2

    def leave(i, carry):
        one, two, three, four = carry
        shaped = group(s.hid, i) * a_2 + b_2
        gate = sigmoid(shaped)
        active = shaped * gate
        put(s.slope, i, gate + active * (1.0 - gate))
        low = active.astype(bf16)
        put(s.act2, i, low)
        outgoing = nn(low, down)
        put(s.out, i, outgoing)
        upstream = group(s.u, i)
        masked = outgoing * mask_of(i)
        return (one + fold(masked), two + fold(masked * outgoing), three + fold(upstream),
                four + fold(upstream * outgoing))

    sums = lax.fori_loop(0, n // G, leave, (zeros(D), zeros(D), zeros(D), zeros(D)))
    start_sum(2, [total(v) for v in sums])
    sums = finish_sum(2, D)
    mean_3, inverse_3 = moments(sums[0], sums[1], seen_row)
    a_3 = gain_3[...] * inverse_3
    b_3 = shift_3[...] - mean_3 * a_3
    sum_shift_3 = sums[2]
    sum_gain_3 = inverse_3 * (sums[3] - mean_3 * sum_shift_3)

    def back(gain, mean, inverse, sum_shift, sum_gain, seen):
        scaled = gain * inverse
        slope = -scaled * inverse * (sum_gain / seen)
        return scaled, slope, -scaled * (sum_shift / seen) - slope * mean

    s_3, v_3, r_3 = back(gain_3[...], mean_3, inverse_3, sum_shift_3, sum_gain_3, seen_row)

    def back_leave(i, carry):
        one, two = carry
        grad = (group(s.u, i) * s_3 + (group(s.out, i) * v_3 + r_3) * mask_of(i)).astype(bf16)
        put(s.gproj, i, grad)
        shaped = nt(grad, down) * group(s.slope, i)
        put(s.slope, i, shaped)
        return one + fold(shaped), two + fold(shaped * group(s.hid, i))

    def down_gradient(i, carry):
        s.gdown[...] += tn(group(s.gproj, i), group(s.act2, i))
        return carry

    def output(i, carry):
        s.tmp[...] = ((residual_of(i) + (group(s.out, i) * a_3 + b_3)) * mask_of(i)).reshape(G, T, D)
        for u in range(G):
            for q in range(H):
                s.osend[q, i * G + u] = s.tmp[u, q * share : (q + 1) * share, :].astype(bf16)
        return carry

    def send_output(i):
        to = out_o.at[pl.ds(me_h * n + i * G, G)]
        for j in range(1, H):
            to_head(s.osend.at[head_peers[j], pl.ds(i * G, G)], to, 5, j).start()

    first, second = lax.fori_loop(0, n // G, back_leave, (zeros(F), zeros(F)))
    start_sum(3, [total(first), total(second)])
    lax.fori_loop(0, n // G, output, 0)
    send_output(0)
    lax.fori_loop(0, n // G, down_gradient, 0)
    sums = finish_sum(3, F)

    sum_shift_2 = sums[0]
    sum_gain_2 = inverse_2 * (sums[1] - mean_2 * sum_shift_2)
    s_2, v_2, r_2 = back(gain_2w, mean_2, inverse_2, sum_shift_2, sum_gain_2, seen_wide)
    s.srow[0:1, :] = sum_gain_2
    s.srow[1:2, :] = sum_shift_2

    def back_enter(i, carry):
        one, two = carry
        mask = jnp.concatenate([mask_of(i)] * (F // D), axis=1)
        grad = (group(s.slope, i) * s_2 + group(s.hid, i) * v_2 + r_2 * mask).astype(bf16)
        put(s.act2, i, grad)
        upstream = group(s.u, i) + nt(grad, s.upcat[...])
        put(s.u, i, upstream)
        return one + fold(upstream), two + fold(upstream * group(s.proj, i))

    first, second = lax.fori_loop(0, n // G, back_enter, (zeros(D), zeros(D)))
    start_sum(4, [total(first), total(second)])

    def up_gradient(i, carry):
        s.gup[...] += tn(residual_of(i).astype(bf16), group(s.act2, i))
        return carry

    if n // G > 1:
        send_output(1)
    lax.fori_loop(0, n // G, up_gradient, 0)
    sums = finish_sum(4, D)
    c_out = local(s.osend.at[me_h], out_o.at[pl.ds(me_h * n, n)], 6)
    sum_shift_1 = sums[0]
    sum_gain_1 = inverse_1 * (sums[1] - mean_1 * sum_shift_1)
    s_1, v_1, r_1 = back(gain_1[...], mean_1, inverse_1, sum_shift_1, sum_gain_1, seen_row)

    def back_project(i, carry):
        grad = (group(s.u, i) * s_1 + group(s.proj, i) * v_1 + r_1 * mask_of(i)).astype(bf16)
        put(s.gproj, i, grad)
        whole = s.gpr[...]
        for u in range(G):
            whole = whole + nn(s.act[i * G + u], s.gproj[i * G + u])
        s.gpr[...] = whole
        return carry

    lax.fori_loop(0, n // G, back_project, 0)

    def shares(buffer, k):
        for j in range(1, H):
            to_head(buffer[0].at[head_peers[j]], buffer[1].at[me_h], k, j).start()

    def shares_done(buffer, k):
        done(to_head(buffer[0].at[some], buffer[1].at[some], k, 1))

    def head_sum(buffer):
        whole = buffer[0][me_h].astype(f32)
        for j in range(1, H):
            whole = whole + buffer[1][head_peers[j]].astype(f32)
        return whole

    def spread(src, dst, k):
        around(B, lambda j: to_batch(src(lax.rem(me_b + j, B)), dst, k, lax.rem(me_b + j, B)).start())

    def spread_done(src, dst, k):
        others = pl.ds(0, B - 1)
        done(to_batch(src.at[others], dst.at[others], k, sibling))

    def batch_sum(own, received):
        if B <= 8:
            whole = own
            for j in range(1, B):
                whole = whole + received[lax.rem(me_b + j, B)]
            return whole
        return lax.fori_loop(1, B, lambda j, c: c + received[lax.rem(me_b + j, B)], own)

    for h in range(H):
        s.ge1[h, 0:D, :] = s.gup[:, h * FH : (h + 1) * FH].astype(bf16)
        s.ge1[h, D : 2 * D, :] = s.gdown[:, h * FH : (h + 1) * FH].astype(bf16)
        for half in range(D // 128):
            at = 2 * D + half * PH
            s.ge1[h, at : at + PH, :] = s.gpr[h * PH : (h + 1) * PH, half * 128 : (half + 1) * 128].astype(bf16)
        if z.re > 2 * D + PH * (D // 128):
            s.ge1[h, 2 * D + PH * (D // 128) :, :] = jnp.zeros((z.re - 2 * D - PH * (D // 128), 128), bf16)
    shares((s.ge1, s.ge1r), 7)
    for i in range(2, n // G):
        send_output(i)

    GB = z.group_back

    def back_attend(i, carry, send=True):
        at = [i * GB + u for u in range(GB)]
        lows, deltas, products = [], [], []
        for j in at:
            att = s.att[j]
            gate = sigmoid(att)
            active = att * gate
            gact = nt(s.projw[...], s.gproj[j]) * (gate + active * (1.0 - gate))
            low, delta = [], []
            for h in range(H):
                rows = slice(h * VAL, (h + 1) * VAL)
                grad = gact[rows] * s.linv[j, h]
                low.append(grad.astype(bf16))
                delta.append(total(grad * att[rows]))
            lows.append(low)
            deltas.append(delta)
            products.append(nn(spaced(s.vnat[j], H), jnp.concatenate(low, axis=0)))
        grads = [[] for _ in at]
        for h in range(H):
            whole = None
            for u, j in enumerate(at):
                gscores = s.p[j, h].astype(f32) * (products[u][h * T : (h + 1) * T] - deltas[u][h])
                whole = gscores if whole is None else whole + gscores
                grads[u].append(gscores.astype(bf16))
            s.dbias[h] += whole
        mixes = []
        for u, j in enumerate(at):
            queries = s.qt[j]
            near = jnp.concatenate(
                [among(queries[h * KEY : (h + 1) * KEY], h * KEY, KH) for h in range(H)], axis=1)
            far = jnp.concatenate([among(lows[u][h], h * VAL, VH) for h in range(H)], axis=1)
            grad_k = nt(jnp.concatenate(grads[u], axis=1), near) * scale
            grad_v = nt(jnp.concatenate([s.p[j, h] for h in range(H)], axis=1), far)
            grad_q = tn(jnp.concatenate(grads[u], axis=0), spaced(s.knat[j], H))[0:T] * scale
            mixes.append(jnp.concatenate([v.astype(bf16) for v in (grad_q, grad_k, grad_v)], axis=1))
        whole = s.gqkv[...]
        for u, j in enumerate(at):
            whole = whole + tn(mixes[u], s.xpad[j, 0:T])
        s.gqkv[...] = whole
        terms = nn(jnp.concatenate(mixes, axis=0), s.w2[...])
        for u, j in enumerate(at):
            s.tmp[u] = s.u[j] + terms[u * T : (u + 1) * T]
            for q in range(H):
                s.tsend[q, j] = s.tmp[u, q * share : (q + 1) * share, :].astype(bf16)
        if send:
            send_tokens(i)
        return carry

    def send_tokens(i):
        to = tg_o.at[pl.ds(me_h * n + i * GB, GB)]
        for j in range(1, H):
            to_head(s.tsend.at[head_peers[j], pl.ds(i * GB, GB)], to, 6, j).start()
        pltpu.make_async_copy(s.tsend.at[me_h, pl.ds(i * GB, GB)], to, s.loc.at[7]).start()

    last = n // GB - 1
    lax.fori_loop(0, last, back_attend, 0)
    shares_done((s.ge1, s.ge1r), 7)
    s.ge2[...] = head_sum((s.ge1, s.ge1r)).reshape(B, z.re // B, 128)
    spread(lambda peer: s.ge2.at[peer], s.ge2r.at[me_b], 3)
    lax.fori_loop(last, last + 1, functools.partial(back_attend, send=False), 0)

    for h in range(H):
        for half in range(D // 128):
            lanes = slice(half * 128, (half + 1) * 128)
            at = half * C
            s.gl1[h, at : at + KEY, :] = s.gqkv[h * KEY : (h + 1) * KEY, lanes].astype(bf16)
            s.gl1[h, at + KEY : at + 2 * KEY, :] = s.gqkv[KH + h * KEY : KH + (h + 1) * KEY, lanes].astype(bf16)
            s.gl1[h, at + 2 * KEY : at + C, :] = s.gqkv[2 * KH + h * VAL : 2 * KH + (h + 1) * VAL, lanes].astype(bf16)
        if z.rl > C * (D // 128):
            s.gl1[h, C * (D // 128) :, :] = jnp.zeros((z.rl - C * (D // 128), 128), bf16)
    shares((s.gl1, s.gl1r), 8)
    spread_done(s.ge2, s.ge2r, 3)
    s.ge3[me_b] = batch_sum(s.ge2[me_b], s.ge2r)
    spread(lambda peer: s.ge3.at[me_b], s.ge3.at[me_b], 4)
    send_tokens(last)

    slot = lax.broadcasted_iota(jnp.int32, (T, L), 1)
    d_row, d_col = grid_of(slot)
    picks = []
    for down_sign in (1, -1):
        for right_sign in (1, -1):
            r = rows_s + down_sign * d_row
            c = cols_s + right_sign * d_col
            good = (r >= 0) & (r < SIDE) & (c >= 0) & (c < SIDE) & (slot < length)
            if down_sign < 0:
                good = good & (d_row > 0)
            if right_sign < 0:
                good = good & (d_col > 0)
            picks.append((jnp.where(good, r * SIDE + c, 0), good))
    bias_rows = []
    for h in range(H):
        whole = s.dbias[h]
        high = whole.astype(bf16)
        rest = (whole - high.astype(f32)).astype(bf16)
        ordered = nn(high, s.onehot[...]) + nn(rest, s.onehot[...])
        line = jnp.zeros((T, L), f32)
        for index, good in picks:
            line = line + jnp.where(good, take(ordered[:, 0:128], ordered[:, 128:256], index), 0.0)
        bias_rows.append(total(line * s.rowmask[...]))
    start_sum(5, bias_rows)

    shares_done((s.gl1, s.gl1r), 8)
    s.gl2[...] = head_sum((s.gl1, s.gl1r)).reshape(B, z.rl // B, 128)
    spread(lambda peer: s.gl2.at[peer], s.gl2r.at[me_b], 5)
    for h, row in enumerate(finish_sum(5, L)):
        s.brow[h] = row
    spread_done(s.gl2, s.gl2r, 5)
    s.gl3[me_b] = batch_sum(s.gl2[me_b], s.gl2r)
    spread(lambda peer: s.gl3.at[me_b], s.gl3.at[me_b], 6)

    small_o[...] = jnp.zeros(small_o.shape, f32)
    small_o[0:1, :] = sum_gain_1
    small_o[1:2, :] = sum_shift_1
    small_o[2:3, :] = sum_gain_3
    small_o[3:4, :] = sum_shift_3
    small_o[4:5, 0:FH] = s.srow[0:1, own]
    small_o[5:6, 0:FH] = s.srow[1:2, own]
    small_o[6:7, :] = s.brow[me_h]

    spread_done(s.ge3, s.ge3, 4)
    early_o[...] = s.ge3[...].reshape(z.re, 128)
    spread_done(s.gl3, s.gl3, 6)
    late_o[...] = s.gl3[...].reshape(z.rl, 128)

    done(to_head(s.osend.at[some], out_o.at[pl.ds(0, n * (H - 1))], 5, 1))
    done(to_head(s.tsend.at[some], tg_o.at[pl.ds(0, n * (H - 1))], 6, 1))
    c_out.wait()
    pltpu.make_async_copy(s.tsend.at[me_h], tg_o.at[pl.ds(me_h * n, n)], s.loc.at[7]).wait()


def finish_kernel(z, out_i, tg_i, early, late, small, out, tg, qkv, bias, proj, g1, s1, up, g2, s2, down, g3, s3):
    at = lax.broadcasted_iota(jnp.int32, (128, 128), 0)
    to = lax.broadcasted_iota(jnp.int32, (128, 128), 1)
    turn = jnp.where(lax.bitwise_and(at, 7) * 16 + lax.shift_right_logical(at, 3) == to, 1.0, 0.0).astype(bf16)
    for src, dst in ((out_i, out), (tg_i, tg)):
        rows = z.share // 16 * 16
        for k in range(0, rows, 16):
            dst[k : k + 16] = nn(turn, src[:, k : k + 16, :].reshape(128, z.D)).reshape(16, 8, z.D)
        for k in range(rows, z.share):
            dst[k] = src[:, k, :].astype(f32)

    @pl.when(pl.program_id(0) == 0)
    def _():
        D, C, PH = z.D, z.C, z.D // z.H
        up[...] = early[0:D, :]
        down[...] = early[D : 2 * D, :].T
        for half in range(D // 128):
            lanes = slice(half * 128, (half + 1) * 128)
            proj[:, lanes] = early[2 * D + half * PH : 2 * D + (half + 1) * PH, :]
            qkv[0, :, lanes] = late[half * C : (half + 1) * C, :]
        g1[...] = small[0:1, :]
        s1[...] = small[1:2, :]
        g3[...] = small[2:3, :]
        s3[...] = small[3:4, :]
        g2[...] = small[4:5, 0 : z.F // z.H]
        s2[...] = small[5:6, 0 : z.F // z.H]
        bias[...] = small[6:7, 0 : z.length]


def on_device(H, B, tokens, image_count, token_place, qkv_weight, bias_table, proj_weight, attention_gain,
              attention_shift, up_weight, hidden_gain, hidden_shift, down_weight, output_gain, output_shift,
              cotangent):
    images, length, width = tokens.shape
    z = types.SimpleNamespace(
        n=images // H, T=round_up(length, 16), L=round_up(length, 128), D=width, F=up_weight.shape[1] * H,
        H=H, B=B, C=qkv_weight.shape[1], share=cotangent.shape[1], length=length)
    z.re = round_up(2 * z.D + z.D // H * (z.D // 128), 8 * max(B, 2))
    z.rl = round_up(z.C * (z.D // 128), 8 * max(B, 2))
    z.group = max(g for g in (1, 2, 3, 4) if z.n % g == 0)
    z.group_back = max(g for g in (1, 2, 3) if z.n % g == 0)
    z.direct = H == 4 and B <= 8
    z.sums = {}
    for k, r in enumerate((2 * z.D, 2 * z.F, 4 * z.D, 2 * z.F, 2 * z.D, H * z.L)):
        z.sums["sum%d" % k] = pltpu.VMEM((H * B if z.direct else H, r // 128, 128), f32)
        if not z.direct:
            z.sums["part%d" % (k % 2)] = pltpu.VMEM((B, 8, 128), f32)

    def bufs(s, k):
        first = getattr(s, "sum%d" % k)
        return first, None if z.direct else getattr(s, "part%d" % (k % 2)).at[:, 0 : first.shape[1]]

    z.bufs = bufs
    scratch = layout(z)
    hbm = pl.BlockSpec(memory_space=pl.ANY)
    vmem = pl.BlockSpec(memory_space=pltpu.VMEM)
    smem = pl.BlockSpec(memory_space=pltpu.SMEM)
    outs = pl.pallas_call(
        functools.partial(block_kernel, z, tuple(scratch)),
        out_shape=(
            jax.ShapeDtypeStruct((images, z.share, width), bf16),
            jax.ShapeDtypeStruct((images, z.share, width), bf16),
            jax.ShapeDtypeStruct((z.re, 128), f32),
            jax.ShapeDtypeStruct((z.rl, 128), f32),
            jax.ShapeDtypeStruct((8, width), f32),
        ),
        in_specs=[hbm, smem, vmem, hbm, vmem, hbm, vmem, vmem, hbm, vmem, vmem, hbm, vmem, vmem, hbm],
        out_specs=(hbm, hbm, vmem, vmem, vmem),
        scratch_shapes=list(scratch.values()),
        compiler_params=pltpu.CompilerParams(
            collective_id=0, has_side_effects=True, vmem_limit_bytes=127 * 512 * 1024
        ),
    )(
        tokens.transpose(1, 0, 2), image_count, token_place.reshape(1, -1), qkv_weight, bias_table, proj_weight,
        attention_gain.reshape(1, -1), attention_shift.reshape(1, -1), up_weight, hidden_gain.reshape(1, -1),
        hidden_shift.reshape(1, -1), down_weight, output_gain.reshape(1, -1), output_shift.reshape(1, -1),
        cotangent.transpose(1, 0, 2),
    )

    steps = images // 8
    block = pl.BlockSpec((8, z.share, width), lambda i: (i, 0, 0))
    turned = pl.BlockSpec((z.share, 8, width), lambda i: (0, i, 0))

    def whole(*shape):
        return jax.ShapeDtypeStruct(shape, f32), pl.BlockSpec(shape, lambda i: (0,) * len(shape))

    fh = z.F // H
    small = [
        whole(1, z.C, width), whole(1, length), whole(width // H, width), whole(1, width), whole(1, width),
        whole(width, fh), whole(1, fh), whole(1, fh), whole(fh, width), whole(1, width), whole(1, width)]
    big = jax.ShapeDtypeStruct((z.share, images, width), f32)
    res = pl.pallas_call(
        functools.partial(finish_kernel, z),
        grid=(steps,),
        out_shape=[big, big] + [a for a, _ in small],
        in_specs=[block, block, whole(z.re, 128)[1], whole(z.rl, 128)[1], whole(8, width)[1]],
        out_specs=[turned, turned] + [b for _, b in small],
    )(*outs)
    res = [res[0].transpose(1, 0, 2), res[1].transpose(1, 0, 2), *res[2:]]
    for k in (5, 6, 8, 9, 11, 12):
        res[k] = res[k].reshape(-1)
    return tuple(res)


def solution(mesh):
    H, B = mesh.shape["head"], mesh.shape["batch"]
    placed = (
        P("batch", None, None),
        P("batch"),
        P(),
        P("head", None, None),
        P("head", None),
        P(),
        P(),
        P(),
        P(None, "head"),
        P("head"),
        P("head"),
        P("head", None),
        P(),
        P(),
        P("batch", "head", None),
    )
    return jax.shard_map(
        functools.partial(on_device, H, B),
        mesh=mesh,
        in_specs=placed,
        out_specs=(
            P("batch", "head", None),
            P("batch", "head", None),
            P("head", None, None),
            P("head", None),
            P("head", None),
            P(),
            P(),
            P(None, "head"),
            P("head"),
            P("head"),
            P("head", None),
            P(),
            P(),
        ),
        check_vma=False,
    )
```

```python
import functools
import types

import jax
import jax.numpy as jnp
from jax import lax
from jax.experimental import pallas as pl
from jax.experimental.pallas import tpu as pltpu
from jax.sharding import PartitionSpec as P

KEY = 32
VAL = 64
SIDE = 14
EPSILON = 1e-05
LOG2E = 1.4426950408889634
MESH = pl.DeviceIdType.MESH
f32 = jnp.float32
bf16 = jnp.bfloat16


def nn(left, right):
    return lax.dot_general(left, right, (((1,), (0,)), ((), ())), preferred_element_type=f32)


def nt(left, right):
    return lax.dot_general(left, right, (((1,), (1,)), ((), ())), preferred_element_type=f32)


def tn(left, right):
    return lax.dot_general(left, right, (((0,), (0,)), ((), ())), preferred_element_type=f32)


def among(block, at, total_rows):
    parts = []
    if at > 0:
        parts.append(jnp.zeros((at, block.shape[1]), block.dtype))
    parts.append(block)
    if at + block.shape[0] < total_rows:
        parts.append(jnp.zeros((total_rows - at - block.shape[0], block.shape[1]), block.dtype))
    return jnp.concatenate(parts, axis=0)


def spaced(value, heads):
    rows, columns = value.shape
    each = columns // heads
    lane = lax.broadcasted_iota(jnp.int32, (rows, columns), 1)
    return jnp.concatenate(
        [jnp.where((lane >= h * each) & (lane < (h + 1) * each), value, jnp.zeros_like(value)) for h in range(heads)],
        axis=0)


def round_up(value, step):
    return -(-value // step) * step


def sigmoid(value):
    return 0.5 * jnp.tanh(0.5 * value) + 0.5


def fold(value):
    rows, columns = value.shape
    return jnp.sum(value.reshape(rows // 8, 8, columns), axis=0)


def total(value):
    return jnp.sum(value, axis=0, keepdims=True)


def lookup(table, index):
    rows = index.shape[0]
    low = jnp.broadcast_to(table[:, 0:128], (rows, 128))
    high = jnp.broadcast_to(table[:, 128:256], (rows, 128))
    return take(low, high, index)


def take(low, high, index):
    parts = []
    for half in range(2):
        at = index[:, half * 128 : (half + 1) * 128]
        inside = lax.bitwise_and(at, 127)
        first = jnp.take_along_axis(low, inside, axis=1, mode="promise_in_bounds")
        second = jnp.take_along_axis(high, inside, axis=1, mode="promise_in_bounds")
        parts.append(jnp.where(at < 128, first, second))
    return jnp.concatenate(parts, axis=1)


def layout(z):
    n, T, L, D, F, H, B, C = z.n, z.T, z.L, z.D, z.F, z.H, z.B, z.C
    dma = pltpu.SemaphoreType.DMA
    vmem = pltpu.VMEM
    return {
        "xt": vmem((T, 16, D), bf16),
        "ct": vmem((T, 16, D), bf16),
        "cin": vmem((round_up(z.share, 4), H * n, D), bf16),
        "mix": vmem((n * 16, 256), bf16),
        "unmix": vmem((n * 16, n * 16), bf16),
        "deal": vmem((H * n * 4, H * n * 4), bf16),
        "qkvg": vmem((H, C, D), bf16),
        "downg": vmem((H, F // H, D), bf16),
        "smallg": vmem((H, 4, 128), f32),
        "w2": vmem((H * C, D), bf16),
        "upcat": vmem((D, F), bf16),
        "projw": vmem((D, D), bf16),
        "bias": vmem((H, T, L), f32),
        "dbias": vmem((H, T, L), f32),
        "rowmask": vmem((T, D), f32),
        "onehot": vmem((L, L), bf16),
        "xpad": vmem((n, L, D), bf16),
        "qt": vmem((n, H * KEY, L), bf16),
        "knat": vmem((n, T, H * KEY), bf16),
        "vnat": vmem((n, T, H * VAL), bf16),
        "tmp": vmem((z.group, T, D), f32),
        "p": vmem((n, H, T, L), bf16),
        "linv": vmem((n, H, 1, L), f32),
        "att": vmem((n, H * VAL, L), f32),
        "act": vmem((n, H * VAL, L), bf16),
        "proj": vmem((n, T, D), f32),
        "hid": vmem((n, T, F), f32),
        "slope": vmem((n, T, F), f32),
        "act2": vmem((n, T, F), bf16),
        "out": vmem((n, T, D), f32),
        "u": vmem((n, T, D), f32),
        "gproj": vmem((n, L, D), bf16),
        "osend": vmem((H, n, z.share, D), bf16),
        "tsend": vmem((H, n, z.share, D), bf16),
        "gdown": vmem((D, F), f32),
        "gup": vmem((D, F), f32),
        "gpr": vmem((D, D), f32),
        "gqkv": vmem((H * C, D), f32),
        "srow": vmem((2, F), f32),
        "brow": vmem((H, 1, L), f32),
        **z.sums,
        "cnt": vmem((B, 1, 128), f32),
        "ge1": vmem((H, z.re, 128), bf16),
        "ge1r": vmem((H, z.re, 128), bf16),
        "ge2": vmem((B, z.re // B, 128), f32),
        "ge2r": vmem((B, z.re // B, 128), f32),
        "ge3": vmem((B, z.re // B, 128), f32),
        "gl1": vmem((H, z.rl, 128), bf16),
        "gl1r": vmem((H, z.rl, 128), bf16),
        "gl2": vmem((B, z.rl // B, 128), f32),
        "gl2r": vmem((B, z.rl // B, 128), f32),
        "gl3": vmem((B, z.rl // B, 128), f32),
        "loc": dma((8,)),
        "hs": dma((9,)),
        "hr": dma((9,)),
        "ass": dma((12,)),
        "asr": dma((12,)),
        "bs": dma((7,)),
        "br": dma((7,)),
        "ready": pltpu.SemaphoreType.REGULAR,
    }


def block_kernel(z, names, *refs):
    (tokens, count, place, qkv_w, table, proj_w, gain_1, shift_1, up_w, gain_2, shift_2, down_w,
     gain_3, shift_3, cot, out_o, tg_o, early_o, late_o, small_o) = refs[:20]
    s = types.SimpleNamespace(**dict(zip(names, refs[20:], strict=True)))
    n, T, L, D, F, H, B, C = z.n, z.T, z.L, z.D, z.F, z.H, z.B, z.C
    share, length = z.share, z.length
    me_h = lax.axis_index("head")
    me_b = lax.axis_index("batch")

    def local(src, dst, k):
        copy = pltpu.make_async_copy(src, dst, s.loc.at[k])
        copy.start()
        return copy

    def to_head(src, dst, k, j):
        return pltpu.make_async_remote_copy(
            src_ref=src, dst_ref=dst, send_sem=s.hs.at[k], recv_sem=s.hr.at[k],
            device_id={"head": head_peers[j]}, device_id_type=MESH)

    def to_batch(src, dst, k, peer):
        return pltpu.make_async_remote_copy(
            src_ref=src, dst_ref=dst, send_sem=s.bs.at[k], recv_sem=s.br.at[k],
            device_id={"batch": peer}, device_id_type=MESH)

    head_peers = [lax.rem(me_h + j, H) for j in range(H)]
    core = lax.rem(me_b, 2)
    sibling = me_b + 1 - 2 * core

    def done(copies):
        copies.wait()

    def around(size, step):
        if size <= 8:
            for j in range(1, size):
                step(j)
        else:
            lax.fori_loop(1, size, lambda j, c: (step(j), c)[1], 0)

    FH = F // H
    PH = D // H
    own = pl.ds(pl.multiple_of(me_h * FH, FH), FH)
    qkv_32, up_32, down_32 = s.gqkv.at[0:C], s.gup.at[:, 0:FH], s.gdown.at[0:FH, 0:D]
    c_qkv = local(qkv_w.at[0], qkv_32, 0)
    c_up = local(up_w, up_32, 1)
    c_down = local(down_w, down_32, 2)
    def window(slot):
        return pl.multiple_of(slot * n // 8 * 8, 8)

    c_tok = local(tokens.at[:, pl.ds(window(me_h), 16)], s.xt.at[pl.ds(0, length)], 3)
    c_proj = local(proj_w, s.gpr, 4)
    c_cot = local(cot, s.cin.at[pl.ds(0, share)], 6)

    def everyone():
        pairs = [(a, b) for a in range(H) for b in range(B) if a or b]
        return sorted(pairs, key=lambda p: -(p[0] % 2 + p[0] // 2 + (2 if p[1] > 1 else p[1] / 4)))

    def at_offset(a, b):
        x, y = lax.rem(me_h, 2), lax.div(me_h, 2)
        other = (y + a // 2 - 2 * y * (a // 2)) * 2 + x + a % 2 - 2 * x * (a % 2)
        return {"head": other, "batch": lax.rem(me_b + b, B)}

    barrier = pltpu.get_barrier_semaphore()
    for j in range(1, H):
        pl.semaphore_signal(barrier, inc=1, device_id={"head": head_peers[j]}, device_id_type=MESH)

    def greet(semaphore):
        around(B, lambda j: pl.semaphore_signal(
            semaphore, inc=1, device_id={"batch": lax.rem(me_b + j, B)}, device_id_type=MESH))

    greet(barrier)
    targets = [at_offset(*pair) for pair in everyone()] if z.direct else []

    s.smallg[me_h] = jnp.concatenate(
        [gain_2[...], shift_2[...], table[:, 0:128], jnp.concatenate(
            [table[:, 128:length], jnp.zeros((1, 256 - length), f32)], axis=1)], axis=0)
    c_qkv.wait()
    s.qkvg[me_h] = qkv_32[...].astype(bf16)
    up_rows = pl.ds(pl.multiple_of(core * (D // 2), D // 2), D // 2)
    down_rows = pl.ds(pl.multiple_of(core * (FH // 2), FH // 2), FH // 2)
    c_up.wait()
    s.upcat[up_rows, own] = s.gup[up_rows, 0:FH].astype(bf16)
    c_down.wait()
    s.downg[me_h, down_rows] = s.gdown[down_rows, 0:D].astype(bf16)

    row_at = lax.broadcasted_iota(jnp.int32, (L, L), 0)
    lane_at = lax.broadcasted_iota(jnp.int32, (L, L), 1)
    s.rowmask[...] = jnp.where(row_at < length, 1.0, 0.0)[0:T]
    place_lane = jnp.broadcast_to(
        jnp.concatenate([place[...].astype(f32), jnp.zeros((1, L - length), f32)], axis=1), (L, L))
    place_row = place_lane.T
    s.onehot[...] = jnp.where((place_row == lane_at.astype(f32)) & (row_at < length), 1.0, 0.0).astype(bf16)

    def grid_of(at):
        at = at.astype(jnp.int32)
        row = lax.shift_right_logical(at * 4682, 16)
        return row, at - row * SIDE

    rows_t, cols_t = grid_of(place_lane[0:T])
    rows_s, cols_s = grid_of(place_row[0:T])
    offsets = jnp.abs(rows_s - rows_t) * SIDE + jnp.abs(cols_s - cols_t)
    for h in range(H):
        s.dbias[h] = jnp.zeros((T, L), f32)
    s.gdown[...] = jnp.zeros(s.gdown.shape, f32)
    s.gup[...] = jnp.zeros(s.gup.shape, f32)
    s.gqkv[...] = jnp.zeros(s.gqkv.shape, f32)

    def valid_of(i):
        return jnp.where(me_h * n + i < count[0], 1.0, 0.0)

    c_proj.wait()
    s.projw[...] = s.gpr[...].astype(bf16)
    s.gpr[...] = jnp.zeros(s.gpr.shape, f32)
    line_at = lax.broadcasted_iota(jnp.int32, (n * 16, 256), 0)
    pick_at = lax.broadcasted_iota(jnp.int32, (n * 16, 256), 1)
    image_at = lax.shift_right_logical(line_at, 4)
    s.mix[...] = jnp.where(
        (lax.bitwise_and(line_at, 15) == lax.shift_right_logical(pick_at, 4))
        & (lax.bitwise_and(pick_at, 15) == image_at + (me_h * n - window(me_h)))
        & (image_at + me_h * n < count[0]),
        1.0, 0.0).astype(bf16)
    s.xt[length:T] = jnp.zeros((T - length, 16, D), bf16)
    s.u[:, T - 16 : T, :] = jnp.zeros((n, 16, D), f32)
    s.xpad[:, T:L, :] = jnp.zeros((n, L - T, D), bf16)
    s.gproj[:, T:L, :] = jnp.zeros((n, L - T, D), bf16)
    c_tok.wait()

    def enter_tokens(k, carry):
        at = pl.ds(pl.multiple_of(k * 16, 16), 16)
        s.xpad[:, at, :] = nn(s.mix[...], s.xt[at].reshape(256, D)).astype(bf16).reshape(n, 16, D)
        return carry

    lax.fori_loop(0, T // 16, enter_tokens, 0)


    blocks = -(-share * n // 16)
    step = n * 4 // 16

    def over(value, divisor):
        return lax.shift_right_logical(value * (65536 // divisor + 1), 16)

    def square(size):
        return (lax.broadcasted_iota(jnp.int32, (size, size), 0),
                lax.broadcasted_iota(jnp.int32, (size, size), 1))

    to, at = square(n * 16)
    image_to = lax.shift_right_logical(to, 4)
    s.unmix[...] = jnp.where(
        (at == lax.bitwise_and(to, 15) * n + image_to) & (image_to + me_h * n < count[0]), 1.0, 0.0).astype(bf16)
    to, at = square(H * n * 4)
    owner = over(to, n * 4)
    inside = to - owner * (n * 4)
    token_to = over(inside, n)
    s.deal[...] = jnp.where(
        at == token_to * (H * n) + owner * n + inside - token_to * n, 1.0, 0.0).astype(bf16)
    s.cin[share:] = jnp.zeros((s.cin.shape[0] - share, H * n, D), bf16)
    c_cot.wait()

    def deal(k, wide):
        dealt = nn(s.deal[...], s.cin[pl.ds(k * 4, 4)].reshape(H * n * 4, D)).astype(bf16)
        for h in range(H):
            piece = dealt[h * n * 4 : h * n * 4 + wide * 16].reshape(wide, 16, D)
            s.xt[pl.ds(h * blocks + k * step, wide)] = piece

    lax.fori_loop(0, share // 4, lambda k, c: (deal(k, step), c)[1], 0)
    if share % 4:
        deal(share // 4, blocks - share // 4 * step)
    own_blocks = pl.ds(me_h * blocks, blocks)
    c_own = local(s.xt.at[own_blocks], s.ct.at[own_blocks], 5)

    def enter_cotangent(q):
        first = q * blocks
        for k in range(share // 16):
            rows = s.ct[first + k * n : first + (k + 1) * n].reshape(n * 16, D)
            at = q * share + k * 16
            s.u[:, at : at + 16, :] = nn(s.unmix[...], rows).reshape(n, 16, D)
        rest = s.ct[first + share // 16 * n].astype(f32)
        for i in range(n):
            at = q * share + share // 16 * 16
            s.u[i, at : at + 1, :] = rest[i : i + 1] * valid_of(i)

    s.cnt[me_b] = jnp.full((1, 128), count[0]).astype(f32)
    pl.semaphore_wait(barrier, H - 1 + B - 1)

    shared = (s.qkvg.at[me_h], s.smallg.at[me_h], s.upcat.at[up_rows, own], s.downg.at[me_h, down_rows])
    for k in (1, 0, 2, 3):
        for j in range(1, H):
            to_head(shared[k], shared[k], k, j).start()
    greet(s.ready)

    cuts = (0, blocks * 6 // 10, blocks)

    def send_cotangent(piece):
        low, high = cuts[piece], cuts[piece + 1]
        for j in range(1, H):
            to_head(s.xt.at[pl.ds(head_peers[j] * blocks + low, high - low)],
                    s.ct.at[pl.ds(me_h * blocks + low, high - low)], 4, j).start()

    around(B, lambda j: to_batch(s.cnt.at[me_b], s.cnt.at[me_b], 0, lax.rem(me_b + j, B)).start())
    send_cotangent(0)

    some = pl.ds(0, H - 1)
    done(to_head(s.smallg.at[some], s.smallg.at[some], 1, 1))
    for h in range(H):
        line = jnp.concatenate([s.smallg[h, 2:3, :], s.smallg[h, 3:4, :]], axis=1)
        s.bias[h] = jnp.where(row_at[0:T] < length, lookup(line, offsets) * LOG2E, -1e30)
    done(to_head(s.qkvg.at[some], s.qkvg.at[some], 0, 1))
    for h in range(H):
        s.w2[h * KEY : (h + 1) * KEY] = s.qkvg[h, 0:KEY]
        s.w2[(H + h) * KEY : (H + h + 1) * KEY] = s.qkvg[h, KEY : 2 * KEY]
        at = 2 * H * KEY + h * VAL
        s.w2[at : at + VAL] = s.qkvg[h, 2 * KEY : C]

    scale = KEY**-0.5
    KH, VH = H * KEY, H * VAL

    def attend(i, carry):
        first, second = carry
        at = [i * z.group + u for u in range(z.group)]
        mixed, scores = [], []
        for j in at:
            x = s.xpad[j]
            mixed.append(nt(s.w2[...], x).astype(bf16))
            s.qt[j] = mixed[-1][0:KH]
            natural = nt(x[0:T], s.w2[KH : H * C]).astype(bf16)
            s.knat[j] = natural[:, 0:KH]
            s.vnat[j] = natural[:, KH:]
            scores.append(natural[:, 0:KH])
        for u in range(z.group):
            scores[u] = nn(spaced(scores[u], H), mixed[u][0:KH])
        for h in range(H):
            for u, j in enumerate(at):
                logits = scores[u][h * T : (h + 1) * T] * (scale * LOG2E) + s.bias[h]
                raised = jnp.exp2(logits - jnp.max(logits, axis=0, keepdims=True))
                inverse = 1.0 / total(raised)
                s.linv[j, h] = inverse
                low = raised.astype(bf16)
                s.p[j, h] = low
                values = mixed[u][2 * KH + h * VAL : 2 * KH + (h + 1) * VAL, 0:T]
                attended = nn(values, low) * inverse
                s.att[j, h * VAL : (h + 1) * VAL] = attended
                s.act[j, h * VAL : (h + 1) * VAL] = (attended * sigmoid(attended)).astype(bf16)
        for j in at:
            projected = tn(s.act[j], s.projw[...])[0:T] * s.rowmask[...]
            s.proj[j] = projected
            first, second = first + fold(projected), second + fold(projected * projected)
        return first, second

    def zeros(width):
        return jnp.zeros((8, width), f32)

    def port(k, src, dst, device):
        return pltpu.make_async_remote_copy(
            src_ref=src, dst_ref=dst, send_sem=s.ass.at[k], recv_sem=s.asr.at[k],
            device_id=device, device_id_type=MESH)

    def sum_slots(buf, size):
        if size <= 32:
            whole = buf[0]
            for b in range(1, size):
                whole = whole + buf[b]
            return whole
        return lax.fori_loop(1, size, lambda b, c: c + buf[b], buf[0])

    def start_sum(k, rows):
        buf = z.bufs(s, k)[0]
        me = me_h * B + me_b if z.direct else me_h
        r = 0
        for row in rows:
            for c in range(row.shape[1] // 128):
                buf[me, r : r + 1, :] = row[:, c * 128 : (c + 1) * 128]
                r += 1
        for target in targets if z.direct else [{"head": p} for p in head_peers[1:]]:
            port(k, buf.at[me], buf.at[me], target).start()

    def finish_sum(k, width):
        others = z.bufs(s, k)[0].at[pl.ds(0, H * B - 1 if z.direct else H - 1)]
        done(port(k, others, others, {"head": head_peers[1]}))
        bufs = z.bufs(s, k)
        if z.direct:
            whole = sum_slots(bufs[0], H * B)
        else:
            bufs[1][me_b] = sum_slots(bufs[0], H)
            mine = bufs[1].at[me_b]
            around(B, lambda j: port(k + 6, mine, mine, {"batch": lax.rem(me_b + j, B)}).start())
            others = bufs[1].at[pl.ds(0, B - 1)]
            done(port(k + 6, others, others, {"batch": lax.rem(me_b + 1, B)}))
            whole = sum_slots(bufs[1], B)
        step = width // 128
        return [
            jnp.concatenate([whole[r + c : r + c + 1] for c in range(step)], axis=1)
            for r in range(0, whole.shape[0], step)
        ]

    first, second = lax.fori_loop(0, n // z.group, attend, (zeros(D), zeros(D)))
    pl.semaphore_wait(s.ready, B - 1)
    some_rows = pl.ds(0, D // 2)
    done(to_head(s.upcat.at[some_rows, pl.ds(0, FH * (H - 1))], s.upcat.at[some_rows, pl.ds(0, FH * (H - 1))], 2, 1))
    down_some = s.downg.at[some, pl.ds(0, FH // 2)]
    done(to_head(down_some, down_some, 3, 1))
    halves = (s.upcat.at[up_rows, :], s.downg.at[:, down_rows])
    for k in range(2):
        to_batch(halves[k], halves[k], k + 1, sibling).start()
    start_sum(0, [total(first), total(second)])
    send_cotangent(1)
    for k in range(2):
        to_batch(halves[k], halves[k], k + 1, sibling).wait()
    down = s.downg[...].reshape(F, D)
    gain_2w = jnp.concatenate([s.smallg[h, 0:1, :] for h in range(H)], axis=1)
    shift_2w = jnp.concatenate([s.smallg[h, 1:2, :] for h in range(H)], axis=1)
    others = s.cnt.at[pl.ds(0, B - 1)]
    done(to_batch(others, others, 0, sibling))
    seen_part = sum_slots(s.cnt, B) * float(length)
    seen_row = jnp.concatenate([seen_part] * (D // 128), axis=1)
    sums = finish_sum(0, D)
    seen_wide = jnp.concatenate([seen_row] * (F // D), axis=1)

    def moments(first, second, seen):
        mean = first / seen
        return mean, lax.rsqrt(second / seen - mean * mean + EPSILON)

    mean_1, inverse_1 = moments(sums[0], sums[1], seen_row)
    a_1 = gain_1[...] * inverse_1
    b_1 = shift_1[...] - mean_1 * a_1

    G = z.group
    GT = G * T

    def group(ref, i):
        return ref[pl.ds(i * G, G), 0:T].reshape(GT, ref.shape[2])

    def put(ref, i, value):
        ref[pl.ds(i * G, G), 0:T] = value.reshape(G, T, value.shape[1])

    def mask_of(i):
        return jnp.concatenate([s.rowmask[...] * valid_of(i * G + u) for u in range(G)], axis=0)

    def residual_of(i):
        return group(s.xpad, i).astype(f32) + (group(s.proj, i) * a_1 + b_1 * mask_of(i))

    def enter(i, carry):
        first, second = carry
        residual = residual_of(i).astype(bf16)
        hidden = nn(residual, s.upcat[...])
        put(s.hid, i, hidden)
        return first + fold(hidden), second + fold(hidden * hidden)

    first, second = lax.fori_loop(0, n // G, enter, (zeros(F), zeros(F)))
    start_sum(1, [total(first), total(second)])
    others = s.ct.at[pl.ds(0, blocks * (H - 1))]
    done(to_head(others, others, 4, 1))
    c_own.wait()
    for q in range(H):
        enter_cotangent(q)
    sums = finish_sum(1, F)
    mean_2, inverse_2 = moments(sums[0], sums[1], seen_wide)
    a_2 = gain_2w * inverse_2
    b_2 = shift_2w - mean_2 * a_2

    def leave(i, carry):
        one, two, three, four = carry
        shaped = group(s.hid, i) * a_2 + b_2
        gate = sigmoid(shaped)
        active = shaped * gate
        put(s.slope, i, gate + active * (1.0 - gate))
        low = active.astype(bf16)
        put(s.act2, i, low)
        outgoing = nn(low, down)
        put(s.out, i, outgoing)
        upstream = group(s.u, i)
        masked = outgoing * mask_of(i)
        return (one + fold(masked), two + fold(masked * outgoing), three + fold(upstream),
                four + fold(upstream * outgoing))

    sums = lax.fori_loop(0, n // G, leave, (zeros(D), zeros(D), zeros(D), zeros(D)))
    start_sum(2, [total(v) for v in sums])
    sums = finish_sum(2, D)
    mean_3, inverse_3 = moments(sums[0], sums[1], seen_row)
    a_3 = gain_3[...] * inverse_3
    b_3 = shift_3[...] - mean_3 * a_3
    sum_shift_3 = sums[2]
    sum_gain_3 = inverse_3 * (sums[3] - mean_3 * sum_shift_3)

    def back(gain, mean, inverse, sum_shift, sum_gain, seen):
        scaled = gain * inverse
        slope = -scaled * inverse * (sum_gain / seen)
        return scaled, slope, -scaled * (sum_shift / seen) - slope * mean

    s_3, v_3, r_3 = back(gain_3[...], mean_3, inverse_3, sum_shift_3, sum_gain_3, seen_row)

    def back_leave(i, carry):
        one, two = carry
        grad = (group(s.u, i) * s_3 + (group(s.out, i) * v_3 + r_3) * mask_of(i)).astype(bf16)
        put(s.gproj, i, grad)
        shaped = nt(grad, down) * group(s.slope, i)
        put(s.slope, i, shaped)
        return one + fold(shaped), two + fold(shaped * group(s.hid, i))

    def down_gradient(i, carry):
        s.gdown[...] += tn(group(s.gproj, i), group(s.act2, i))
        return carry

    def output(i):
        s.tmp[...] = ((residual_of(i) + (group(s.out, i) * a_3 + b_3)) * mask_of(i)).reshape(G, T, D)
        for u in range(G):
            for q in range(H):
                s.osend[q, i * G + u] = s.tmp[u, q * share : (q + 1) * share, :].astype(bf16)

    def early(at, parts):
        for h, part in enumerate(parts):
            s.ge1[h, at : at + part.shape[0], :] = part.astype(bf16)

    def send_early(low, high):
        rows = pl.ds(low, high - low)
        for j in range(1, H):
            to_head(s.ge1.at[head_peers[j], rows], s.ge1r.at[me_h, rows], 7, j).start()

    def send_output(i):
        to = out_o.at[pl.ds(me_h * n + i * G, G)]
        for j in range(1, H):
            to_head(s.osend.at[head_peers[j], pl.ds(i * G, G)], to, 5, j).start()

    first, second = lax.fori_loop(0, n // G, back_leave, (zeros(F), zeros(F)))
    start_sum(3, [total(first), total(second)])
    output(0)
    send_output(0)
    lax.fori_loop(0, n // G, down_gradient, 0)
    early(0, [s.gdown[:, h * FH : (h + 1) * FH] for h in range(H)])
    sums = finish_sum(3, F)

    sum_shift_2 = sums[0]
    sum_gain_2 = inverse_2 * (sums[1] - mean_2 * sum_shift_2)
    s_2, v_2, r_2 = back(gain_2w, mean_2, inverse_2, sum_shift_2, sum_gain_2, seen_wide)
    s.srow[0:1, :] = sum_gain_2
    s.srow[1:2, :] = sum_shift_2

    def back_enter(i, carry):
        one, two = carry
        mask = jnp.concatenate([mask_of(i)] * (F // D), axis=1)
        grad = (group(s.slope, i) * s_2 + group(s.hid, i) * v_2 + r_2 * mask).astype(bf16)
        put(s.act2, i, grad)
        upstream = group(s.u, i) + nt(grad, s.upcat[...])
        put(s.u, i, upstream)
        return one + fold(upstream), two + fold(upstream * group(s.proj, i))

    first, second = lax.fori_loop(0, n // G, back_enter, (zeros(D), zeros(D)))
    start_sum(4, [total(first), total(second)])
    send_early(0, D)

    def up_gradient(i, carry):
        s.gup[...] += tn(residual_of(i).astype(bf16), group(s.act2, i))
        return carry

    lax.fori_loop(0, n // G, up_gradient, 0)
    early(D, [s.gup[:, h * FH : (h + 1) * FH] for h in range(H)])
    send_early(D, 2 * D)
    for i in range(1, n // G):
        output(i)
    sums = finish_sum(4, D)
    c_out = local(s.osend.at[me_h], out_o.at[pl.ds(me_h * n, n)], 6)
    sum_shift_1 = sums[0]
    sum_gain_1 = inverse_1 * (sums[1] - mean_1 * sum_shift_1)
    s_1, v_1, r_1 = back(gain_1[...], mean_1, inverse_1, sum_shift_1, sum_gain_1, seen_row)

    def back_project(i, carry):
        grad = (group(s.u, i) * s_1 + group(s.proj, i) * v_1 + r_1 * mask_of(i)).astype(bf16)
        put(s.gproj, i, grad)
        whole = s.gpr[...]
        for u in range(G):
            whole = whole + nn(s.act[i * G + u], s.gproj[i * G + u])
        s.gpr[...] = whole
        return carry

    lax.fori_loop(0, n // G, back_project, 0)

    def shares(buffer, k):
        for j in range(1, H):
            to_head(buffer[0].at[head_peers[j]], buffer[1].at[me_h], k, j).start()

    def shares_done(buffer, k):
        done(to_head(buffer[0].at[some], buffer[1].at[some], k, 1))

    def head_sum(buffer):
        whole = buffer[0][me_h].astype(f32)
        for j in range(1, H):
            whole = whole + buffer[1][head_peers[j]].astype(f32)
        return whole

    def spread(src, dst, k):
        around(B, lambda j: to_batch(src(lax.rem(me_b + j, B)), dst, k, lax.rem(me_b + j, B)).start())

    def spread_done(src, dst, k):
        others = pl.ds(0, B - 1)
        done(to_batch(src.at[others], dst.at[others], k, sibling))

    def batch_sum(own, received):
        if B <= 8:
            whole = own
            for j in range(1, B):
                whole = whole + received[lax.rem(me_b + j, B)]
            return whole
        return lax.fori_loop(1, B, lambda j, c: c + received[lax.rem(me_b + j, B)], own)

    for half in range(D // 128):
        lanes = slice(half * 128, (half + 1) * 128)
        early(2 * D + half * PH, [s.gpr[h * PH : (h + 1) * PH, lanes] for h in range(H)])
    filled = 2 * D + D // 128 * PH
    if z.re > filled:
        s.ge1[:, filled:, :] = jnp.zeros((H, z.re - filled, 128), bf16)
    send_early(2 * D, z.re)
    for i in range(1, n // G):
        send_output(i)

    GB = z.group_back

    def back_attend(i, carry):
        at = [i * GB + u for u in range(GB)]
        lows, deltas, products = [], [], []
        for j in at:
            att = s.att[j]
            gate = sigmoid(att)
            active = att * gate
            gact = nt(s.projw[...], s.gproj[j]) * (gate + active * (1.0 - gate))
            low, delta = [], []
            for h in range(H):
                rows = slice(h * VAL, (h + 1) * VAL)
                grad = gact[rows] * s.linv[j, h]
                low.append(grad.astype(bf16))
                delta.append(total(grad * att[rows]))
            lows.append(low)
            deltas.append(delta)
            products.append(nn(spaced(s.vnat[j], H), jnp.concatenate(low, axis=0)))
        grads = [[] for _ in at]
        for h in range(H):
            whole = None
            for u, j in enumerate(at):
                gscores = s.p[j, h].astype(f32) * (products[u][h * T : (h + 1) * T] - deltas[u][h])
                whole = gscores if whole is None else whole + gscores
                grads[u].append(gscores.astype(bf16))
            s.dbias[h] += whole
        mixes = []
        for u, j in enumerate(at):
            queries = s.qt[j]
            near = jnp.concatenate(
                [among(queries[h * KEY : (h + 1) * KEY], h * KEY, KH) for h in range(H)], axis=1)
            far = jnp.concatenate([among(lows[u][h], h * VAL, VH) for h in range(H)], axis=1)
            grad_k = nt(jnp.concatenate(grads[u], axis=1), near) * scale
            grad_v = nt(jnp.concatenate([s.p[j, h] for h in range(H)], axis=1), far)
            grad_q = tn(jnp.concatenate(grads[u], axis=0), spaced(s.knat[j], H))[0:T] * scale
            mixes.append(jnp.concatenate([v.astype(bf16) for v in (grad_q, grad_k, grad_v)], axis=1))
        whole = s.gqkv[...]
        for u, j in enumerate(at):
            whole = whole + tn(mixes[u], s.xpad[j, 0:T])
        s.gqkv[...] = whole
        terms = nn(jnp.concatenate(mixes, axis=0), s.w2[...])
        for u, j in enumerate(at):
            s.tmp[u] = s.u[j] + terms[u * T : (u + 1) * T]
            for q in range(H):
                s.tsend[q, j] = s.tmp[u, q * share : (q + 1) * share, :].astype(bf16)
        pl.when(i == 0)(lambda: send_tokens(0))

        @pl.when(i == 1)
        def _():
            shares_done((s.ge1, s.ge1r), 7)
            s.ge2[...] = head_sum((s.ge1, s.ge1r)).reshape(B, z.re // B, 128)
            spread(lambda peer: s.ge2.at[peer], s.ge2r.at[me_b], 3)

        return carry

    def send_tokens(i):
        to = tg_o.at[pl.ds(me_h * n + i * GB, GB)]
        for j in range(1, H):
            to_head(s.tsend.at[head_peers[j], pl.ds(i * GB, GB)], to, 6, j).start()
        pltpu.make_async_copy(s.tsend.at[me_h, pl.ds(i * GB, GB)], to, s.loc.at[7]).start()

    lax.fori_loop(0, n // GB, back_attend, 0)

    for h in range(H):
        for half in range(D // 128):
            lanes = slice(half * 128, (half + 1) * 128)
            at = half * C
            s.gl1[h, at : at + KEY, :] = s.gqkv[h * KEY : (h + 1) * KEY, lanes].astype(bf16)
            s.gl1[h, at + KEY : at + 2 * KEY, :] = s.gqkv[KH + h * KEY : KH + (h + 1) * KEY, lanes].astype(bf16)
            s.gl1[h, at + 2 * KEY : at + C, :] = s.gqkv[2 * KH + h * VAL : 2 * KH + (h + 1) * VAL, lanes].astype(bf16)
        if z.rl > C * (D // 128):
            s.gl1[h, C * (D // 128) :, :] = jnp.zeros((z.rl - C * (D // 128), 128), bf16)
    shares((s.gl1, s.gl1r), 8)
    spread_done(s.ge2, s.ge2r, 3)
    s.ge3[me_b] = batch_sum(s.ge2[me_b], s.ge2r)
    spread(lambda peer: s.ge3.at[me_b], s.ge3.at[me_b], 4)

    slot = lax.broadcasted_iota(jnp.int32, (T, L), 1)
    d_row, d_col = grid_of(slot)
    picks = []
    for down_sign in (1, -1):
        for right_sign in (1, -1):
            r = rows_s + down_sign * d_row
            c = cols_s + right_sign * d_col
            good = (r >= 0) & (r < SIDE) & (c >= 0) & (c < SIDE) & (slot < length)
            if down_sign < 0:
                good = good & (d_row > 0)
            if right_sign < 0:
                good = good & (d_col > 0)
            picks.append((jnp.where(good, r * SIDE + c, 0), good))
    bias_rows = []
    for h in range(H):
        whole = s.dbias[h]
        high = whole.astype(bf16)
        rest = (whole - high.astype(f32)).astype(bf16)
        ordered = nn(high, s.onehot[...]) + nn(rest, s.onehot[...])
        line = jnp.zeros((T, L), f32)
        for index, good in picks:
            line = line + jnp.where(good, take(ordered[:, 0:128], ordered[:, 128:256], index), 0.0)
        bias_rows.append(total(line * s.rowmask[...]))
    start_sum(5, bias_rows)
    for i in range(1, n // GB):
        send_tokens(i)

    shares_done((s.gl1, s.gl1r), 8)
    s.gl2[...] = head_sum((s.gl1, s.gl1r)).reshape(B, z.rl // B, 128)
    spread(lambda peer: s.gl2.at[peer], s.gl2r.at[me_b], 5)
    for h, row in enumerate(finish_sum(5, L)):
        s.brow[h] = row
    spread_done(s.gl2, s.gl2r, 5)
    s.gl3[me_b] = batch_sum(s.gl2[me_b], s.gl2r)
    spread(lambda peer: s.gl3.at[me_b], s.gl3.at[me_b], 6)

    small_o[...] = jnp.zeros(small_o.shape, f32)
    small_o[0:1, :] = sum_gain_1
    small_o[1:2, :] = sum_shift_1
    small_o[2:3, :] = sum_gain_3
    small_o[3:4, :] = sum_shift_3
    small_o[4:5, 0:FH] = s.srow[0:1, own]
    small_o[5:6, 0:FH] = s.srow[1:2, own]
    small_o[6:7, :] = s.brow[me_h]

    spread_done(s.ge3, s.ge3, 4)
    early_o[...] = s.ge3[...].reshape(z.re, 128)
    spread_done(s.gl3, s.gl3, 6)
    late_o[...] = s.gl3[...].reshape(z.rl, 128)

    done(to_head(s.osend.at[some], out_o.at[pl.ds(0, n * (H - 1))], 5, 1))
    done(to_head(s.tsend.at[some], tg_o.at[pl.ds(0, n * (H - 1))], 6, 1))
    c_out.wait()
    pltpu.make_async_copy(s.tsend.at[me_h], tg_o.at[pl.ds(me_h * n, n)], s.loc.at[7]).wait()


def finish_kernel(z, out_i, tg_i, early, late, small, out, tg, qkv, bias, proj, g1, s1, up, g2, s2, down, g3, s3):
    at = lax.broadcasted_iota(jnp.int32, (128, 128), 0)
    to = lax.broadcasted_iota(jnp.int32, (128, 128), 1)
    turn = jnp.where(lax.bitwise_and(at, 7) * 16 + lax.shift_right_logical(at, 3) == to, 1.0, 0.0).astype(bf16)
    whole = z.share // 16 * 16
    for src, dst in ((out_i, out), (tg_i, tg)):
        for i in range(0, src.shape[0], 8):
            for k in range(0, whole, 16):
                rows = src[i : i + 8, k : k + 16, :].reshape(128, z.D)
                dst[k : k + 16, i : i + 8, :] = nn(turn, rows).reshape(16, 8, z.D)
            for k in range(whole, z.share):
                dst[k, i : i + 8, :] = src[i : i + 8, k, :].astype(f32)

    @pl.when(pl.program_id(0) == 0)
    def _():
        D, C, PH = z.D, z.C, z.D // z.H
        down[...] = early[0:D, :].T
        up[...] = early[D : 2 * D, :]
        for half in range(D // 128):
            lanes = slice(half * 128, (half + 1) * 128)
            proj[:, lanes] = early[2 * D + half * PH : 2 * D + (half + 1) * PH, :]
            qkv[0, :, lanes] = late[half * C : (half + 1) * C, :]
        g1[...] = small[0:1, :]
        s1[...] = small[1:2, :]
        g3[...] = small[2:3, :]
        s3[...] = small[3:4, :]
        g2[...] = small[4:5, 0 : z.F // z.H]
        s2[...] = small[5:6, 0 : z.F // z.H]
        bias[...] = small[6:7, 0 : z.length]


def on_device(H, B, tokens, image_count, token_place, qkv_weight, bias_table, proj_weight, attention_gain,
              attention_shift, up_weight, hidden_gain, hidden_shift, down_weight, output_gain, output_shift,
              cotangent):
    images, length, width = tokens.shape
    z = types.SimpleNamespace(
        n=images // H, T=round_up(length, 16), L=round_up(length, 128), D=width, F=up_weight.shape[1] * H,
        H=H, B=B, C=qkv_weight.shape[1], share=cotangent.shape[1], length=length)
    z.re = round_up(2 * z.D + z.D // H * (z.D // 128), 8 * max(B, 2))
    z.rl = round_up(z.C * (z.D // 128), 8 * max(B, 2))
    z.group = max(g for g in (1, 2, 3, 4) if z.n % g == 0)
    z.group_back = max(g for g in (1, 2, 3) if z.n % g == 0)
    z.direct = H == 4 and B <= 8
    z.sums = {}
    for k, r in enumerate((2 * z.D, 2 * z.F, 4 * z.D, 2 * z.F, 2 * z.D, H * z.L)):
        z.sums["sum%d" % k] = pltpu.VMEM((H * B if z.direct else H, r // 128, 128), f32)
        if not z.direct:
            z.sums["part%d" % (k % 2)] = pltpu.VMEM((B, 8, 128), f32)

    def bufs(s, k):
        first = getattr(s, "sum%d" % k)
        return first, None if z.direct else getattr(s, "part%d" % (k % 2)).at[:, 0 : first.shape[1]]

    z.bufs = bufs
    scratch = layout(z)
    hbm = pl.BlockSpec(memory_space=pl.ANY)
    vmem = pl.BlockSpec(memory_space=pltpu.VMEM)
    smem = pl.BlockSpec(memory_space=pltpu.SMEM)
    outs = pl.pallas_call(
        functools.partial(block_kernel, z, tuple(scratch)),
        out_shape=(
            jax.ShapeDtypeStruct((images, z.share, width), bf16),
            jax.ShapeDtypeStruct((images, z.share, width), bf16),
            jax.ShapeDtypeStruct((z.re, 128), f32),
            jax.ShapeDtypeStruct((z.rl, 128), f32),
            jax.ShapeDtypeStruct((8, width), f32),
        ),
        in_specs=[hbm, smem, vmem, hbm, vmem, hbm, vmem, vmem, hbm, vmem, vmem, hbm, vmem, vmem, hbm],
        out_specs=(hbm, hbm, vmem, vmem, vmem),
        scratch_shapes=list(scratch.values()),
        compiler_params=pltpu.CompilerParams(
            collective_id=0, has_side_effects=True, vmem_limit_bytes=127 * 512 * 1024
        ),
    )(
        tokens.transpose(1, 0, 2), image_count, token_place.reshape(1, -1), qkv_weight, bias_table, proj_weight,
        attention_gain.reshape(1, -1), attention_shift.reshape(1, -1), up_weight, hidden_gain.reshape(1, -1),
        hidden_shift.reshape(1, -1), down_weight, output_gain.reshape(1, -1), output_shift.reshape(1, -1),
        cotangent.transpose(1, 0, 2),
    )

    steps = 2
    block = pl.BlockSpec((images // steps, z.share, width), lambda i: (i, 0, 0))
    turned = pl.BlockSpec((z.share, images // steps, width), lambda i: (0, i, 0))

    def whole(*shape):
        return jax.ShapeDtypeStruct(shape, f32), pl.BlockSpec(shape, lambda i: (0,) * len(shape))

    fh = z.F // H
    small = [
        whole(1, z.C, width), whole(1, length), whole(width // H, width), whole(1, width), whole(1, width),
        whole(width, fh), whole(1, fh), whole(1, fh), whole(fh, width), whole(1, width), whole(1, width)]
    big = jax.ShapeDtypeStruct((z.share, images, width), f32)
    res = pl.pallas_call(
        functools.partial(finish_kernel, z),
        grid=(steps,),
        out_shape=[big, big] + [a for a, _ in small],
        in_specs=[block, block, whole(z.re, 128)[1], whole(z.rl, 128)[1], whole(8, width)[1]],
        out_specs=[turned, turned] + [b for _, b in small],
        compiler_params=pltpu.CompilerParams(vmem_limit_bytes=32 * 1024 * 1024),
    )(*outs)
    res = [res[0].transpose(1, 0, 2), res[1].transpose(1, 0, 2), *res[2:]]
    for k in (5, 6, 8, 9, 11, 12):
        res[k] = res[k].reshape(-1)
    return tuple(res)


def solution(mesh):
    H, B = mesh.shape["head"], mesh.shape["batch"]
    placed = (
        P("batch", None, None),
        P("batch"),
        P(),
        P("head", None, None),
        P("head", None),
        P(),
        P(),
        P(),
        P(None, "head"),
        P("head"),
        P("head"),
        P("head", None),
        P(),
        P(),
        P("batch", "head", None),
    )
    return jax.shard_map(
        functools.partial(on_device, H, B),
        mesh=mesh,
        in_specs=placed,
        out_specs=(
            P("batch", "head", None),
            P("batch", "head", None),
            P("head", None, None),
            P("head", None),
            P("head", None),
            P(),
            P(),
            P(None, "head"),
            P("head"),
            P("head"),
            P("head", None),
            P(),
            P(),
        ),
        check_vma=False,
    )
```

```python
import functools
import types

import jax
import jax.numpy as jnp
from jax import lax
from jax.experimental import pallas as pl
from jax.experimental.pallas import tpu as pltpu
from jax.sharding import PartitionSpec as P

KEY = 32
VAL = 64
SIDE = 14
EPSILON = 1e-05
LOG2E = 1.4426950408889634
MESH = pl.DeviceIdType.MESH
f32 = jnp.float32
bf16 = jnp.bfloat16


def nn(left, right):
    return lax.dot_general(left, right, (((1,), (0,)), ((), ())), preferred_element_type=f32)


def nt(left, right):
    return lax.dot_general(left, right, (((1,), (1,)), ((), ())), preferred_element_type=f32)


def tn(left, right):
    return lax.dot_general(left, right, (((0,), (0,)), ((), ())), preferred_element_type=f32)


def among(block, at, total_rows):
    parts = []
    if at > 0:
        parts.append(jnp.zeros((at, block.shape[1]), block.dtype))
    parts.append(block)
    if at + block.shape[0] < total_rows:
        parts.append(jnp.zeros((total_rows - at - block.shape[0], block.shape[1]), block.dtype))
    return jnp.concatenate(parts, axis=0)


def spaced(value, heads):
    rows, columns = value.shape
    each = columns // heads
    lane = lax.broadcasted_iota(jnp.int32, (rows, columns), 1)
    return jnp.concatenate(
        [jnp.where((lane >= h * each) & (lane < (h + 1) * each), value, jnp.zeros_like(value)) for h in range(heads)],
        axis=0)


def round_up(value, step):
    return -(-value // step) * step


def sigmoid(value):
    return 0.5 * jnp.tanh(0.5 * value) + 0.5


def fold(value):
    rows, columns = value.shape
    return jnp.sum(value.reshape(rows // 8, 8, columns), axis=0)


def total(value):
    return jnp.sum(value, axis=0, keepdims=True)


def lookup(table, index):
    rows = index.shape[0]
    low = jnp.broadcast_to(table[:, 0:128], (rows, 128))
    high = jnp.broadcast_to(table[:, 128:256], (rows, 128))
    return take(low, high, index)


def take(low, high, index):
    parts = []
    for half in range(2):
        at = index[:, half * 128 : (half + 1) * 128]
        inside = lax.bitwise_and(at, 127)
        first = jnp.take_along_axis(low, inside, axis=1, mode="promise_in_bounds")
        second = jnp.take_along_axis(high, inside, axis=1, mode="promise_in_bounds")
        parts.append(jnp.where(at < 128, first, second))
    return jnp.concatenate(parts, axis=1)


def layout(z):
    n, T, L, D, F, H, B, C = z.n, z.T, z.L, z.D, z.F, z.H, z.B, z.C
    dma = pltpu.SemaphoreType.DMA
    vmem = pltpu.VMEM
    return {
        "xt": vmem((T, 16, D), bf16),
        "ct": vmem((T, 16, D), bf16),
        "cin": vmem((round_up(z.share, 4), H * n, D), bf16),
        "mix": vmem((n * 16, 256), bf16),
        "unmix": vmem((n * 16, n * 16), bf16),
        "deal": vmem((H * n * 4, H * n * 4), bf16),
        "qkvg": vmem((H, C, D), bf16),
        "downg": vmem((H, F // H, D), bf16),
        "smallg": vmem((H, 4, 128), f32),
        "w2": vmem((H * C, D), bf16),
        "upcat": vmem((D, F), bf16),
        "projw": vmem((D, D), bf16),
        "bias": vmem((H, T, L), f32),
        "dbias": vmem((H, T, L), f32),
        "rowmask": vmem((T, D), f32),
        "onehot": vmem((L, L), bf16),
        "xpad": vmem((n, L, D), bf16),
        "qt": vmem((n, H * KEY, L), bf16),
        "knat": vmem((n, T, H * KEY), bf16),
        "vnat": vmem((n, T, H * VAL), bf16),
        "tmp": vmem((z.group, T, D), f32),
        "p": vmem((n, H, T, L), bf16),
        "linv": vmem((n, H, 1, L), f32),
        "att": vmem((n, H * VAL, L), f32),
        "act": vmem((n, H * VAL, L), bf16),
        "proj": vmem((n, T, D), f32),
        "hid": vmem((n, T, F), f32),
        "slope": vmem((n, T, F), f32),
        "act2": vmem((n, T, F), bf16),
        "out": vmem((n, T, D), f32),
        "u": vmem((n, T, D), f32),
        "gproj": vmem((n, L, D), bf16),
        "osend": vmem((H, n, z.share, D), bf16),
        "tsend": vmem((H, n, z.share, D), bf16),
        "gdown": vmem((D, F), f32),
        "gup": vmem((D, F), f32),
        "gpr": vmem((D, D), f32),
        "gqkv": vmem((H * C, D), f32),
        "srow": vmem((2, F), f32),
        "brow": vmem((H, 1, L), f32),
        **z.sums,
        "cnt": vmem((B, 1, 128), f32),
        "ge1": vmem((H, z.re, 128), bf16),
        "ge1r": vmem((H, z.re, 128), bf16),
        "ge2": vmem((B, z.re // B, 128), f32),
        "ge2r": vmem((B, z.re // B, 128), f32),
        "ge3": vmem((B, z.re // B, 128), f32),
        "gl1": vmem((H, z.rl, 128), bf16),
        "gl1r": vmem((H, z.rl, 128), bf16),
        "gl2": vmem((B, z.rl // B, 128), f32),
        "gl2r": vmem((B, z.rl // B, 128), f32),
        "gl3": vmem((B, z.rl // B, 128), f32),
        "loc": dma((8,)),
        "hs": dma((9,)),
        "hr": dma((9,)),
        "ass": dma((12,)),
        "asr": dma((12,)),
        "bs": dma((7,)),
        "br": dma((7,)),
        "ready": pltpu.SemaphoreType.REGULAR,
    }


def block_kernel(z, names, *refs):
    (tokens, count, place, qkv_w, table, proj_w, gain_1, shift_1, up_w, gain_2, shift_2, down_w,
     gain_3, shift_3, cot, out_o, tg_o, early_o, late_o, small_o) = refs[:20]
    s = types.SimpleNamespace(**dict(zip(names, refs[20:], strict=True)))
    n, T, L, D, F, H, B, C = z.n, z.T, z.L, z.D, z.F, z.H, z.B, z.C
    share, length = z.share, z.length
    me_h = lax.axis_index("head")
    me_b = lax.axis_index("batch")

    def local(src, dst, k):
        copy = pltpu.make_async_copy(src, dst, s.loc.at[k])
        copy.start()
        return copy

    def to_head(src, dst, k, j):
        return pltpu.make_async_remote_copy(
            src_ref=src, dst_ref=dst, send_sem=s.hs.at[k], recv_sem=s.hr.at[k],
            device_id={"head": head_peers[j]}, device_id_type=MESH)

    def to_batch(src, dst, k, peer):
        return pltpu.make_async_remote_copy(
            src_ref=src, dst_ref=dst, send_sem=s.bs.at[k], recv_sem=s.br.at[k],
            device_id={"batch": peer}, device_id_type=MESH)

    head_peers = [lax.rem(me_h + j, H) for j in range(H)]
    core = lax.rem(me_b, 2)
    sibling = me_b + 1 - 2 * core

    def done(copies):
        copies.wait()

    def around(size, step):
        if size <= 8:
            for j in range(1, size):
                step(j)
        else:
            lax.fori_loop(1, size, lambda j, c: (step(j), c)[1], 0)

    FH = F // H
    PH = D // H
    own = pl.ds(pl.multiple_of(me_h * FH, FH), FH)
    qkv_32, up_32, down_32 = s.gqkv.at[0:C], s.gup.at[:, 0:FH], s.gdown.at[0:FH, 0:D]
    c_qkv = local(qkv_w.at[0], qkv_32, 0)
    c_up = local(up_w, up_32, 1)
    c_down = local(down_w, down_32, 2)
    def window(slot):
        return pl.multiple_of(slot * n // 8 * 8, 8)

    c_tok = local(tokens.at[:, pl.ds(window(me_h), 16)], s.xt.at[pl.ds(0, length)], 3)
    c_proj = local(proj_w, s.gpr, 4)
    c_cot = local(cot, s.cin.at[pl.ds(0, share)], 6)

    def everyone():
        pairs = [(a, b) for a in range(H) for b in range(B) if a or b]
        return sorted(pairs, key=lambda p: -(p[0] % 2 + p[0] // 2 + (2 if p[1] > 1 else p[1] / 4)))

    def at_offset(a, b):
        x, y = lax.rem(me_h, 2), lax.div(me_h, 2)
        other = (y + a // 2 - 2 * y * (a // 2)) * 2 + x + a % 2 - 2 * x * (a % 2)
        return {"head": other, "batch": lax.rem(me_b + b, B)}

    barrier = pltpu.get_barrier_semaphore()
    for j in range(1, H):
        pl.semaphore_signal(barrier, inc=1, device_id={"head": head_peers[j]}, device_id_type=MESH)

    def greet(semaphore):
        around(B, lambda j: pl.semaphore_signal(
            semaphore, inc=1, device_id={"batch": lax.rem(me_b + j, B)}, device_id_type=MESH))

    greet(barrier)
    targets = [at_offset(*pair) for pair in everyone()] if z.direct else []

    s.smallg[me_h] = jnp.concatenate(
        [gain_2[...], shift_2[...], table[:, 0:128], jnp.concatenate(
            [table[:, 128:length], jnp.zeros((1, 256 - length), f32)], axis=1)], axis=0)
    c_qkv.wait()
    s.qkvg[me_h] = qkv_32[...].astype(bf16)
    up_rows = pl.ds(pl.multiple_of(core * (D // 2), D // 2), D // 2)
    down_rows = pl.ds(pl.multiple_of(core * (FH // 2), FH // 2), FH // 2)
    c_up.wait()
    s.upcat[up_rows, own] = s.gup[up_rows, 0:FH].astype(bf16)
    c_down.wait()
    s.downg[me_h, down_rows] = s.gdown[down_rows, 0:D].astype(bf16)

    row_at = lax.broadcasted_iota(jnp.int32, (L, L), 0)
    lane_at = lax.broadcasted_iota(jnp.int32, (L, L), 1)
    s.rowmask[...] = jnp.where(row_at < length, 1.0, 0.0)[0:T]
    place_lane = jnp.broadcast_to(
        jnp.concatenate([place[...].astype(f32), jnp.zeros((1, L - length), f32)], axis=1), (L, L))
    place_row = place_lane.T
    s.onehot[...] = jnp.where((place_row == lane_at.astype(f32)) & (row_at < length), 1.0, 0.0).astype(bf16)

    def grid_of(at):
        at = at.astype(jnp.int32)
        row = lax.shift_right_logical(at * 4682, 16)
        return row, at - row * SIDE

    rows_t, cols_t = grid_of(place_lane[0:T])
    rows_s, cols_s = grid_of(place_row[0:T])
    offsets = jnp.abs(rows_s - rows_t) * SIDE + jnp.abs(cols_s - cols_t)
    for h in range(H):
        s.dbias[h] = jnp.zeros((T, L), f32)
    s.gdown[...] = jnp.zeros(s.gdown.shape, f32)
    s.gup[...] = jnp.zeros(s.gup.shape, f32)
    s.gqkv[...] = jnp.zeros(s.gqkv.shape, f32)

    def valid_of(i):
        return jnp.where(me_h * n + i < count[0], 1.0, 0.0)

    c_proj.wait()
    s.projw[...] = s.gpr[...].astype(bf16)
    s.gpr[...] = jnp.zeros(s.gpr.shape, f32)
    line_at = lax.broadcasted_iota(jnp.int32, (n * 16, 256), 0)
    pick_at = lax.broadcasted_iota(jnp.int32, (n * 16, 256), 1)
    image_at = lax.shift_right_logical(line_at, 4)
    s.mix[...] = jnp.where(
        (lax.bitwise_and(line_at, 15) == lax.shift_right_logical(pick_at, 4))
        & (lax.bitwise_and(pick_at, 15) == image_at + (me_h * n - window(me_h)))
        & (image_at + me_h * n < count[0]),
        1.0, 0.0).astype(bf16)
    s.xt[length:T] = jnp.zeros((T - length, 16, D), bf16)
    s.u[:, T - 16 : T, :] = jnp.zeros((n, 16, D), f32)
    s.xpad[:, T:L, :] = jnp.zeros((n, L - T, D), bf16)
    s.gproj[:, T:L, :] = jnp.zeros((n, L - T, D), bf16)
    c_tok.wait()

    def enter_tokens(k, carry):
        at = pl.ds(pl.multiple_of(k * 16, 16), 16)
        s.xpad[:, at, :] = nn(s.mix[...], s.xt[at].reshape(256, D)).astype(bf16).reshape(n, 16, D)
        return carry

    lax.fori_loop(0, T // 16, enter_tokens, 0)


    blocks = -(-share * n // 16)
    step = n * 4 // 16

    def over(value, divisor):
        return lax.shift_right_logical(value * (65536 // divisor + 1), 16)

    def square(size):
        return (lax.broadcasted_iota(jnp.int32, (size, size), 0),
                lax.broadcasted_iota(jnp.int32, (size, size), 1))

    to, at = square(n * 16)
    image_to = lax.shift_right_logical(to, 4)
    s.unmix[...] = jnp.where(
        (at == lax.bitwise_and(to, 15) * n + image_to) & (image_to + me_h * n < count[0]), 1.0, 0.0).astype(bf16)
    to, at = square(H * n * 4)
    owner = over(to, n * 4)
    inside = to - owner * (n * 4)
    token_to = over(inside, n)
    s.deal[...] = jnp.where(
        at == token_to * (H * n) + owner * n + inside - token_to * n, 1.0, 0.0).astype(bf16)
    s.cin[share:] = jnp.zeros((s.cin.shape[0] - share, H * n, D), bf16)
    c_cot.wait()

    def deal(k, wide):
        dealt = nn(s.deal[...], s.cin[pl.ds(k * 4, 4)].reshape(H * n * 4, D)).astype(bf16)
        for h in range(H):
            piece = dealt[h * n * 4 : h * n * 4 + wide * 16].reshape(wide, 16, D)
            s.xt[pl.ds(h * blocks + k * step, wide)] = piece

    lax.fori_loop(0, share // 4, lambda k, c: (deal(k, step), c)[1], 0)
    if share % 4:
        deal(share // 4, blocks - share // 4 * step)
    own_blocks = pl.ds(me_h * blocks, blocks)
    c_own = local(s.xt.at[own_blocks], s.ct.at[own_blocks], 5)

    def enter_cotangent(q):
        first = q * blocks
        for k in range(share // 16):
            rows = s.ct[first + k * n : first + (k + 1) * n].reshape(n * 16, D)
            at = q * share + k * 16
            s.u[:, at : at + 16, :] = nn(s.unmix[...], rows).reshape(n, 16, D)
        rest = s.ct[first + share // 16 * n].astype(f32)
        for i in range(n):
            at = q * share + share // 16 * 16
            s.u[i, at : at + 1, :] = rest[i : i + 1] * valid_of(i)

    s.cnt[me_b] = jnp.full((1, 128), count[0]).astype(f32)
    pl.semaphore_wait(barrier, H - 1 + B - 1)

    shared = (s.qkvg.at[me_h], s.smallg.at[me_h], s.upcat.at[up_rows, own], s.downg.at[me_h, down_rows])
    for k in (1, 0, 2, 3):
        for j in range(1, H):
            to_head(shared[k], shared[k], k, j).start()
    greet(s.ready)

    cuts = (0, blocks * 6 // 10, blocks)

    def send_cotangent(piece):
        low, high = cuts[piece], cuts[piece + 1]
        for j in range(1, H):
            to_head(s.xt.at[pl.ds(head_peers[j] * blocks + low, high - low)],
                    s.ct.at[pl.ds(me_h * blocks + low, high - low)], 4, j).start()

    around(B, lambda j: to_batch(s.cnt.at[me_b], s.cnt.at[me_b], 0, lax.rem(me_b + j, B)).start())
    send_cotangent(0)

    some = pl.ds(0, H - 1)
    done(to_head(s.smallg.at[some], s.smallg.at[some], 1, 1))
    for h in range(H):
        line = jnp.concatenate([s.smallg[h, 2:3, :], s.smallg[h, 3:4, :]], axis=1)
        s.bias[h] = jnp.where(row_at[0:T] < length, lookup(line, offsets) * LOG2E, -1e30)
    done(to_head(s.qkvg.at[some], s.qkvg.at[some], 0, 1))
    for h in range(H):
        s.w2[h * KEY : (h + 1) * KEY] = s.qkvg[h, 0:KEY]
        s.w2[(H + h) * KEY : (H + h + 1) * KEY] = s.qkvg[h, KEY : 2 * KEY]
        at = 2 * H * KEY + h * VAL
        s.w2[at : at + VAL] = s.qkvg[h, 2 * KEY : C]

    scale = KEY**-0.5
    KH, VH = H * KEY, H * VAL

    def attend(i, carry):
        first, second = carry
        at = [i * z.group + u for u in range(z.group)]
        mixed, scores = [], []
        for j in at:
            x = s.xpad[j]
            mixed.append(nt(s.w2[...], x).astype(bf16))
            s.qt[j] = mixed[-1][0:KH]
            natural = nt(x[0:T], s.w2[KH : H * C]).astype(bf16)
            s.knat[j] = natural[:, 0:KH]
            s.vnat[j] = natural[:, KH:]
            scores.append(natural[:, 0:KH])
        for u in range(z.group):
            scores[u] = nn(spaced(scores[u], H), mixed[u][0:KH])
        for h in range(H):
            for u, j in enumerate(at):
                logits = scores[u][h * T : (h + 1) * T] * (scale * LOG2E) + s.bias[h]
                raised = jnp.exp2(logits - jnp.max(logits, axis=0, keepdims=True))
                inverse = 1.0 / total(raised)
                s.linv[j, h] = inverse
                low = raised.astype(bf16)
                s.p[j, h] = low
                values = mixed[u][2 * KH + h * VAL : 2 * KH + (h + 1) * VAL, 0:T]
                attended = nn(values, low) * inverse
                s.att[j, h * VAL : (h + 1) * VAL] = attended
                s.act[j, h * VAL : (h + 1) * VAL] = (attended * sigmoid(attended)).astype(bf16)
        for j in at:
            projected = tn(s.act[j], s.projw[...])[0:T] * s.rowmask[...]
            s.proj[j] = projected
            first, second = first + fold(projected), second + fold(projected * projected)
        return first, second

    def zeros(width):
        return jnp.zeros((8, width), f32)

    def port(k, src, dst, device):
        return pltpu.make_async_remote_copy(
            src_ref=src, dst_ref=dst, send_sem=s.ass.at[k], recv_sem=s.asr.at[k],
            device_id=device, device_id_type=MESH)

    def sum_slots(buf, size):
        if size <= 32:
            whole = buf[0]
            for b in range(1, size):
                whole = whole + buf[b]
            return whole
        return lax.fori_loop(1, size, lambda b, c: c + buf[b], buf[0])

    def start_sum(k, rows):
        buf = z.bufs(s, k)[0]
        me = me_h * B + me_b if z.direct else me_h
        r = 0
        for row in rows:
            for c in range(row.shape[1] // 128):
                buf[me, r : r + 1, :] = row[:, c * 128 : (c + 1) * 128]
                r += 1
        for target in targets if z.direct else [{"head": p} for p in head_peers[1:]]:
            port(k, buf.at[me], buf.at[me], target).start()

    def finish_sum(k, width):
        others = z.bufs(s, k)[0].at[pl.ds(0, H * B - 1 if z.direct else H - 1)]
        done(port(k, others, others, {"head": head_peers[1]}))
        bufs = z.bufs(s, k)
        if z.direct:
            whole = sum_slots(bufs[0], H * B)
        else:
            bufs[1][me_b] = sum_slots(bufs[0], H)
            mine = bufs[1].at[me_b]
            around(B, lambda j: port(k + 6, mine, mine, {"batch": lax.rem(me_b + j, B)}).start())
            others = bufs[1].at[pl.ds(0, B - 1)]
            done(port(k + 6, others, others, {"batch": lax.rem(me_b + 1, B)}))
            whole = sum_slots(bufs[1], B)
        step = width // 128
        return [
            jnp.concatenate([whole[r + c : r + c + 1] for c in range(step)], axis=1)
            for r in range(0, whole.shape[0], step)
        ]

    first, second = lax.fori_loop(0, n // z.group, attend, (zeros(D), zeros(D)))
    pl.semaphore_wait(s.ready, B - 1)
    some_rows = pl.ds(0, D // 2)
    done(to_head(s.upcat.at[some_rows, pl.ds(0, FH * (H - 1))], s.upcat.at[some_rows, pl.ds(0, FH * (H - 1))], 2, 1))
    down_some = s.downg.at[some, pl.ds(0, FH // 2)]
    done(to_head(down_some, down_some, 3, 1))
    halves = (s.upcat.at[up_rows, :], s.downg.at[:, down_rows])
    for k in range(2):
        to_batch(halves[k], halves[k], k + 1, sibling).start()
    start_sum(0, [total(first), total(second)])
    send_cotangent(1)
    for k in range(2):
        to_batch(halves[k], halves[k], k + 1, sibling).wait()
    down = s.downg[...].reshape(F, D)
    gain_2w = jnp.concatenate([s.smallg[h, 0:1, :] for h in range(H)], axis=1)
    shift_2w = jnp.concatenate([s.smallg[h, 1:2, :] for h in range(H)], axis=1)
    others = s.cnt.at[pl.ds(0, B - 1)]
    done(to_batch(others, others, 0, sibling))
    seen_part = sum_slots(s.cnt, B) * float(length)
    seen_row = jnp.concatenate([seen_part] * (D // 128), axis=1)
    sums = finish_sum(0, D)
    seen_wide = jnp.concatenate([seen_row] * (F // D), axis=1)

    def moments(first, second, seen):
        mean = first / seen
        return mean, lax.rsqrt(second / seen - mean * mean + EPSILON)

    mean_1, inverse_1 = moments(sums[0], sums[1], seen_row)
    a_1 = gain_1[...] * inverse_1
    b_1 = shift_1[...] - mean_1 * a_1

    G = z.group
    GT = G * T

    def group(ref, i):
        return ref[pl.ds(i * G, G), 0:T].reshape(GT, ref.shape[2])

    def put(ref, i, value):
        ref[pl.ds(i * G, G), 0:T] = value.reshape(G, T, value.shape[1])

    def mask_of(i):
        return jnp.concatenate([s.rowmask[...] * valid_of(i * G + u) for u in range(G)], axis=0)

    def residual_of(i):
        return group(s.xpad, i).astype(f32) + (group(s.proj, i) * a_1 + b_1 * mask_of(i))

    def enter(i, carry):
        first, second = carry
        residual = residual_of(i).astype(bf16)
        hidden = nn(residual, s.upcat[...])
        put(s.hid, i, hidden)
        return first + fold(hidden), second + fold(hidden * hidden)

    first, second = lax.fori_loop(0, n // G, enter, (zeros(F), zeros(F)))
    start_sum(1, [total(first), total(second)])
    others = s.ct.at[pl.ds(0, blocks * (H - 1))]
    done(to_head(others, others, 4, 1))
    c_own.wait()
    for q in range(H):
        enter_cotangent(q)
    sums = finish_sum(1, F)
    mean_2, inverse_2 = moments(sums[0], sums[1], seen_wide)
    a_2 = gain_2w * inverse_2
    b_2 = shift_2w - mean_2 * a_2

    def leave(i, carry):
        one, two, three, four = carry
        shaped = group(s.hid, i) * a_2 + b_2
        gate = sigmoid(shaped)
        active = shaped * gate
        put(s.slope, i, gate + active * (1.0 - gate))
        low = active.astype(bf16)
        put(s.act2, i, low)
        outgoing = nn(low, down)
        put(s.out, i, outgoing)
        upstream = group(s.u, i)
        masked = outgoing * mask_of(i)
        return (one + fold(masked), two + fold(masked * outgoing), three + fold(upstream),
                four + fold(upstream * outgoing))

    sums = lax.fori_loop(0, n // G, leave, (zeros(D), zeros(D), zeros(D), zeros(D)))
    start_sum(2, [total(v) for v in sums])
    sums = finish_sum(2, D)
    mean_3, inverse_3 = moments(sums[0], sums[1], seen_row)
    a_3 = gain_3[...] * inverse_3
    b_3 = shift_3[...] - mean_3 * a_3
    sum_shift_3 = sums[2]
    sum_gain_3 = inverse_3 * (sums[3] - mean_3 * sum_shift_3)

    def back(gain, mean, inverse, sum_shift, sum_gain, seen):
        scaled = gain * inverse
        slope = -scaled * inverse * (sum_gain / seen)
        return scaled, slope, -scaled * (sum_shift / seen) - slope * mean

    s_3, v_3, r_3 = back(gain_3[...], mean_3, inverse_3, sum_shift_3, sum_gain_3, seen_row)

    def back_leave(i, carry):
        one, two = carry
        grad = (group(s.u, i) * s_3 + (group(s.out, i) * v_3 + r_3) * mask_of(i)).astype(bf16)
        put(s.gproj, i, grad)
        shaped = nt(grad, down) * group(s.slope, i)
        put(s.slope, i, shaped)
        return one + fold(shaped), two + fold(shaped * group(s.hid, i))

    def down_gradient(i, carry):
        s.gdown[...] += tn(group(s.gproj, i), group(s.act2, i))
        return carry

    def output(i):
        s.tmp[...] = ((residual_of(i) + (group(s.out, i) * a_3 + b_3)) * mask_of(i)).reshape(G, T, D)
        for u in range(G):
            for q in range(H):
                s.osend[q, i * G + u] = s.tmp[u, q * share : (q + 1) * share, :].astype(bf16)

    def early(at, parts):
        for h, part in enumerate(parts):
            s.ge1[h, at : at + part.shape[0], :] = part.astype(bf16)

    def send_early(low, high):
        rows = pl.ds(low, high - low)
        for j in range(1, H):
            to_head(s.ge1.at[head_peers[j], rows], s.ge1r.at[me_h, rows], 7, j).start()

    def send_output(low, high):
        low, high = low * n // 12, high * n // 12
        if high > low:
            to = out_o.at[pl.ds(me_h * n + low, high - low)]
            for j in range(1, H):
                to_head(s.osend.at[head_peers[j], pl.ds(low, high - low)], to, 5, j).start()

    first, second = lax.fori_loop(0, n // G, back_leave, (zeros(F), zeros(F)))
    start_sum(3, [total(first), total(second)])
    output(0)
    send_output(0, 4)
    lax.fori_loop(0, n // G, down_gradient, 0)
    for i in range(1, n // G):
        output(i)
    early(0, [s.gdown[:, h * FH : (h + 1) * FH] for h in range(H)])
    sums = finish_sum(3, F)

    sum_shift_2 = sums[0]
    sum_gain_2 = inverse_2 * (sums[1] - mean_2 * sum_shift_2)
    s_2, v_2, r_2 = back(gain_2w, mean_2, inverse_2, sum_shift_2, sum_gain_2, seen_wide)
    s.srow[0:1, :] = sum_gain_2
    s.srow[1:2, :] = sum_shift_2

    def back_enter(i, carry):
        one, two = carry
        mask = jnp.concatenate([mask_of(i)] * (F // D), axis=1)
        grad = (group(s.slope, i) * s_2 + group(s.hid, i) * v_2 + r_2 * mask).astype(bf16)
        put(s.act2, i, grad)
        upstream = group(s.u, i) + nt(grad, s.upcat[...])
        put(s.u, i, upstream)
        return one + fold(upstream), two + fold(upstream * group(s.proj, i))

    first, second = lax.fori_loop(0, n // G, back_enter, (zeros(D), zeros(D)))
    start_sum(4, [total(first), total(second)])
    send_early(0, D)

    def up_gradient(i, carry):
        s.gup[...] += tn(residual_of(i).astype(bf16), group(s.act2, i))
        return carry

    lax.fori_loop(0, n // G, up_gradient, 0)
    early(D, [s.gup[:, h * FH : (h + 1) * FH] for h in range(H)])
    send_early(D, 2 * D)
    sums = finish_sum(4, D)
    c_out = local(s.osend.at[me_h], out_o.at[pl.ds(me_h * n, n)], 6)
    sum_shift_1 = sums[0]
    sum_gain_1 = inverse_1 * (sums[1] - mean_1 * sum_shift_1)
    s_1, v_1, r_1 = back(gain_1[...], mean_1, inverse_1, sum_shift_1, sum_gain_1, seen_row)

    def back_project(i, carry):
        grad = (group(s.u, i) * s_1 + group(s.proj, i) * v_1 + r_1 * mask_of(i)).astype(bf16)
        put(s.gproj, i, grad)
        whole = s.gpr[...]
        for u in range(G):
            whole = whole + nn(s.act[i * G + u], s.gproj[i * G + u])
        s.gpr[...] = whole
        return carry

    lax.fori_loop(0, n // G, back_project, 0)

    def shares(buffer, k):
        for j in range(1, H):
            to_head(buffer[0].at[head_peers[j]], buffer[1].at[me_h], k, j).start()

    def shares_done(buffer, k):
        done(to_head(buffer[0].at[some], buffer[1].at[some], k, 1))

    def head_sum(buffer):
        whole = buffer[0][me_h].astype(f32)
        for j in range(1, H):
            whole = whole + buffer[1][head_peers[j]].astype(f32)
        return whole

    def spread(src, dst, k):
        around(B, lambda j: to_batch(src(lax.rem(me_b + j, B)), dst, k, lax.rem(me_b + j, B)).start())

    def spread_done(src, dst, k):
        others = pl.ds(0, B - 1)
        done(to_batch(src.at[others], dst.at[others], k, sibling))

    def batch_sum(own, received):
        if B <= 8:
            whole = own
            for j in range(1, B):
                whole = whole + received[lax.rem(me_b + j, B)]
            return whole
        return lax.fori_loop(1, B, lambda j, c: c + received[lax.rem(me_b + j, B)], own)

    for half in range(D // 128):
        lanes = slice(half * 128, (half + 1) * 128)
        early(2 * D + half * PH, [s.gpr[h * PH : (h + 1) * PH, lanes] for h in range(H)])
    filled = 2 * D + D // 128 * PH
    if z.re > filled:
        s.ge1[:, filled:, :] = jnp.zeros((H, z.re - filled, 128), bf16)
    send_early(2 * D, z.re)
    send_output(4, 12)

    GB = z.group_back

    def back_attend(i, carry):
        at = [i * GB + u for u in range(GB)]
        lows, deltas, products = [], [], []
        for j in at:
            att = s.att[j]
            gate = sigmoid(att)
            active = att * gate
            gact = nt(s.projw[...], s.gproj[j]) * (gate + active * (1.0 - gate))
            low, delta = [], []
            for h in range(H):
                rows = slice(h * VAL, (h + 1) * VAL)
                grad = gact[rows] * s.linv[j, h]
                low.append(grad.astype(bf16))
                delta.append(total(grad * att[rows]))
            lows.append(low)
            deltas.append(delta)
            products.append(nn(spaced(s.vnat[j], H), jnp.concatenate(low, axis=0)))
        grads = [[] for _ in at]
        for h in range(H):
            whole = None
            for u, j in enumerate(at):
                gscores = s.p[j, h].astype(f32) * (products[u][h * T : (h + 1) * T] - deltas[u][h])
                whole = gscores if whole is None else whole + gscores
                grads[u].append(gscores.astype(bf16))
            s.dbias[h] += whole
        mixes = []
        for u, j in enumerate(at):
            queries = s.qt[j]
            near = jnp.concatenate(
                [among(queries[h * KEY : (h + 1) * KEY], h * KEY, KH) for h in range(H)], axis=1)
            far = jnp.concatenate([among(lows[u][h], h * VAL, VH) for h in range(H)], axis=1)
            grad_k = nt(jnp.concatenate(grads[u], axis=1), near) * scale
            grad_v = nt(jnp.concatenate([s.p[j, h] for h in range(H)], axis=1), far)
            grad_q = tn(jnp.concatenate(grads[u], axis=0), spaced(s.knat[j], H))[0:T] * scale
            mixes.append(jnp.concatenate([v.astype(bf16) for v in (grad_q, grad_k, grad_v)], axis=1))
        whole = s.gqkv[...]
        for u, j in enumerate(at):
            whole = whole + tn(mixes[u], s.xpad[j, 0:T])
        s.gqkv[...] = whole
        terms = nn(jnp.concatenate(mixes, axis=0), s.w2[...])
        for u, j in enumerate(at):
            s.tmp[u] = s.u[j] + terms[u * T : (u + 1) * T]
            for q in range(H):
                s.tsend[q, j] = s.tmp[u, q * share : (q + 1) * share, :].astype(bf16)
        pl.when(i == 0)(lambda: send_tokens(0))

        @pl.when(i == 1)
        def _():
            shares_done((s.ge1, s.ge1r), 7)
            s.ge2[...] = head_sum((s.ge1, s.ge1r)).reshape(B, z.re // B, 128)
            spread(lambda peer: s.ge2.at[peer], s.ge2r.at[me_b], 3)

        return carry

    def send_tokens(i):
        to = tg_o.at[pl.ds(me_h * n + i * GB, GB)]
        for j in range(1, H):
            to_head(s.tsend.at[head_peers[j], pl.ds(i * GB, GB)], to, 6, j).start()
        pltpu.make_async_copy(s.tsend.at[me_h, pl.ds(i * GB, GB)], to, s.loc.at[7]).start()

    lax.fori_loop(0, n // GB, back_attend, 0)

    for h in range(H):
        for half in range(D // 128):
            lanes = slice(half * 128, (half + 1) * 128)
            at = half * C
            s.gl1[h, at : at + KEY, :] = s.gqkv[h * KEY : (h + 1) * KEY, lanes].astype(bf16)
            s.gl1[h, at + KEY : at + 2 * KEY, :] = s.gqkv[KH + h * KEY : KH + (h + 1) * KEY, lanes].astype(bf16)
            s.gl1[h, at + 2 * KEY : at + C, :] = s.gqkv[2 * KH + h * VAL : 2 * KH + (h + 1) * VAL, lanes].astype(bf16)
        if z.rl > C * (D // 128):
            s.gl1[h, C * (D // 128) :, :] = jnp.zeros((z.rl - C * (D // 128), 128), bf16)
    shares((s.gl1, s.gl1r), 8)
    spread_done(s.ge2, s.ge2r, 3)
    s.ge3[me_b] = batch_sum(s.ge2[me_b], s.ge2r)
    spread(lambda peer: s.ge3.at[me_b], s.ge3.at[me_b], 4)

    slot = lax.broadcasted_iota(jnp.int32, (T, L), 1)
    d_row, d_col = grid_of(slot)
    picks = []
    for down_sign in (1, -1):
        for right_sign in (1, -1):
            r = rows_s + down_sign * d_row
            c = cols_s + right_sign * d_col
            good = (r >= 0) & (r < SIDE) & (c >= 0) & (c < SIDE) & (slot < length)
            if down_sign < 0:
                good = good & (d_row > 0)
            if right_sign < 0:
                good = good & (d_col > 0)
            picks.append((jnp.where(good, r * SIDE + c, 0), good))
    bias_rows = []
    for h in range(H):
        whole = s.dbias[h]
        high = whole.astype(bf16)
        rest = (whole - high.astype(f32)).astype(bf16)
        ordered = nn(high, s.onehot[...]) + nn(rest, s.onehot[...])
        line = jnp.zeros((T, L), f32)
        for index, good in picks:
            line = line + jnp.where(good, take(ordered[:, 0:128], ordered[:, 128:256], index), 0.0)
        bias_rows.append(total(line * s.rowmask[...]))
    start_sum(5, bias_rows)
    for i in range(1, n // GB):
        send_tokens(i)

    shares_done((s.gl1, s.gl1r), 8)
    s.gl2[...] = head_sum((s.gl1, s.gl1r)).reshape(B, z.rl // B, 128)
    spread(lambda peer: s.gl2.at[peer], s.gl2r.at[me_b], 5)
    for h, row in enumerate(finish_sum(5, L)):
        s.brow[h] = row
    spread_done(s.gl2, s.gl2r, 5)
    s.gl3[me_b] = batch_sum(s.gl2[me_b], s.gl2r)
    spread(lambda peer: s.gl3.at[me_b], s.gl3.at[me_b], 6)

    small_o[...] = jnp.zeros(small_o.shape, f32)
    small_o[0:1, :] = sum_gain_1
    small_o[1:2, :] = sum_shift_1
    small_o[2:3, :] = sum_gain_3
    small_o[3:4, :] = sum_shift_3
    small_o[4:5, 0:FH] = s.srow[0:1, own]
    small_o[5:6, 0:FH] = s.srow[1:2, own]
    small_o[6:7, :] = s.brow[me_h]

    spread_done(s.ge3, s.ge3, 4)
    early_o[...] = s.ge3[...].reshape(z.re, 128)
    spread_done(s.gl3, s.gl3, 6)
    late_o[...] = s.gl3[...].reshape(z.rl, 128)

    done(to_head(s.osend.at[some], out_o.at[pl.ds(0, n * (H - 1))], 5, 1))
    done(to_head(s.tsend.at[some], tg_o.at[pl.ds(0, n * (H - 1))], 6, 1))
    c_out.wait()
    pltpu.make_async_copy(s.tsend.at[me_h], tg_o.at[pl.ds(me_h * n, n)], s.loc.at[7]).wait()


def finish_kernel(z, out_i, tg_i, early, late, small, out, tg, qkv, bias, proj, g1, s1, up, g2, s2, down, g3, s3):
    at = lax.broadcasted_iota(jnp.int32, (128, 128), 0)
    to = lax.broadcasted_iota(jnp.int32, (128, 128), 1)
    turn = jnp.where(lax.bitwise_and(at, 7) * 16 + lax.shift_right_logical(at, 3) == to, 1.0, 0.0).astype(bf16)
    whole = z.share // 16 * 16
    for src, dst in ((out_i, out), (tg_i, tg)):
        for i in range(0, src.shape[0], 8):
            for k in range(0, whole, 16):
                rows = src[i : i + 8, k : k + 16, :].reshape(128, z.D)
                dst[k : k + 16, i : i + 8, :] = nn(turn, rows).reshape(16, 8, z.D)
            for k in range(whole, z.share):
                dst[k, i : i + 8, :] = src[i : i + 8, k, :].astype(f32)

    @pl.when(pl.program_id(0) == 0)
    def _():
        D, C, PH = z.D, z.C, z.D // z.H
        down[...] = early[0:D, :].T
        up[...] = early[D : 2 * D, :]
        for half in range(D // 128):
            lanes = slice(half * 128, (half + 1) * 128)
            proj[:, lanes] = early[2 * D + half * PH : 2 * D + (half + 1) * PH, :]
            qkv[0, :, lanes] = late[half * C : (half + 1) * C, :]
        g1[...] = small[0:1, :]
        s1[...] = small[1:2, :]
        g3[...] = small[2:3, :]
        s3[...] = small[3:4, :]
        g2[...] = small[4:5, 0 : z.F // z.H]
        s2[...] = small[5:6, 0 : z.F // z.H]
        bias[...] = small[6:7, 0 : z.length]


def on_device(H, B, tokens, image_count, token_place, qkv_weight, bias_table, proj_weight, attention_gain,
              attention_shift, up_weight, hidden_gain, hidden_shift, down_weight, output_gain, output_shift,
              cotangent):
    images, length, width = tokens.shape
    z = types.SimpleNamespace(
        n=images // H, T=round_up(length, 16), L=round_up(length, 128), D=width, F=up_weight.shape[1] * H,
        H=H, B=B, C=qkv_weight.shape[1], share=cotangent.shape[1], length=length)
    z.re = round_up(2 * z.D + z.D // H * (z.D // 128), 8 * max(B, 2))
    z.rl = round_up(z.C * (z.D // 128), 8 * max(B, 2))
    z.group = max(g for g in (1, 2, 3, 4) if z.n % g == 0)
    z.group_back = max(g for g in (1, 2, 3) if z.n % g == 0)
    z.direct = H == 4 and B <= 8
    z.sums = {}
    for k, r in enumerate((2 * z.D, 2 * z.F, 4 * z.D, 2 * z.F, 2 * z.D, H * z.L)):
        z.sums["sum%d" % k] = pltpu.VMEM((H * B if z.direct else H, r // 128, 128), f32)
        if not z.direct:
            z.sums["part%d" % (k % 2)] = pltpu.VMEM((B, 8, 128), f32)

    def bufs(s, k):
        first = getattr(s, "sum%d" % k)
        return first, None if z.direct else getattr(s, "part%d" % (k % 2)).at[:, 0 : first.shape[1]]

    z.bufs = bufs
    scratch = layout(z)
    hbm = pl.BlockSpec(memory_space=pl.ANY)
    vmem = pl.BlockSpec(memory_space=pltpu.VMEM)
    smem = pl.BlockSpec(memory_space=pltpu.SMEM)
    outs = pl.pallas_call(
        functools.partial(block_kernel, z, tuple(scratch)),
        out_shape=(
            jax.ShapeDtypeStruct((images, z.share, width), bf16),
            jax.ShapeDtypeStruct((images, z.share, width), bf16),
            jax.ShapeDtypeStruct((z.re, 128), f32),
            jax.ShapeDtypeStruct((z.rl, 128), f32),
            jax.ShapeDtypeStruct((8, width), f32),
        ),
        in_specs=[hbm, smem, vmem, hbm, vmem, hbm, vmem, vmem, hbm, vmem, vmem, hbm, vmem, vmem, hbm],
        out_specs=(hbm, hbm, vmem, vmem, vmem),
        scratch_shapes=list(scratch.values()),
        compiler_params=pltpu.CompilerParams(
            collective_id=0, has_side_effects=True, vmem_limit_bytes=127 * 512 * 1024
        ),
    )(
        tokens.transpose(1, 0, 2), image_count, token_place.reshape(1, -1), qkv_weight, bias_table, proj_weight,
        attention_gain.reshape(1, -1), attention_shift.reshape(1, -1), up_weight, hidden_gain.reshape(1, -1),
        hidden_shift.reshape(1, -1), down_weight, output_gain.reshape(1, -1), output_shift.reshape(1, -1),
        cotangent.transpose(1, 0, 2),
    )

    steps = 2
    block = pl.BlockSpec((images // steps, z.share, width), lambda i: (i, 0, 0))
    turned = pl.BlockSpec((z.share, images // steps, width), lambda i: (0, i, 0))

    def whole(*shape):
        return jax.ShapeDtypeStruct(shape, f32), pl.BlockSpec(shape, lambda i: (0,) * len(shape))

    fh = z.F // H
    small = [
        whole(1, z.C, width), whole(1, length), whole(width // H, width), whole(1, width), whole(1, width),
        whole(width, fh), whole(1, fh), whole(1, fh), whole(fh, width), whole(1, width), whole(1, width)]
    big = jax.ShapeDtypeStruct((z.share, images, width), f32)
    res = pl.pallas_call(
        functools.partial(finish_kernel, z),
        grid=(steps,),
        out_shape=[big, big] + [a for a, _ in small],
        in_specs=[block, block, whole(z.re, 128)[1], whole(z.rl, 128)[1], whole(8, width)[1]],
        out_specs=[turned, turned] + [b for _, b in small],
        compiler_params=pltpu.CompilerParams(vmem_limit_bytes=127 * 512 * 1024),
    )(*outs)
    res = [res[0].transpose(1, 0, 2), res[1].transpose(1, 0, 2), *res[2:]]
    for k in (5, 6, 8, 9, 11, 12):
        res[k] = res[k].reshape(-1)
    return tuple(res)


def solution(mesh):
    H, B = mesh.shape["head"], mesh.shape["batch"]
    placed = (
        P("batch", None, None),
        P("batch"),
        P(),
        P("head", None, None),
        P("head", None),
        P(),
        P(),
        P(),
        P(None, "head"),
        P("head"),
        P("head"),
        P("head", None),
        P(),
        P(),
        P("batch", "head", None),
    )
    return jax.shard_map(
        functools.partial(on_device, H, B),
        mesh=mesh,
        in_specs=placed,
        out_specs=(
            P("batch", "head", None),
            P("batch", "head", None),
            P("head", None, None),
            P("head", None),
            P("head", None),
            P(),
            P(),
            P(None, "head"),
            P("head"),
            P("head"),
            P("head", None),
            P(),
            P(),
        ),
        check_vma=False,
    )
```

```python
import functools
import types

import jax
import jax.numpy as jnp
from jax import lax
from jax.experimental import pallas as pl
from jax.experimental.pallas import tpu as pltpu
from jax.sharding import PartitionSpec as P

KEY = 32
VAL = 64
SIDE = 14
EPSILON = 1e-05
LOG2E = 1.4426950408889634
MESH = pl.DeviceIdType.MESH
f32 = jnp.float32
bf16 = jnp.bfloat16


def nn(left, right):
    return lax.dot_general(left, right, (((1,), (0,)), ((), ())), preferred_element_type=f32)


def nt(left, right):
    return lax.dot_general(left, right, (((1,), (1,)), ((), ())), preferred_element_type=f32)


def tn(left, right):
    return lax.dot_general(left, right, (((0,), (0,)), ((), ())), preferred_element_type=f32)


def among(block, at, total_rows):
    parts = []
    if at > 0:
        parts.append(jnp.zeros((at, block.shape[1]), block.dtype))
    parts.append(block)
    if at + block.shape[0] < total_rows:
        parts.append(jnp.zeros((total_rows - at - block.shape[0], block.shape[1]), block.dtype))
    return jnp.concatenate(parts, axis=0)


def spaced(value, heads):
    rows, columns = value.shape
    each = columns // heads
    lane = lax.broadcasted_iota(jnp.int32, (rows, columns), 1)
    return jnp.concatenate(
        [jnp.where((lane >= h * each) & (lane < (h + 1) * each), value, jnp.zeros_like(value)) for h in range(heads)],
        axis=0)


def round_up(value, step):
    return -(-value // step) * step


def sigmoid(value):
    return 0.5 * jnp.tanh(0.5 * value) + 0.5


def fold(value):
    rows, columns = value.shape
    return jnp.sum(value.reshape(rows // 8, 8, columns), axis=0)


def total(value):
    return jnp.sum(value, axis=0, keepdims=True)


def lookup(table, index):
    rows = index.shape[0]
    low = jnp.broadcast_to(table[:, 0:128], (rows, 128))
    high = jnp.broadcast_to(table[:, 128:256], (rows, 128))
    return take(low, high, index)


def take(low, high, index):
    parts = []
    for half in range(2):
        at = index[:, half * 128 : (half + 1) * 128]
        inside = lax.bitwise_and(at, 127)
        first = jnp.take_along_axis(low, inside, axis=1, mode="promise_in_bounds")
        second = jnp.take_along_axis(high, inside, axis=1, mode="promise_in_bounds")
        parts.append(jnp.where(at < 128, first, second))
    return jnp.concatenate(parts, axis=1)


def layout(z):
    n, T, L, D, F, H, B, C = z.n, z.T, z.L, z.D, z.F, z.H, z.B, z.C
    dma = pltpu.SemaphoreType.DMA
    vmem = pltpu.VMEM
    return {
        "xt": vmem((T, 16, D), bf16),
        "ct": vmem((T, 16, D), bf16),
        "cin": vmem((round_up(z.share, 4), H * n, D), bf16),
        "mix": vmem((n * 16, 256), bf16),
        "unmix": vmem((n * 16, n * 16), bf16),
        "deal": vmem((H * n * 4, H * n * 4), bf16),
        "qkvg": vmem((H, C, D), bf16),
        "downg": vmem((H, F // H, D), bf16),
        "smallg": vmem((H, 4, 128), f32),
        "w2": vmem((H * C, D), bf16),
        "upcat": vmem((D, F), bf16),
        "projw": vmem((D, D), bf16),
        "bias": vmem((H, T, L), f32),
        "dbias": vmem((H, T, L), f32),
        "rowmask": vmem((T, D), f32),
        "onehot": vmem((L, L), bf16),
        "xpad": vmem((n, L, D), bf16),
        "qt": vmem((n, H * KEY, L), bf16),
        "knat": vmem((n, T, H * KEY), bf16),
        "vnat": vmem((n, T, H * VAL), bf16),
        "tmp": vmem((z.group, T, D), f32),
        "p": vmem((n, H, T, L), bf16),
        "linv": vmem((n, H, 1, L), f32),
        "att": vmem((n, H * VAL, L), f32),
        "act": vmem((n, H * VAL, L), bf16),
        "proj": vmem((n, T, D), f32),
        "hid": vmem((n, T, F), f32),
        "slope": vmem((n, T, F), f32),
        "act2": vmem((n, T, F), bf16),
        "out": vmem((n, T, D), f32),
        "u": vmem((n, T, D), f32),
        "gproj": vmem((n, L, D), bf16),
        "osend": vmem((H, n, z.share, D), bf16),
        "tsend": vmem((H, n, z.share, D), bf16),
        "gdown": vmem((D, F), f32),
        "gup": vmem((D, F), f32),
        "gpr": vmem((D, D), f32),
        "gqkv": vmem((H * C, D), f32),
        "srow": vmem((2, F), f32),
        "brow": vmem((H, 1, L), f32),
        **z.sums,
        "cnt": vmem((B, 1, 128), f32),
        "ge1": vmem((H, z.re, 128), bf16),
        "ge1r": vmem((H, z.re, 128), bf16),
        "ge2": vmem((B, z.re // B, 128), f32),
        "ge2r": vmem((B, z.re // B, 128), f32),
        "ge3": vmem((B, z.re // B, 128), f32),
        "gl1": vmem((H, z.rl, 128), bf16),
        "gl1r": vmem((H, z.rl, 128), bf16),
        "gl2": vmem((B, z.rl // B, 128), f32),
        "gl2r": vmem((B, z.rl // B, 128), f32),
        "gl3": vmem((B, z.rl // B, 128), f32),
        "loc": dma((8,)),
        "hs": dma((9,)),
        "hr": dma((9,)),
        "ass": dma((12,)),
        "asr": dma((12,)),
        "bs": dma((7,)),
        "br": dma((7,)),
        "ready": pltpu.SemaphoreType.REGULAR,
    }


def block_kernel(z, names, *refs):
    (tokens, count, place, qkv_w, table, proj_w, gain_1, shift_1, up_w, gain_2, shift_2, down_w,
     gain_3, shift_3, cot, out_o, tg_o, early_o, late_o, small_o) = refs[:20]
    s = types.SimpleNamespace(**dict(zip(names, refs[20:], strict=True)))
    n, T, L, D, F, H, B, C = z.n, z.T, z.L, z.D, z.F, z.H, z.B, z.C
    share, length = z.share, z.length
    me_h = lax.axis_index("head")
    me_b = lax.axis_index("batch")

    def local(src, dst, k):
        copy = pltpu.make_async_copy(src, dst, s.loc.at[k])
        copy.start()
        return copy

    def to_head(src, dst, k, j):
        return pltpu.make_async_remote_copy(
            src_ref=src, dst_ref=dst, send_sem=s.hs.at[k], recv_sem=s.hr.at[k],
            device_id={"head": head_peers[j]}, device_id_type=MESH)

    def to_batch(src, dst, k, peer):
        return pltpu.make_async_remote_copy(
            src_ref=src, dst_ref=dst, send_sem=s.bs.at[k], recv_sem=s.br.at[k],
            device_id={"batch": peer}, device_id_type=MESH)

    head_peers = [lax.rem(me_h + j, H) for j in range(H)]
    core = lax.rem(me_b, 2)
    sibling = me_b + 1 - 2 * core

    def done(copies):
        copies.wait()

    def around(size, step):
        if size <= 8:
            for j in range(1, size):
                step(j)
        else:
            lax.fori_loop(1, size, lambda j, c: (step(j), c)[1], 0)

    FH = F // H
    PH = D // H
    own = pl.ds(pl.multiple_of(me_h * FH, FH), FH)
    qkv_32, up_32, down_32 = s.gqkv.at[0:C], s.gup.at[:, 0:FH], s.gdown.at[0:FH, 0:D]
    c_qkv = local(qkv_w.at[0], qkv_32, 0)
    c_up = local(up_w, up_32, 1)
    c_down = local(down_w, down_32, 2)
    def window(slot):
        return pl.multiple_of(slot * n // 8 * 8, 8)

    c_tok = local(tokens.at[:, pl.ds(window(me_h), 16)], s.xt.at[pl.ds(0, length)], 3)
    c_proj = local(proj_w, s.gpr, 4)
    c_cot = local(cot, s.cin.at[pl.ds(0, share)], 6)

    def everyone():
        pairs = [(a, b) for a in range(H) for b in range(B) if a or b]
        return sorted(pairs, key=lambda p: -(p[0] % 2 + p[0] // 2 + (2 if p[1] > 1 else p[1] / 4)))

    def at_offset(a, b):
        x, y = lax.rem(me_h, 2), lax.div(me_h, 2)
        other = (y + a // 2 - 2 * y * (a // 2)) * 2 + x + a % 2 - 2 * x * (a % 2)
        return {"head": other, "batch": lax.rem(me_b + b, B)}

    barrier = pltpu.get_barrier_semaphore()
    for j in range(1, H):
        pl.semaphore_signal(barrier, inc=1, device_id={"head": head_peers[j]}, device_id_type=MESH)

    def greet(semaphore):
        around(B, lambda j: pl.semaphore_signal(
            semaphore, inc=1, device_id={"batch": lax.rem(me_b + j, B)}, device_id_type=MESH))

    greet(barrier)
    targets = [at_offset(*pair) for pair in everyone()] if z.direct else []

    s.smallg[me_h] = jnp.concatenate(
        [gain_2[...], shift_2[...], table[:, 0:128], jnp.concatenate(
            [table[:, 128:length], jnp.zeros((1, 256 - length), f32)], axis=1)], axis=0)
    c_qkv.wait()
    s.qkvg[me_h] = qkv_32[...].astype(bf16)
    up_rows = pl.ds(pl.multiple_of(core * (D // 2), D // 2), D // 2)
    down_rows = pl.ds(pl.multiple_of(core * (FH // 2), FH // 2), FH // 2)
    c_up.wait()
    s.upcat[up_rows, own] = s.gup[up_rows, 0:FH].astype(bf16)
    c_down.wait()
    s.downg[me_h, down_rows] = s.gdown[down_rows, 0:D].astype(bf16)

    s.cnt[me_b] = jnp.full((1, 128), count[0]).astype(f32)
    pl.semaphore_wait(barrier, H - 1 + B - 1)

    shared = (s.qkvg.at[me_h], s.smallg.at[me_h], s.upcat.at[up_rows, own], s.downg.at[me_h, down_rows])
    for k in (1, 0, 2, 3):
        for j in range(1, H):
            to_head(shared[k], shared[k], k, j).start()
    greet(s.ready)

    around(B, lambda j: to_batch(s.cnt.at[me_b], s.cnt.at[me_b], 0, lax.rem(me_b + j, B)).start())
    row_at = lax.broadcasted_iota(jnp.int32, (L, L), 0)
    lane_at = lax.broadcasted_iota(jnp.int32, (L, L), 1)
    s.rowmask[...] = jnp.where(row_at < length, 1.0, 0.0)[0:T]
    place_lane = jnp.broadcast_to(
        jnp.concatenate([place[...].astype(f32), jnp.zeros((1, L - length), f32)], axis=1), (L, L))
    place_row = place_lane.T
    s.onehot[...] = jnp.where((place_row == lane_at.astype(f32)) & (row_at < length), 1.0, 0.0).astype(bf16)

    def grid_of(at):
        at = at.astype(jnp.int32)
        row = lax.shift_right_logical(at * 4682, 16)
        return row, at - row * SIDE

    rows_t, cols_t = grid_of(place_lane[0:T])
    rows_s, cols_s = grid_of(place_row[0:T])
    offsets = jnp.abs(rows_s - rows_t) * SIDE + jnp.abs(cols_s - cols_t)
    for h in range(H):
        s.dbias[h] = jnp.zeros((T, L), f32)
    s.gdown[...] = jnp.zeros(s.gdown.shape, f32)
    s.gup[...] = jnp.zeros(s.gup.shape, f32)
    s.gqkv[...] = jnp.zeros(s.gqkv.shape, f32)

    def valid_of(i):
        return jnp.where(me_h * n + i < count[0], 1.0, 0.0)

    c_proj.wait()
    s.projw[...] = s.gpr[...].astype(bf16)
    s.gpr[...] = jnp.zeros(s.gpr.shape, f32)
    line_at = lax.broadcasted_iota(jnp.int32, (n * 16, 256), 0)
    pick_at = lax.broadcasted_iota(jnp.int32, (n * 16, 256), 1)
    image_at = lax.shift_right_logical(line_at, 4)
    s.mix[...] = jnp.where(
        (lax.bitwise_and(line_at, 15) == lax.shift_right_logical(pick_at, 4))
        & (lax.bitwise_and(pick_at, 15) == image_at + (me_h * n - window(me_h)))
        & (image_at + me_h * n < count[0]),
        1.0, 0.0).astype(bf16)
    s.xt[length:T] = jnp.zeros((T - length, 16, D), bf16)
    s.u[:, T - 16 : T, :] = jnp.zeros((n, 16, D), f32)
    s.xpad[:, T:L, :] = jnp.zeros((n, L - T, D), bf16)
    s.gproj[:, T:L, :] = jnp.zeros((n, L - T, D), bf16)
    c_tok.wait()

    def enter_tokens(k, carry):
        at = pl.ds(pl.multiple_of(k * 16, 16), 16)
        s.xpad[:, at, :] = nn(s.mix[...], s.xt[at].reshape(256, D)).astype(bf16).reshape(n, 16, D)
        return carry

    lax.fori_loop(0, T // 16, enter_tokens, 0)


    blocks = -(-share * n // 16)
    step = n * 4 // 16

    def over(value, divisor):
        return lax.shift_right_logical(value * (65536 // divisor + 1), 16)

    def square(size):
        return (lax.broadcasted_iota(jnp.int32, (size, size), 0),
                lax.broadcasted_iota(jnp.int32, (size, size), 1))

    to, at = square(n * 16)
    image_to = lax.shift_right_logical(to, 4)
    s.unmix[...] = jnp.where(
        (at == lax.bitwise_and(to, 15) * n + image_to) & (image_to + me_h * n < count[0]), 1.0, 0.0).astype(bf16)
    to, at = square(H * n * 4)
    owner = over(to, n * 4)
    inside = to - owner * (n * 4)
    token_to = over(inside, n)
    s.deal[...] = jnp.where(
        at == token_to * (H * n) + owner * n + inside - token_to * n, 1.0, 0.0).astype(bf16)
    s.cin[share:] = jnp.zeros((s.cin.shape[0] - share, H * n, D), bf16)
    c_cot.wait()

    def deal(k, wide):
        dealt = nn(s.deal[...], s.cin[pl.ds(k * 4, 4)].reshape(H * n * 4, D)).astype(bf16)
        for h in range(H):
            piece = dealt[h * n * 4 : h * n * 4 + wide * 16].reshape(wide, 16, D)
            s.xt[pl.ds(h * blocks + k * step, wide)] = piece

    lax.fori_loop(0, share // 4, lambda k, c: (deal(k, step), c)[1], 0)
    if share % 4:
        deal(share // 4, blocks - share // 4 * step)
    own_blocks = pl.ds(me_h * blocks, blocks)
    c_own = local(s.xt.at[own_blocks], s.ct.at[own_blocks], 5)

    def enter_cotangent(q):
        first = q * blocks
        for k in range(share // 16):
            rows = s.ct[first + k * n : first + (k + 1) * n].reshape(n * 16, D)
            at = q * share + k * 16
            s.u[:, at : at + 16, :] = nn(s.unmix[...], rows).reshape(n, 16, D)
        rest = s.ct[first + share // 16 * n].astype(f32)
        for i in range(n):
            at = q * share + share // 16 * 16
            s.u[i, at : at + 1, :] = rest[i : i + 1] * valid_of(i)

    cuts = (0, blocks * 6 // 10, blocks)

    def send_cotangent(piece):
        low, high = cuts[piece], cuts[piece + 1]
        for j in range(1, H):
            to_head(s.xt.at[pl.ds(head_peers[j] * blocks + low, high - low)],
                    s.ct.at[pl.ds(me_h * blocks + low, high - low)], 4, j).start()

    send_cotangent(0)

    some = pl.ds(0, H - 1)
    done(to_head(s.smallg.at[some], s.smallg.at[some], 1, 1))
    for h in range(H):
        line = jnp.concatenate([s.smallg[h, 2:3, :], s.smallg[h, 3:4, :]], axis=1)
        s.bias[h] = jnp.where(row_at[0:T] < length, lookup(line, offsets) * LOG2E, -1e30)
    done(to_head(s.qkvg.at[some], s.qkvg.at[some], 0, 1))
    for h in range(H):
        s.w2[h * KEY : (h + 1) * KEY] = s.qkvg[h, 0:KEY]
        s.w2[(H + h) * KEY : (H + h + 1) * KEY] = s.qkvg[h, KEY : 2 * KEY]
        at = 2 * H * KEY + h * VAL
        s.w2[at : at + VAL] = s.qkvg[h, 2 * KEY : C]

    scale = KEY**-0.5
    KH, VH = H * KEY, H * VAL

    def attend(i, carry):
        first, second = carry
        at = [i * z.group + u for u in range(z.group)]
        mixed, scores = [], []
        for j in at:
            x = s.xpad[j]
            mixed.append(nt(s.w2[...], x).astype(bf16))
            s.qt[j] = mixed[-1][0:KH]
            natural = nt(x[0:T], s.w2[KH : H * C]).astype(bf16)
            s.knat[j] = natural[:, 0:KH]
            s.vnat[j] = natural[:, KH:]
            scores.append(natural[:, 0:KH])
        for u in range(z.group):
            scores[u] = nn(spaced(scores[u], H), mixed[u][0:KH])
        for h in range(H):
            for u, j in enumerate(at):
                logits = scores[u][h * T : (h + 1) * T] * (scale * LOG2E) + s.bias[h]
                raised = jnp.exp2(logits - jnp.max(logits, axis=0, keepdims=True))
                inverse = 1.0 / total(raised)
                s.linv[j, h] = inverse
                low = raised.astype(bf16)
                s.p[j, h] = low
                values = mixed[u][2 * KH + h * VAL : 2 * KH + (h + 1) * VAL, 0:T]
                attended = nn(values, low) * inverse
                s.att[j, h * VAL : (h + 1) * VAL] = attended
                s.act[j, h * VAL : (h + 1) * VAL] = (attended * sigmoid(attended)).astype(bf16)
        for j in at:
            projected = tn(s.act[j], s.projw[...])[0:T] * s.rowmask[...]
            s.proj[j] = projected
            first, second = first + fold(projected), second + fold(projected * projected)
        return first, second

    def zeros(width):
        return jnp.zeros((8, width), f32)

    def port(k, src, dst, device):
        return pltpu.make_async_remote_copy(
            src_ref=src, dst_ref=dst, send_sem=s.ass.at[k], recv_sem=s.asr.at[k],
            device_id=device, device_id_type=MESH)

    def sum_slots(buf, size):
        if size <= 32:
            whole = buf[0]
            for b in range(1, size):
                whole = whole + buf[b]
            return whole
        return lax.fori_loop(1, size, lambda b, c: c + buf[b], buf[0])

    def start_sum(k, rows):
        buf = z.bufs(s, k)[0]
        me = me_h * B + me_b if z.direct else me_h
        r = 0
        for row in rows:
            for c in range(row.shape[1] // 128):
                buf[me, r : r + 1, :] = row[:, c * 128 : (c + 1) * 128]
                r += 1
        for target in targets if z.direct else [{"head": p} for p in head_peers[1:]]:
            port(k, buf.at[me], buf.at[me], target).start()

    def finish_sum(k, width):
        others = z.bufs(s, k)[0].at[pl.ds(0, H * B - 1 if z.direct else H - 1)]
        done(port(k, others, others, {"head": head_peers[1]}))
        bufs = z.bufs(s, k)
        if z.direct:
            whole = sum_slots(bufs[0], H * B)
        else:
            bufs[1][me_b] = sum_slots(bufs[0], H)
            mine = bufs[1].at[me_b]
            around(B, lambda j: port(k + 6, mine, mine, {"batch": lax.rem(me_b + j, B)}).start())
            others = bufs[1].at[pl.ds(0, B - 1)]
            done(port(k + 6, others, others, {"batch": lax.rem(me_b + 1, B)}))
            whole = sum_slots(bufs[1], B)
        step = width // 128
        return [
            jnp.concatenate([whole[r + c : r + c + 1] for c in range(step)], axis=1)
            for r in range(0, whole.shape[0], step)
        ]

    first, second = lax.fori_loop(0, n // z.group, attend, (zeros(D), zeros(D)))
    pl.semaphore_wait(s.ready, B - 1)
    some_rows = pl.ds(0, D // 2)
    done(to_head(s.upcat.at[some_rows, pl.ds(0, FH * (H - 1))], s.upcat.at[some_rows, pl.ds(0, FH * (H - 1))], 2, 1))
    down_some = s.downg.at[some, pl.ds(0, FH // 2)]
    done(to_head(down_some, down_some, 3, 1))
    halves = (s.upcat.at[up_rows, :], s.downg.at[:, down_rows])
    for k in range(2):
        to_batch(halves[k], halves[k], k + 1, sibling).start()
    start_sum(0, [total(first), total(second)])
    send_cotangent(1)
    for k in range(2):
        to_batch(halves[k], halves[k], k + 1, sibling).wait()
    down = s.downg[...].reshape(F, D)
    gain_2w = jnp.concatenate([s.smallg[h, 0:1, :] for h in range(H)], axis=1)
    shift_2w = jnp.concatenate([s.smallg[h, 1:2, :] for h in range(H)], axis=1)
    others = s.cnt.at[pl.ds(0, B - 1)]
    done(to_batch(others, others, 0, sibling))
    seen_part = sum_slots(s.cnt, B) * float(length)
    seen_row = jnp.concatenate([seen_part] * (D // 128), axis=1)
    sums = finish_sum(0, D)
    seen_wide = jnp.concatenate([seen_row] * (F // D), axis=1)

    def moments(first, second, seen):
        mean = first / seen
        return mean, lax.rsqrt(second / seen - mean * mean + EPSILON)

    mean_1, inverse_1 = moments(sums[0], sums[1], seen_row)
    a_1 = gain_1[...] * inverse_1
    b_1 = shift_1[...] - mean_1 * a_1

    G = z.group
    GT = G * T

    def group(ref, i):
        return ref[pl.ds(i * G, G), 0:T].reshape(GT, ref.shape[2])

    def put(ref, i, value):
        ref[pl.ds(i * G, G), 0:T] = value.reshape(G, T, value.shape[1])

    def mask_of(i):
        return jnp.concatenate([s.rowmask[...] * valid_of(i * G + u) for u in range(G)], axis=0)

    def residual_of(i):
        return group(s.xpad, i).astype(f32) + (group(s.proj, i) * a_1 + b_1 * mask_of(i))

    def enter(i, carry):
        first, second = carry
        residual = residual_of(i).astype(bf16)
        hidden = nn(residual, s.upcat[...])
        put(s.hid, i, hidden)
        return first + fold(hidden), second + fold(hidden * hidden)

    first, second = lax.fori_loop(0, n // G, enter, (zeros(F), zeros(F)))
    start_sum(1, [total(first), total(second)])
    others = s.ct.at[pl.ds(0, blocks * (H - 1))]
    done(to_head(others, others, 4, 1))
    c_own.wait()
    for q in range(H):
        enter_cotangent(q)
    sums = finish_sum(1, F)
    mean_2, inverse_2 = moments(sums[0], sums[1], seen_wide)
    a_2 = gain_2w * inverse_2
    b_2 = shift_2w - mean_2 * a_2

    def leave(i, carry):
        one, two, three, four = carry
        shaped = group(s.hid, i) * a_2 + b_2
        gate = sigmoid(shaped)
        active = shaped * gate
        low = active.astype(bf16)
        put(s.act2, i, low)
        outgoing = nn(low, down)
        put(s.out, i, outgoing)
        upstream = group(s.u, i)
        masked = outgoing * mask_of(i)
        return (one + fold(masked), two + fold(masked * outgoing), three + fold(upstream),
                four + fold(upstream * outgoing))

    sums = lax.fori_loop(0, n // G, leave, (zeros(D), zeros(D), zeros(D), zeros(D)))
    start_sum(2, [total(v) for v in sums])

    def slope(i, carry):
        shaped = group(s.hid, i) * a_2 + b_2
        gate = sigmoid(shaped)
        put(s.slope, i, gate + shaped * gate * (1.0 - gate))
        return carry

    lax.fori_loop(0, n // G, slope, 0)
    sums = finish_sum(2, D)
    mean_3, inverse_3 = moments(sums[0], sums[1], seen_row)
    a_3 = gain_3[...] * inverse_3
    b_3 = shift_3[...] - mean_3 * a_3
    sum_shift_3 = sums[2]
    sum_gain_3 = inverse_3 * (sums[3] - mean_3 * sum_shift_3)

    def back(gain, mean, inverse, sum_shift, sum_gain, seen):
        scaled = gain * inverse
        slope = -scaled * inverse * (sum_gain / seen)
        return scaled, slope, -scaled * (sum_shift / seen) - slope * mean

    s_3, v_3, r_3 = back(gain_3[...], mean_3, inverse_3, sum_shift_3, sum_gain_3, seen_row)

    def back_leave(i, carry):
        one, two = carry
        grad = (group(s.u, i) * s_3 + (group(s.out, i) * v_3 + r_3) * mask_of(i)).astype(bf16)
        put(s.gproj, i, grad)
        shaped = nt(grad, down) * group(s.slope, i)
        put(s.slope, i, shaped)
        return one + fold(shaped), two + fold(shaped * group(s.hid, i))

    def down_gradient(i, carry):
        s.gdown[...] += tn(group(s.gproj, i), group(s.act2, i))
        return carry

    def output(i):
        s.tmp[...] = ((residual_of(i) + (group(s.out, i) * a_3 + b_3)) * mask_of(i)).reshape(G, T, D)
        for u in range(G):
            for q in range(H):
                s.osend[q, i * G + u] = s.tmp[u, q * share : (q + 1) * share, :].astype(bf16)

    def early(at, parts):
        for h, part in enumerate(parts):
            s.ge1[h, at : at + part.shape[0], :] = part.astype(bf16)

    def send_early(low, high):
        rows = pl.ds(low, high - low)
        for j in range(1, H):
            to_head(s.ge1.at[head_peers[j], rows], s.ge1r.at[me_h, rows], 7, j).start()

    def send_output(low, high):
        low, high = low * n // 12, high * n // 12
        if high > low:
            to = out_o.at[pl.ds(me_h * n + low, high - low)]
            for j in range(1, H):
                to_head(s.osend.at[head_peers[j], pl.ds(low, high - low)], to, 5, j).start()

    first, second = lax.fori_loop(0, n // G, back_leave, (zeros(F), zeros(F)))
    start_sum(3, [total(first), total(second)])
    output(0)
    send_output(0, 4)
    lax.fori_loop(0, n // G, down_gradient, 0)
    for i in range(1, n // G):
        output(i)
    early(0, [s.gdown[:, h * FH : (h + 1) * FH] for h in range(H)])
    sums = finish_sum(3, F)

    sum_shift_2 = sums[0]
    sum_gain_2 = inverse_2 * (sums[1] - mean_2 * sum_shift_2)
    s_2, v_2, r_2 = back(gain_2w, mean_2, inverse_2, sum_shift_2, sum_gain_2, seen_wide)
    s.srow[0:1, :] = sum_gain_2
    s.srow[1:2, :] = sum_shift_2

    def back_enter(i, carry):
        one, two = carry
        mask = jnp.concatenate([mask_of(i)] * (F // D), axis=1)
        grad = (group(s.slope, i) * s_2 + group(s.hid, i) * v_2 + r_2 * mask).astype(bf16)
        put(s.act2, i, grad)
        upstream = group(s.u, i) + nt(grad, s.upcat[...])
        put(s.u, i, upstream)
        return one + fold(upstream), two + fold(upstream * group(s.proj, i))

    first, second = lax.fori_loop(0, n // G, back_enter, (zeros(D), zeros(D)))
    start_sum(4, [total(first), total(second)])
    send_early(0, D)

    def up_gradient(i, carry):
        s.gup[...] += tn(residual_of(i).astype(bf16), group(s.act2, i))
        return carry

    lax.fori_loop(0, n // G, up_gradient, 0)
    early(D, [s.gup[:, h * FH : (h + 1) * FH] for h in range(H)])
    send_early(D, 2 * D)
    sums = finish_sum(4, D)
    c_out = local(s.osend.at[me_h], out_o.at[pl.ds(me_h * n, n)], 6)
    sum_shift_1 = sums[0]
    sum_gain_1 = inverse_1 * (sums[1] - mean_1 * sum_shift_1)
    s_1, v_1, r_1 = back(gain_1[...], mean_1, inverse_1, sum_shift_1, sum_gain_1, seen_row)

    def back_project(i, carry):
        grad = (group(s.u, i) * s_1 + group(s.proj, i) * v_1 + r_1 * mask_of(i)).astype(bf16)
        put(s.gproj, i, grad)
        whole = s.gpr[...]
        for u in range(G):
            whole = whole + nn(s.act[i * G + u], s.gproj[i * G + u])
        s.gpr[...] = whole
        return carry

    lax.fori_loop(0, n // G, back_project, 0)

    def shares(buffer, k):
        for j in range(1, H):
            to_head(buffer[0].at[head_peers[j]], buffer[1].at[me_h], k, j).start()

    def shares_done(buffer, k):
        done(to_head(buffer[0].at[some], buffer[1].at[some], k, 1))

    def head_sum(buffer):
        whole = buffer[0][me_h].astype(f32)
        for j in range(1, H):
            whole = whole + buffer[1][head_peers[j]].astype(f32)
        return whole

    def spread(src, dst, k):
        around(B, lambda j: to_batch(src(lax.rem(me_b + j, B)), dst, k, lax.rem(me_b + j, B)).start())

    def spread_done(src, dst, k):
        others = pl.ds(0, B - 1)
        done(to_batch(src.at[others], dst.at[others], k, sibling))

    def batch_sum(own, received):
        if B <= 8:
            whole = own
            for j in range(1, B):
                whole = whole + received[lax.rem(me_b + j, B)]
            return whole
        return lax.fori_loop(1, B, lambda j, c: c + received[lax.rem(me_b + j, B)], own)

    for half in range(D // 128):
        lanes = slice(half * 128, (half + 1) * 128)
        early(2 * D + half * PH, [s.gpr[h * PH : (h + 1) * PH, lanes] for h in range(H)])
    filled = 2 * D + D // 128 * PH
    if z.re > filled:
        s.ge1[:, filled:, :] = jnp.zeros((H, z.re - filled, 128), bf16)
    send_early(2 * D, z.re)
    send_output(4, 12)

    GB = z.group_back

    def back_attend(i, carry):
        at = [i * GB + u for u in range(GB)]
        lows, deltas, products = [], [], []
        for j in at:
            att = s.att[j]
            gate = sigmoid(att)
            active = att * gate
            gact = nt(s.projw[...], s.gproj[j]) * (gate + active * (1.0 - gate))
            low, delta = [], []
            for h in range(H):
                rows = slice(h * VAL, (h + 1) * VAL)
                grad = gact[rows] * s.linv[j, h]
                low.append(grad.astype(bf16))
                delta.append(total(grad * att[rows]))
            lows.append(low)
            deltas.append(delta)
            products.append(nn(spaced(s.vnat[j], H), jnp.concatenate(low, axis=0)))
        grads = [[] for _ in at]
        for h in range(H):
            whole = None
            for u, j in enumerate(at):
                gscores = s.p[j, h].astype(f32) * (products[u][h * T : (h + 1) * T] - deltas[u][h])
                whole = gscores if whole is None else whole + gscores
                grads[u].append(gscores.astype(bf16))
            s.dbias[h] += whole
        mixes = []
        for u, j in enumerate(at):
            queries = s.qt[j]
            near = jnp.concatenate(
                [among(queries[h * KEY : (h + 1) * KEY], h * KEY, KH) for h in range(H)], axis=1)
            far = jnp.concatenate([among(lows[u][h], h * VAL, VH) for h in range(H)], axis=1)
            grad_k = nt(jnp.concatenate(grads[u], axis=1), near) * scale
            grad_v = nt(jnp.concatenate([s.p[j, h] for h in range(H)], axis=1), far)
            grad_q = tn(jnp.concatenate(grads[u], axis=0), spaced(s.knat[j], H))[0:T] * scale
            mixes.append(jnp.concatenate([v.astype(bf16) for v in (grad_q, grad_k, grad_v)], axis=1))
        whole = s.gqkv[...]
        for u, j in enumerate(at):
            whole = whole + tn(mixes[u], s.xpad[j, 0:T])
        s.gqkv[...] = whole
        terms = nn(jnp.concatenate(mixes, axis=0), s.w2[...])
        for u, j in enumerate(at):
            s.tmp[u] = s.u[j] + terms[u * T : (u + 1) * T]
            for q in range(H):
                s.tsend[q, j] = s.tmp[u, q * share : (q + 1) * share, :].astype(bf16)
        pl.when(i == 0)(lambda: send_tokens(0))

        @pl.when(i == 1)
        def _():
            shares_done((s.ge1, s.ge1r), 7)
            s.ge2[...] = head_sum((s.ge1, s.ge1r)).reshape(B, z.re // B, 128)
            spread(lambda peer: s.ge2.at[peer], s.ge2r.at[me_b], 3)

        return carry

    def send_tokens(i):
        to = tg_o.at[pl.ds(me_h * n + i * GB, GB)]
        for j in range(1, H):
            to_head(s.tsend.at[head_peers[j], pl.ds(i * GB, GB)], to, 6, j).start()
        pltpu.make_async_copy(s.tsend.at[me_h, pl.ds(i * GB, GB)], to, s.loc.at[7]).start()

    lax.fori_loop(0, n // GB, back_attend, 0)

    for h in range(H):
        for half in range(D // 128):
            lanes = slice(half * 128, (half + 1) * 128)
            at = half * C
            s.gl1[h, at : at + KEY, :] = s.gqkv[h * KEY : (h + 1) * KEY, lanes].astype(bf16)
            s.gl1[h, at + KEY : at + 2 * KEY, :] = s.gqkv[KH + h * KEY : KH + (h + 1) * KEY, lanes].astype(bf16)
            s.gl1[h, at + 2 * KEY : at + C, :] = s.gqkv[2 * KH + h * VAL : 2 * KH + (h + 1) * VAL, lanes].astype(bf16)
        if z.rl > C * (D // 128):
            s.gl1[h, C * (D // 128) :, :] = jnp.zeros((z.rl - C * (D // 128), 128), bf16)
    shares((s.gl1, s.gl1r), 8)
    spread_done(s.ge2, s.ge2r, 3)
    s.ge3[me_b] = batch_sum(s.ge2[me_b], s.ge2r)
    spread(lambda peer: s.ge3.at[me_b], s.ge3.at[me_b], 4)

    slot = lax.broadcasted_iota(jnp.int32, (T, L), 1)
    d_row, d_col = grid_of(slot)
    picks = []
    for down_sign in (1, -1):
        for right_sign in (1, -1):
            r = rows_s + down_sign * d_row
            c = cols_s + right_sign * d_col
            good = (r >= 0) & (r < SIDE) & (c >= 0) & (c < SIDE) & (slot < length)
            if down_sign < 0:
                good = good & (d_row > 0)
            if right_sign < 0:
                good = good & (d_col > 0)
            picks.append((jnp.where(good, r * SIDE + c, 0), good))
    bias_rows = []
    for h in range(H):
        whole = s.dbias[h]
        high = whole.astype(bf16)
        rest = (whole - high.astype(f32)).astype(bf16)
        ordered = nn(high, s.onehot[...]) + nn(rest, s.onehot[...])
        line = jnp.zeros((T, L), f32)
        for index, good in picks:
            line = line + jnp.where(good, take(ordered[:, 0:128], ordered[:, 128:256], index), 0.0)
        bias_rows.append(total(line * s.rowmask[...]))
    start_sum(5, bias_rows)

    for i in range(1, n // GB):
        send_tokens(i)
    shares_done((s.gl1, s.gl1r), 8)
    s.gl2[...] = head_sum((s.gl1, s.gl1r)).reshape(B, z.rl // B, 128)
    spread(lambda peer: s.gl2.at[peer], s.gl2r.at[me_b], 5)
    for h, row in enumerate(finish_sum(5, L)):
        s.brow[h] = row
    spread_done(s.gl2, s.gl2r, 5)
    s.gl3[me_b] = batch_sum(s.gl2[me_b], s.gl2r)
    spread(lambda peer: s.gl3.at[me_b], s.gl3.at[me_b], 6)

    small_o[...] = jnp.zeros(small_o.shape, f32)
    small_o[0:1, :] = sum_gain_1
    small_o[1:2, :] = sum_shift_1
    small_o[2:3, :] = sum_gain_3
    small_o[3:4, :] = sum_shift_3
    small_o[4:5, 0:FH] = s.srow[0:1, own]
    small_o[5:6, 0:FH] = s.srow[1:2, own]
    small_o[6:7, :] = s.brow[me_h]

    spread_done(s.ge3, s.ge3, 4)
    early_o[...] = s.ge3[...].reshape(z.re, 128)
    spread_done(s.gl3, s.gl3, 6)
    late_o[...] = s.gl3[...].reshape(z.rl, 128)

    done(to_head(s.osend.at[some], out_o.at[pl.ds(0, n * (H - 1))], 5, 1))
    done(to_head(s.tsend.at[some], tg_o.at[pl.ds(0, n * (H - 1))], 6, 1))
    c_out.wait()
    pltpu.make_async_copy(s.tsend.at[me_h], tg_o.at[pl.ds(me_h * n, n)], s.loc.at[7]).wait()


def finish_kernel(z, out_i, tg_i, early, late, small, out, tg, qkv, bias, proj, g1, s1, up, g2, s2, down, g3, s3):
    at = lax.broadcasted_iota(jnp.int32, (128, 128), 0)
    to = lax.broadcasted_iota(jnp.int32, (128, 128), 1)
    turn = jnp.where(lax.bitwise_and(at, 7) * 16 + lax.shift_right_logical(at, 3) == to, 1.0, 0.0).astype(bf16)
    whole = z.share // 16 * 16
    for src, dst in ((out_i, out), (tg_i, tg)):
        for i in range(0, src.shape[0], 8):
            for k in range(0, whole, 16):
                rows = src[i : i + 8, k : k + 16, :].reshape(128, z.D)
                dst[k : k + 16, i : i + 8, :] = nn(turn, rows).reshape(16, 8, z.D)
            for k in range(whole, z.share):
                dst[k, i : i + 8, :] = src[i : i + 8, k, :].astype(f32)

    @pl.when(pl.program_id(0) == 0)
    def _():
        D, C, PH = z.D, z.C, z.D // z.H
        down[...] = early[0:D, :].T
        up[...] = early[D : 2 * D, :]
        for half in range(D // 128):
            lanes = slice(half * 128, (half + 1) * 128)
            proj[:, lanes] = early[2 * D + half * PH : 2 * D + (half + 1) * PH, :]
            qkv[0, :, lanes] = late[half * C : (half + 1) * C, :]
        g1[...] = small[0:1, :]
        s1[...] = small[1:2, :]
        g3[...] = small[2:3, :]
        s3[...] = small[3:4, :]
        g2[...] = small[4:5, 0 : z.F // z.H]
        s2[...] = small[5:6, 0 : z.F // z.H]
        bias[...] = small[6:7, 0 : z.length]


def on_device(H, B, tokens, image_count, token_place, qkv_weight, bias_table, proj_weight, attention_gain,
              attention_shift, up_weight, hidden_gain, hidden_shift, down_weight, output_gain, output_shift,
              cotangent):
    images, length, width = tokens.shape
    z = types.SimpleNamespace(
        n=images // H, T=round_up(length, 16), L=round_up(length, 128), D=width, F=up_weight.shape[1] * H,
        H=H, B=B, C=qkv_weight.shape[1], share=cotangent.shape[1], length=length)
    z.re = round_up(2 * z.D + z.D // H * (z.D // 128), 8 * max(B, 2))
    z.rl = round_up(z.C * (z.D // 128), 8 * max(B, 2))
    z.group = max(g for g in (1, 2, 3, 4) if z.n % g == 0)
    z.group_back = max(g for g in (1, 2, 3) if z.n % g == 0)
    z.direct = H == 4 and B <= 8
    z.sums = {}
    for k, r in enumerate((2 * z.D, 2 * z.F, 4 * z.D, 2 * z.F, 2 * z.D, H * z.L)):
        z.sums["sum%d" % k] = pltpu.VMEM((H * B if z.direct else H, r // 128, 128), f32)
        if not z.direct:
            z.sums["part%d" % (k % 2)] = pltpu.VMEM((B, 8, 128), f32)

    def bufs(s, k):
        first = getattr(s, "sum%d" % k)
        return first, None if z.direct else getattr(s, "part%d" % (k % 2)).at[:, 0 : first.shape[1]]

    z.bufs = bufs
    scratch = layout(z)
    hbm = pl.BlockSpec(memory_space=pl.ANY)
    vmem = pl.BlockSpec(memory_space=pltpu.VMEM)
    smem = pl.BlockSpec(memory_space=pltpu.SMEM)
    outs = pl.pallas_call(
        functools.partial(block_kernel, z, tuple(scratch)),
        out_shape=(
            jax.ShapeDtypeStruct((images, z.share, width), bf16),
            jax.ShapeDtypeStruct((images, z.share, width), bf16),
            jax.ShapeDtypeStruct((z.re, 128), f32),
            jax.ShapeDtypeStruct((z.rl, 128), f32),
            jax.ShapeDtypeStruct((8, width), f32),
        ),
        in_specs=[hbm, smem, vmem, hbm, vmem, hbm, vmem, vmem, hbm, vmem, vmem, hbm, vmem, vmem, hbm],
        out_specs=(hbm, hbm, vmem, vmem, vmem),
        scratch_shapes=list(scratch.values()),
        compiler_params=pltpu.CompilerParams(
            collective_id=0, has_side_effects=True, vmem_limit_bytes=127 * 512 * 1024
        ),
    )(
        tokens.transpose(1, 0, 2), image_count, token_place.reshape(1, -1), qkv_weight, bias_table, proj_weight,
        attention_gain.reshape(1, -1), attention_shift.reshape(1, -1), up_weight, hidden_gain.reshape(1, -1),
        hidden_shift.reshape(1, -1), down_weight, output_gain.reshape(1, -1), output_shift.reshape(1, -1),
        cotangent.transpose(1, 0, 2),
    )

    steps = 2
    block = pl.BlockSpec((images // steps, z.share, width), lambda i: (i, 0, 0))
    turned = pl.BlockSpec((z.share, images // steps, width), lambda i: (0, i, 0))

    def whole(*shape):
        return jax.ShapeDtypeStruct(shape, f32), pl.BlockSpec(shape, lambda i: (0,) * len(shape))

    fh = z.F // H
    small = [
        whole(1, z.C, width), whole(1, length), whole(width // H, width), whole(1, width), whole(1, width),
        whole(width, fh), whole(1, fh), whole(1, fh), whole(fh, width), whole(1, width), whole(1, width)]
    big = jax.ShapeDtypeStruct((z.share, images, width), f32)
    res = pl.pallas_call(
        functools.partial(finish_kernel, z),
        grid=(steps,),
        out_shape=[big, big] + [a for a, _ in small],
        in_specs=[block, block, whole(z.re, 128)[1], whole(z.rl, 128)[1], whole(8, width)[1]],
        out_specs=[turned, turned] + [b for _, b in small],
        compiler_params=pltpu.CompilerParams(vmem_limit_bytes=127 * 512 * 1024),
    )(*outs)
    res = [res[0].transpose(1, 0, 2), res[1].transpose(1, 0, 2), *res[2:]]
    for k in (5, 6, 8, 9, 11, 12):
        res[k] = res[k].reshape(-1)
    return tuple(res)


def solution(mesh):
    H, B = mesh.shape["head"], mesh.shape["batch"]
    placed = (
        P("batch", None, None),
        P("batch"),
        P(),
        P("head", None, None),
        P("head", None),
        P(),
        P(),
        P(),
        P(None, "head"),
        P("head"),
        P("head"),
        P("head", None),
        P(),
        P(),
        P("batch", "head", None),
    )
    return jax.shard_map(
        functools.partial(on_device, H, B),
        mesh=mesh,
        in_specs=placed,
        out_specs=(
            P("batch", "head", None),
            P("batch", "head", None),
            P("head", None, None),
            P("head", None),
            P("head", None),
            P(),
            P(),
            P(None, "head"),
            P("head"),
            P("head"),
            P("head", None),
            P(),
            P(),
        ),
        check_vma=False,
    )
```

```python
import functools
import types

import jax
import jax.numpy as jnp
from jax import lax
from jax.experimental import pallas as pl
from jax.experimental.pallas import tpu as pltpu
from jax.sharding import PartitionSpec as P

KEY = 32
VAL = 64
SIDE = 14
EPSILON = 1e-05
LOG2E = 1.4426950408889634
MESH = pl.DeviceIdType.MESH
f32 = jnp.float32
bf16 = jnp.bfloat16


def nn(left, right):
    return lax.dot_general(left, right, (((1,), (0,)), ((), ())), preferred_element_type=f32)


def nt(left, right):
    return lax.dot_general(left, right, (((1,), (1,)), ((), ())), preferred_element_type=f32)


def tn(left, right):
    return lax.dot_general(left, right, (((0,), (0,)), ((), ())), preferred_element_type=f32)


def among(block, at, total_rows):
    parts = []
    if at > 0:
        parts.append(jnp.zeros((at, block.shape[1]), block.dtype))
    parts.append(block)
    if at + block.shape[0] < total_rows:
        parts.append(jnp.zeros((total_rows - at - block.shape[0], block.shape[1]), block.dtype))
    return jnp.concatenate(parts, axis=0)


def spaced(value, heads):
    rows, columns = value.shape
    each = columns // heads
    lane = lax.broadcasted_iota(jnp.int32, (rows, columns), 1)
    return jnp.concatenate(
        [jnp.where((lane >= h * each) & (lane < (h + 1) * each), value, jnp.zeros_like(value)) for h in range(heads)],
        axis=0)


def round_up(value, step):
    return -(-value // step) * step


def sigmoid(value):
    return 0.5 * jnp.tanh(0.5 * value) + 0.5


def fold(value):
    rows, columns = value.shape
    return jnp.sum(value.reshape(rows // 8, 8, columns), axis=0)


def total(value):
    return jnp.sum(value, axis=0, keepdims=True)


def lookup(table, index):
    rows = index.shape[0]
    low = jnp.broadcast_to(table[:, 0:128], (rows, 128))
    high = jnp.broadcast_to(table[:, 128:256], (rows, 128))
    return take(low, high, index)


def take(low, high, index):
    parts = []
    for half in range(2):
        at = index[:, half * 128 : (half + 1) * 128]
        inside = lax.bitwise_and(at, 127)
        first = jnp.take_along_axis(low, inside, axis=1, mode="promise_in_bounds")
        second = jnp.take_along_axis(high, inside, axis=1, mode="promise_in_bounds")
        parts.append(jnp.where(at < 128, first, second))
    return jnp.concatenate(parts, axis=1)


def layout(z):
    n, T, L, D, F, H, B, C = z.n, z.T, z.L, z.D, z.F, z.H, z.B, z.C
    dma = pltpu.SemaphoreType.DMA
    vmem = pltpu.VMEM
    return {
        "xt": vmem((T, 16, D), bf16),
        "ct": vmem((T, 16, D), bf16),
        "cin": vmem((round_up(z.share, 4), H * n, D), bf16),
        "mix": vmem((n * 16, 256), bf16),
        "unmix": vmem((n * 16, n * 16), bf16),
        "deal": vmem((H * n * 4, H * n * 4), bf16),
        "qkvg": vmem((H, C, D), bf16),
        "downg": vmem((H, F // H, D), bf16),
        "smallg": vmem((H, 4, 128), f32),
        "w2": vmem((H * C, D), bf16),
        "upcat": vmem((D, F), bf16),
        "projw": vmem((D, D), bf16),
        "bias": vmem((H, T, L), f32),
        "dbias": vmem((H, T, L), f32),
        "rowmask": vmem((T, D), f32),
        "onehot": vmem((L, L), bf16),
        "xpad": vmem((n, L, D), bf16),
        "qt": vmem((n, H * KEY, L), bf16),
        "knat": vmem((n, T, H * KEY), bf16),
        "vnat": vmem((n, T, H * VAL), bf16),
        "tmp": vmem((z.group, T, D), f32),
        "p": vmem((n, H, T, L), bf16),
        "linv": vmem((n, H, 1, L), f32),
        "att": vmem((n, H * VAL, L), f32),
        "act": vmem((n, H * VAL, L), bf16),
        "proj": vmem((n, T, D), f32),
        "hid": vmem((n, T, F), f32),
        "slope": vmem((n, T, F), f32),
        "act2": vmem((n, T, F), bf16),
        "out": vmem((n, T, D), f32),
        "u": vmem((n, T, D), f32),
        "gproj": vmem((n, L, D), bf16),
        "osend": vmem((H, n, z.share, D), bf16),
        "tsend": vmem((H, n, z.share, D), bf16),
        "gdown": vmem((D, F), f32),
        "gup": vmem((D, F), f32),
        "gpr": vmem((D, D), f32),
        "gqkv": vmem((H * C, D), f32),
        "srow": vmem((2, F), f32),
        "brow": vmem((H, 1, L), f32),
        **z.sums,
        "cnt": vmem((B, 1, 128), f32),
        "ge1": vmem((H, z.re, 128), bf16),
        "ge1r": vmem((H, z.re, 128), bf16),
        "ge2": vmem((B, z.re // B, 128), f32),
        "ge2r": vmem((B, z.re // B, 128), f32),
        "ge3": vmem((B, z.re // B, 128), f32),
        "gl1": vmem((H, z.rl, 128), bf16),
        "gl1r": vmem((H, z.rl, 128), bf16),
        "gl2": vmem((B, z.rl // B, 128), f32),
        "gl2r": vmem((B, z.rl // B, 128), f32),
        "gl3": vmem((B, z.rl // B, 128), f32),
        **{"vector%d" % k: vmem((1, size), kind) for k, (size, kind) in enumerate(z.vectors)},
        "vec": dma((len(z.vectors),)),
        "loc": dma((8,)),
        "hs": dma((9,)),
        "hr": dma((9,)),
        "ass": dma((12,)),
        "asr": dma((12,)),
        "bs": dma((7,)),
        "br": dma((7,)),
        "ready": pltpu.SemaphoreType.REGULAR,
    }


def block_kernel(z, names, *refs):
    (tokens, count, place, qkv_w, table, proj_w, gain_1, shift_1, up_w, gain_2, shift_2, down_w,
     gain_3, shift_3, cot, out_o, tg_o, early_o, late_o, small_o) = refs[:20]
    s = types.SimpleNamespace(**dict(zip(names, refs[20:], strict=True)))
    n, T, L, D, F, H, B, C = z.n, z.T, z.L, z.D, z.F, z.H, z.B, z.C
    share, length = z.share, z.length
    me_h = lax.axis_index("head")
    me_b = lax.axis_index("batch")

    def local(src, dst, k):
        copy = pltpu.make_async_copy(src, dst, s.loc.at[k])
        copy.start()
        return copy

    def to_head(src, dst, k, j):
        return pltpu.make_async_remote_copy(
            src_ref=src, dst_ref=dst, send_sem=s.hs.at[k], recv_sem=s.hr.at[k],
            device_id={"head": head_peers[j]}, device_id_type=MESH)

    def to_batch(src, dst, k, peer):
        return pltpu.make_async_remote_copy(
            src_ref=src, dst_ref=dst, send_sem=s.bs.at[k], recv_sem=s.br.at[k],
            device_id={"batch": peer}, device_id_type=MESH)

    head_peers = [lax.rem(me_h + j, H) for j in range(H)]
    core = lax.rem(me_b, 2)
    sibling = me_b + 1 - 2 * core

    def done(copies):
        copies.wait()

    def around(size, step):
        if size <= 8:
            for j in range(1, size):
                step(j)
        else:
            lax.fori_loop(1, size, lambda j, c: (step(j), c)[1], 0)

    vectors = (place, table, gain_1, shift_1, gain_2, shift_2, gain_3, shift_3)
    kept = [getattr(s, "vector%d" % k) for k in range(len(vectors))]
    fetched = [pltpu.make_async_copy(src, dst, s.vec.at[k]) for k, (src, dst) in enumerate(zip(vectors, kept))]
    for copy in fetched:
        copy.start()
    place, table, gain_1, shift_1, gain_2, shift_2, gain_3, shift_3 = kept

    FH = F // H
    PH = D // H
    own = pl.ds(pl.multiple_of(me_h * FH, FH), FH)
    qkv_32, up_32, down_32 = s.gqkv.at[0:C], s.gup.at[:, 0:FH], s.gdown.at[0:FH, 0:D]
    c_qkv = local(qkv_w.at[0], qkv_32, 0)
    c_up = local(up_w, up_32, 1)
    c_down = local(down_w, down_32, 2)
    def window(slot):
        return pl.multiple_of(slot * n // 8 * 8, 8)

    c_tok = local(tokens.at[:, pl.ds(window(me_h), 16)], s.xt.at[pl.ds(0, length)], 3)
    c_proj = local(proj_w, s.gpr, 4)
    c_cot = local(cot, s.cin.at[pl.ds(0, share)], 6)

    def everyone():
        pairs = [(a, b) for a in range(H) for b in range(B) if a or b]
        return sorted(pairs, key=lambda p: -(p[0] % 2 + p[0] // 2 + (2 if p[1] > 1 else p[1] / 4)))

    def at_offset(a, b):
        x, y = lax.rem(me_h, 2), lax.div(me_h, 2)
        other = (y + a // 2 - 2 * y * (a // 2)) * 2 + x + a % 2 - 2 * x * (a % 2)
        return {"head": other, "batch": lax.rem(me_b + b, B)}

    barrier = pltpu.get_barrier_semaphore()
    def greet(semaphore):
        around(B, lambda j: pl.semaphore_signal(
            semaphore, inc=1, device_id={"batch": lax.rem(me_b + j, B)}, device_id_type=MESH))

    greet(barrier)
    for j in range(1, H):
        pl.semaphore_signal(barrier, inc=1, device_id={"head": head_peers[j]}, device_id_type=MESH)
    targets = [at_offset(*pair) for pair in everyone()] if z.direct else []

    for copy in fetched:
        copy.wait()
    s.smallg[me_h] = jnp.concatenate(
        [gain_2[...], shift_2[...], table[:, 0:128], jnp.concatenate(
            [table[:, 128:length], jnp.zeros((1, 256 - length), f32)], axis=1)], axis=0)
    c_qkv.wait()
    s.qkvg[me_h] = qkv_32[...].astype(bf16)
    up_rows = pl.ds(pl.multiple_of(core * (D // 2), D // 2), D // 2)
    down_rows = pl.ds(pl.multiple_of(core * (FH // 2), FH // 2), FH // 2)
    c_up.wait()
    s.upcat[up_rows, own] = s.gup[up_rows, 0:FH].astype(bf16)
    c_down.wait()
    s.downg[me_h, down_rows] = s.gdown[down_rows, 0:D].astype(bf16)

    s.cnt[me_b] = jnp.full((1, 128), count[0]).astype(f32)
    pl.semaphore_wait(barrier, H - 1 + B - 1)

    shared = (s.qkvg.at[me_h], s.smallg.at[me_h], s.upcat.at[up_rows, own], s.downg.at[me_h, down_rows])
    for k in (1, 0, 2, 3):
        for j in range(1, H):
            to_head(shared[k], shared[k], k, j).start()
    greet(s.ready)

    around(B, lambda j: to_batch(s.cnt.at[me_b], s.cnt.at[me_b], 0, lax.rem(me_b + j, B)).start())
    row_at = lax.broadcasted_iota(jnp.int32, (L, L), 0)
    lane_at = lax.broadcasted_iota(jnp.int32, (L, L), 1)
    s.rowmask[...] = jnp.where(row_at < length, 1.0, 0.0)[0:T]
    place_lane = jnp.broadcast_to(
        jnp.concatenate([place[...].astype(f32), jnp.zeros((1, L - length), f32)], axis=1), (L, L))
    place_row = place_lane.T
    s.onehot[...] = jnp.where((place_row == lane_at.astype(f32)) & (row_at < length), 1.0, 0.0).astype(bf16)

    def grid_of(at):
        at = at.astype(jnp.int32)
        row = lax.shift_right_logical(at * 4682, 16)
        return row, at - row * SIDE

    rows_t, cols_t = grid_of(place_lane[0:T])
    rows_s, cols_s = grid_of(place_row[0:T])
    offsets = jnp.abs(rows_s - rows_t) * SIDE + jnp.abs(cols_s - cols_t)
    for h in range(H):
        s.dbias[h] = jnp.zeros((T, L), f32)
    s.gdown[...] = jnp.zeros(s.gdown.shape, f32)
    s.gup[...] = jnp.zeros(s.gup.shape, f32)
    s.gqkv[...] = jnp.zeros(s.gqkv.shape, f32)

    def valid_of(i):
        return jnp.where(me_h * n + i < count[0], 1.0, 0.0)

    c_proj.wait()
    s.projw[...] = s.gpr[...].astype(bf16)
    s.gpr[...] = jnp.zeros(s.gpr.shape, f32)
    line_at = lax.broadcasted_iota(jnp.int32, (n * 16, 256), 0)
    pick_at = lax.broadcasted_iota(jnp.int32, (n * 16, 256), 1)
    image_at = lax.shift_right_logical(line_at, 4)
    s.mix[...] = jnp.where(
        (lax.bitwise_and(line_at, 15) == lax.shift_right_logical(pick_at, 4))
        & (lax.bitwise_and(pick_at, 15) == image_at + (me_h * n - window(me_h)))
        & (image_at + me_h * n < count[0]),
        1.0, 0.0).astype(bf16)
    s.xt[length:T] = jnp.zeros((T - length, 16, D), bf16)
    s.u[:, T - 16 : T, :] = jnp.zeros((n, 16, D), f32)
    s.xpad[:, T:L, :] = jnp.zeros((n, L - T, D), bf16)
    s.gproj[:, T:L, :] = jnp.zeros((n, L - T, D), bf16)
    c_tok.wait()

    def enter_tokens(k, carry):
        at = pl.ds(pl.multiple_of(k * 16, 16), 16)
        s.xpad[:, at, :] = nn(s.mix[...], s.xt[at].reshape(256, D)).astype(bf16).reshape(n, 16, D)
        return carry

    lax.fori_loop(0, T // 16, enter_tokens, 0)


    blocks = -(-share * n // 16)
    step = n * 4 // 16

    def over(value, divisor):
        return lax.shift_right_logical(value * (65536 // divisor + 1), 16)

    def square(size):
        return (lax.broadcasted_iota(jnp.int32, (size, size), 0),
                lax.broadcasted_iota(jnp.int32, (size, size), 1))

    to, at = square(n * 16)
    image_to = lax.shift_right_logical(to, 4)
    s.unmix[...] = jnp.where(
        (at == lax.bitwise_and(to, 15) * n + image_to) & (image_to + me_h * n < count[0]), 1.0, 0.0).astype(bf16)
    to, at = square(H * n * 4)
    owner = over(to, n * 4)
    inside = to - owner * (n * 4)
    token_to = over(inside, n)
    s.deal[...] = jnp.where(
        at == token_to * (H * n) + owner * n + inside - token_to * n, 1.0, 0.0).astype(bf16)
    s.cin[share:] = jnp.zeros((s.cin.shape[0] - share, H * n, D), bf16)
    c_cot.wait()

    def deal(k, wide):
        dealt = nn(s.deal[...], s.cin[pl.ds(k * 4, 4)].reshape(H * n * 4, D)).astype(bf16)
        for h in range(H):
            piece = dealt[h * n * 4 : h * n * 4 + wide * 16].reshape(wide, 16, D)
            s.xt[pl.ds(h * blocks + k * step, wide)] = piece

    lax.fori_loop(0, share // 4, lambda k, c: (deal(k, step), c)[1], 0)
    if share % 4:
        deal(share // 4, blocks - share // 4 * step)
    own_blocks = pl.ds(me_h * blocks, blocks)
    c_own = local(s.xt.at[own_blocks], s.ct.at[own_blocks], 5)

    def enter_cotangent(q):
        first = q * blocks
        for k in range(share // 16):
            rows = s.ct[first + k * n : first + (k + 1) * n].reshape(n * 16, D)
            at = q * share + k * 16
            s.u[:, at : at + 16, :] = nn(s.unmix[...], rows).reshape(n, 16, D)
        rest = s.ct[first + share // 16 * n].astype(f32)
        for i in range(n):
            at = q * share + share // 16 * 16
            s.u[i, at : at + 1, :] = rest[i : i + 1] * valid_of(i)

    cuts = (0, blocks * 6 // 10, blocks)

    def send_cotangent(piece):
        low, high = cuts[piece], cuts[piece + 1]
        for j in range(1, H):
            to_head(s.xt.at[pl.ds(head_peers[j] * blocks + low, high - low)],
                    s.ct.at[pl.ds(me_h * blocks + low, high - low)], 4, j).start()

    send_cotangent(0)

    some = pl.ds(0, H - 1)
    done(to_head(s.smallg.at[some], s.smallg.at[some], 1, 1))
    for h in range(H):
        line = jnp.concatenate([s.smallg[h, 2:3, :], s.smallg[h, 3:4, :]], axis=1)
        s.bias[h] = jnp.where(row_at[0:T] < length, lookup(line, offsets) * LOG2E, -1e30)
    done(to_head(s.qkvg.at[some], s.qkvg.at[some], 0, 1))
    for h in range(H):
        s.w2[h * KEY : (h + 1) * KEY] = s.qkvg[h, 0:KEY]
        s.w2[(H + h) * KEY : (H + h + 1) * KEY] = s.qkvg[h, KEY : 2 * KEY]
        at = 2 * H * KEY + h * VAL
        s.w2[at : at + VAL] = s.qkvg[h, 2 * KEY : C]

    scale = KEY**-0.5
    KH, VH = H * KEY, H * VAL

    def attend(i, carry):
        first, second = carry
        at = [i * z.group + u for u in range(z.group)]
        mixed, scores = [], []
        for j in at:
            x = s.xpad[j]
            mixed.append(nt(s.w2[...], x).astype(bf16))
            s.qt[j] = mixed[-1][0:KH]
            natural = nt(x[0:T], s.w2[KH : H * C]).astype(bf16)
            s.knat[j] = natural[:, 0:KH]
            s.vnat[j] = natural[:, KH:]
            scores.append(natural[:, 0:KH])
        for u in range(z.group):
            scores[u] = nn(spaced(scores[u], H), mixed[u][0:KH])
        for h in range(H):
            for u, j in enumerate(at):
                logits = scores[u][h * T : (h + 1) * T] * (scale * LOG2E) + s.bias[h]
                raised = jnp.exp2(logits - jnp.max(logits, axis=0, keepdims=True))
                inverse = 1.0 / total(raised)
                s.linv[j, h] = inverse
                low = raised.astype(bf16)
                s.p[j, h] = low
                values = mixed[u][2 * KH + h * VAL : 2 * KH + (h + 1) * VAL, 0:T]
                attended = nn(values, low) * inverse
                s.att[j, h * VAL : (h + 1) * VAL] = attended
                s.act[j, h * VAL : (h + 1) * VAL] = (attended * sigmoid(attended)).astype(bf16)
        for j in at:
            projected = tn(s.act[j], s.projw[...])[0:T] * s.rowmask[...]
            s.proj[j] = projected
            first, second = first + fold(projected), second + fold(projected * projected)
        return first, second

    def zeros(width):
        return jnp.zeros((8, width), f32)

    def port(k, src, dst, device):
        return pltpu.make_async_remote_copy(
            src_ref=src, dst_ref=dst, send_sem=s.ass.at[k], recv_sem=s.asr.at[k],
            device_id=device, device_id_type=MESH)

    def sum_slots(buf, size):
        if size <= 32:
            whole = buf[0]
            for b in range(1, size):
                whole = whole + buf[b]
            return whole
        return lax.fori_loop(1, size, lambda b, c: c + buf[b], buf[0])

    def start_sum(k, rows):
        buf = z.bufs(s, k)[0]
        me = me_h * B + me_b if z.direct else me_h
        r = 0
        for row in rows:
            for c in range(row.shape[1] // 128):
                buf[me, r : r + 1, :] = row[:, c * 128 : (c + 1) * 128]
                r += 1
        for target in targets if z.direct else [{"head": p} for p in head_peers[1:]]:
            port(k, buf.at[me], buf.at[me], target).start()

    def finish_sum(k, width):
        others = z.bufs(s, k)[0].at[pl.ds(0, H * B - 1 if z.direct else H - 1)]
        done(port(k, others, others, {"head": head_peers[1]}))
        bufs = z.bufs(s, k)
        if z.direct:
            whole = sum_slots(bufs[0], H * B)
        else:
            bufs[1][me_b] = sum_slots(bufs[0], H)
            mine = bufs[1].at[me_b]
            around(B, lambda j: port(k + 6, mine, mine, {"batch": lax.rem(me_b + j, B)}).start())
            others = bufs[1].at[pl.ds(0, B - 1)]
            done(port(k + 6, others, others, {"batch": lax.rem(me_b + 1, B)}))
            whole = sum_slots(bufs[1], B)
        step = width // 128
        return [
            jnp.concatenate([whole[r + c : r + c + 1] for c in range(step)], axis=1)
            for r in range(0, whole.shape[0], step)
        ]

    first, second = lax.fori_loop(0, n // z.group, attend, (zeros(D), zeros(D)))
    pl.semaphore_wait(s.ready, B - 1)
    some_rows = pl.ds(0, D // 2)
    done(to_head(s.upcat.at[some_rows, pl.ds(0, FH * (H - 1))], s.upcat.at[some_rows, pl.ds(0, FH * (H - 1))], 2, 1))
    down_some = s.downg.at[some, pl.ds(0, FH // 2)]
    done(to_head(down_some, down_some, 3, 1))
    halves = (s.upcat.at[up_rows, :], s.downg.at[:, down_rows])
    for k in range(2):
        to_batch(halves[k], halves[k], k + 1, sibling).start()
    start_sum(0, [total(first), total(second)])
    send_cotangent(1)
    for k in range(2):
        to_batch(halves[k], halves[k], k + 1, sibling).wait()
    down = s.downg[...].reshape(F, D)
    gain_2w = jnp.concatenate([s.smallg[h, 0:1, :] for h in range(H)], axis=1)
    shift_2w = jnp.concatenate([s.smallg[h, 1:2, :] for h in range(H)], axis=1)
    others = s.cnt.at[pl.ds(0, B - 1)]
    done(to_batch(others, others, 0, sibling))
    seen_part = sum_slots(s.cnt, B) * float(length)
    seen_row = jnp.concatenate([seen_part] * (D // 128), axis=1)
    sums = finish_sum(0, D)
    seen_wide = jnp.concatenate([seen_row] * (F // D), axis=1)

    def moments(first, second, seen):
        mean = first / seen
        return mean, lax.rsqrt(second / seen - mean * mean + EPSILON)

    mean_1, inverse_1 = moments(sums[0], sums[1], seen_row)
    a_1 = gain_1[...] * inverse_1
    b_1 = shift_1[...] - mean_1 * a_1

    G = z.group
    GT = G * T

    def group(ref, i):
        return ref[pl.ds(i * G, G), 0:T].reshape(GT, ref.shape[2])

    def put(ref, i, value):
        ref[pl.ds(i * G, G), 0:T] = value.reshape(G, T, value.shape[1])

    def mask_of(i):
        return jnp.concatenate([s.rowmask[...] * valid_of(i * G + u) for u in range(G)], axis=0)

    def residual_of(i):
        return group(s.xpad, i).astype(f32) + (group(s.proj, i) * a_1 + b_1 * mask_of(i))

    def enter(i, carry):
        first, second = carry
        residual = residual_of(i).astype(bf16)
        hidden = nn(residual, s.upcat[...])
        put(s.hid, i, hidden)
        return first + fold(hidden), second + fold(hidden * hidden)

    first, second = lax.fori_loop(0, n // G, enter, (zeros(F), zeros(F)))
    start_sum(1, [total(first), total(second)])
    others = s.ct.at[pl.ds(0, blocks * (H - 1))]
    done(to_head(others, others, 4, 1))
    c_own.wait()
    for q in range(H):
        enter_cotangent(q)
    sums = finish_sum(1, F)
    mean_2, inverse_2 = moments(sums[0], sums[1], seen_wide)
    a_2 = gain_2w * inverse_2
    b_2 = shift_2w - mean_2 * a_2

    def leave(i, carry):
        one, two, three, four = carry
        shaped = group(s.hid, i) * a_2 + b_2
        gate = sigmoid(shaped)
        active = shaped * gate
        low = active.astype(bf16)
        put(s.act2, i, low)
        outgoing = nn(low, down)
        put(s.out, i, outgoing)
        upstream = group(s.u, i)
        masked = outgoing * mask_of(i)
        return (one + fold(masked), two + fold(masked * outgoing), three + fold(upstream),
                four + fold(upstream * outgoing))

    sums = lax.fori_loop(0, n // G, leave, (zeros(D), zeros(D), zeros(D), zeros(D)))
    start_sum(2, [total(v) for v in sums])

    def slope(i, carry):
        shaped = group(s.hid, i) * a_2 + b_2
        gate = sigmoid(shaped)
        put(s.slope, i, gate + shaped * gate * (1.0 - gate))
        return carry

    lax.fori_loop(0, n // G, slope, 0)
    sums = finish_sum(2, D)
    mean_3, inverse_3 = moments(sums[0], sums[1], seen_row)
    a_3 = gain_3[...] * inverse_3
    b_3 = shift_3[...] - mean_3 * a_3
    sum_shift_3 = sums[2]
    sum_gain_3 = inverse_3 * (sums[3] - mean_3 * sum_shift_3)

    def back(gain, mean, inverse, sum_shift, sum_gain, seen):
        scaled = gain * inverse
        slope = -scaled * inverse * (sum_gain / seen)
        return scaled, slope, -scaled * (sum_shift / seen) - slope * mean

    s_3, v_3, r_3 = back(gain_3[...], mean_3, inverse_3, sum_shift_3, sum_gain_3, seen_row)

    def back_leave(i, carry):
        one, two = carry
        grad = (group(s.u, i) * s_3 + (group(s.out, i) * v_3 + r_3) * mask_of(i)).astype(bf16)
        put(s.gproj, i, grad)
        shaped = nt(grad, down) * group(s.slope, i)
        put(s.slope, i, shaped)
        return one + fold(shaped), two + fold(shaped * group(s.hid, i))

    def down_gradient(i, carry):
        s.gdown[...] += tn(group(s.gproj, i), group(s.act2, i))
        return carry

    def output(i):
        s.tmp[...] = ((residual_of(i) + (group(s.out, i) * a_3 + b_3)) * mask_of(i)).reshape(G, T, D)
        for u in range(G):
            for q in range(H):
                s.osend[q, i * G + u] = s.tmp[u, q * share : (q + 1) * share, :].astype(bf16)

    def early(at, parts):
        for h, part in enumerate(parts):
            s.ge1[h, at : at + part.shape[0], :] = part.astype(bf16)

    def send_early(low, high):
        rows = pl.ds(low, high - low)
        for j in range(1, H):
            to_head(s.ge1.at[head_peers[j], rows], s.ge1r.at[me_h, rows], 7, j).start()

    def send_output(low, high):
        low, high = low * n // 12, high * n // 12
        if high > low:
            to = out_o.at[pl.ds(me_h * n + low, high - low)]
            for j in range(1, H):
                to_head(s.osend.at[head_peers[j], pl.ds(low, high - low)], to, 5, j).start()

    first, second = lax.fori_loop(0, n // G, back_leave, (zeros(F), zeros(F)))
    start_sum(3, [total(first), total(second)])
    output(0)
    send_output(0, 4)
    lax.fori_loop(0, n // G, down_gradient, 0)
    for i in range(1, n // G):
        output(i)
    early(0, [s.gdown[:, h * FH : (h + 1) * FH] for h in range(H)])
    sums = finish_sum(3, F)

    sum_shift_2 = sums[0]
    sum_gain_2 = inverse_2 * (sums[1] - mean_2 * sum_shift_2)
    s_2, v_2, r_2 = back(gain_2w, mean_2, inverse_2, sum_shift_2, sum_gain_2, seen_wide)
    s.srow[0:1, :] = sum_gain_2
    s.srow[1:2, :] = sum_shift_2

    def back_enter(i, carry):
        one, two = carry
        mask = jnp.concatenate([mask_of(i)] * (F // D), axis=1)
        grad = (group(s.slope, i) * s_2 + group(s.hid, i) * v_2 + r_2 * mask).astype(bf16)
        put(s.act2, i, grad)
        upstream = group(s.u, i) + nt(grad, s.upcat[...])
        put(s.u, i, upstream)
        return one + fold(upstream), two + fold(upstream * group(s.proj, i))

    first, second = lax.fori_loop(0, n // G, back_enter, (zeros(D), zeros(D)))
    start_sum(4, [total(first), total(second)])
    send_early(0, D)

    def up_gradient(i, carry):
        s.gup[...] += tn(residual_of(i).astype(bf16), group(s.act2, i))
        return carry

    lax.fori_loop(0, n // G, up_gradient, 0)
    early(D, [s.gup[:, h * FH : (h + 1) * FH] for h in range(H)])
    send_early(D, 2 * D)
    sums = finish_sum(4, D)
    c_out = local(s.osend.at[me_h], out_o.at[pl.ds(me_h * n, n)], 6)
    sum_shift_1 = sums[0]
    sum_gain_1 = inverse_1 * (sums[1] - mean_1 * sum_shift_1)
    s_1, v_1, r_1 = back(gain_1[...], mean_1, inverse_1, sum_shift_1, sum_gain_1, seen_row)

    def back_project(i, carry):
        grad = (group(s.u, i) * s_1 + group(s.proj, i) * v_1 + r_1 * mask_of(i)).astype(bf16)
        put(s.gproj, i, grad)
        whole = s.gpr[...]
        for u in range(G):
            whole = whole + nn(s.act[i * G + u], s.gproj[i * G + u])
        s.gpr[...] = whole
        return carry

    lax.fori_loop(0, n // G, back_project, 0)

    def shares(buffer, k):
        for j in range(1, H):
            to_head(buffer[0].at[head_peers[j]], buffer[1].at[me_h], k, j).start()

    def shares_done(buffer, k):
        done(to_head(buffer[0].at[some], buffer[1].at[some], k, 1))

    def head_sum(buffer):
        whole = buffer[0][me_h].astype(f32)
        for j in range(1, H):
            whole = whole + buffer[1][head_peers[j]].astype(f32)
        return whole

    def spread(src, dst, k):
        around(B, lambda j: to_batch(src(lax.rem(me_b + j, B)), dst, k, lax.rem(me_b + j, B)).start())

    def spread_done(src, dst, k):
        others = pl.ds(0, B - 1)
        done(to_batch(src.at[others], dst.at[others], k, sibling))

    def batch_sum(own, received):
        if B <= 8:
            whole = own
            for j in range(1, B):
                whole = whole + received[lax.rem(me_b + j, B)]
            return whole
        return lax.fori_loop(1, B, lambda j, c: c + received[lax.rem(me_b + j, B)], own)

    for half in range(D // 128):
        lanes = slice(half * 128, (half + 1) * 128)
        early(2 * D + half * PH, [s.gpr[h * PH : (h + 1) * PH, lanes] for h in range(H)])
    filled = 2 * D + D // 128 * PH
    if z.re > filled:
        s.ge1[:, filled:, :] = jnp.zeros((H, z.re - filled, 128), bf16)
    send_early(2 * D, z.re)
    send_output(4, 12)

    GB = z.group_back

    def back_attend(i, carry):
        at = [i * GB + u for u in range(GB)]
        lows, deltas, products = [], [], []
        for j in at:
            att = s.att[j]
            gate = sigmoid(att)
            active = att * gate
            gact = nt(s.projw[...], s.gproj[j]) * (gate + active * (1.0 - gate))
            low, delta = [], []
            for h in range(H):
                rows = slice(h * VAL, (h + 1) * VAL)
                grad = gact[rows] * s.linv[j, h]
                low.append(grad.astype(bf16))
                delta.append(total(grad * att[rows]))
            lows.append(low)
            deltas.append(delta)
            products.append(nn(spaced(s.vnat[j], H), jnp.concatenate(low, axis=0)))
        grads = [[] for _ in at]
        for h in range(H):
            whole = None
            for u, j in enumerate(at):
                gscores = s.p[j, h].astype(f32) * (products[u][h * T : (h + 1) * T] - deltas[u][h])
                whole = gscores if whole is None else whole + gscores
                grads[u].append(gscores.astype(bf16))
            s.dbias[h] += whole
        mixes = []
        for u, j in enumerate(at):
            queries = s.qt[j]
            near = jnp.concatenate(
                [among(queries[h * KEY : (h + 1) * KEY], h * KEY, KH) for h in range(H)], axis=1)
            far = jnp.concatenate([among(lows[u][h], h * VAL, VH) for h in range(H)], axis=1)
            grad_k = nt(jnp.concatenate(grads[u], axis=1), near) * scale
            grad_v = nt(jnp.concatenate([s.p[j, h] for h in range(H)], axis=1), far)
            grad_q = tn(jnp.concatenate(grads[u], axis=0), spaced(s.knat[j], H))[0:T] * scale
            mixes.append(jnp.concatenate([v.astype(bf16) for v in (grad_q, grad_k, grad_v)], axis=1))
        whole = s.gqkv[...]
        for u, j in enumerate(at):
            whole = whole + tn(mixes[u], s.xpad[j, 0:T])
        s.gqkv[...] = whole
        terms = nn(jnp.concatenate(mixes, axis=0), s.w2[...])
        for u, j in enumerate(at):
            s.tmp[u] = s.u[j] + terms[u * T : (u + 1) * T]
            for q in range(H):
                s.tsend[q, j] = s.tmp[u, q * share : (q + 1) * share, :].astype(bf16)
        pl.when(i == 0)(lambda: send_tokens(0))

        @pl.when(i == 1)
        def _():
            shares_done((s.ge1, s.ge1r), 7)
            s.ge2[...] = head_sum((s.ge1, s.ge1r)).reshape(B, z.re // B, 128)
            spread(lambda peer: s.ge2.at[peer], s.ge2r.at[me_b], 3)

        return carry

    def send_tokens(i):
        to = tg_o.at[pl.ds(me_h * n + i * GB, GB)]
        for j in range(1, H):
            to_head(s.tsend.at[head_peers[j], pl.ds(i * GB, GB)], to, 6, j).start()
        pltpu.make_async_copy(s.tsend.at[me_h, pl.ds(i * GB, GB)], to, s.loc.at[7]).start()

    lax.fori_loop(0, n // GB, back_attend, 0)

    for h in range(H):
        for half in range(D // 128):
            lanes = slice(half * 128, (half + 1) * 128)
            at = half * C
            s.gl1[h, at : at + KEY, :] = s.gqkv[h * KEY : (h + 1) * KEY, lanes].astype(bf16)
            s.gl1[h, at + KEY : at + 2 * KEY, :] = s.gqkv[KH + h * KEY : KH + (h + 1) * KEY, lanes].astype(bf16)
            s.gl1[h, at + 2 * KEY : at + C, :] = s.gqkv[2 * KH + h * VAL : 2 * KH + (h + 1) * VAL, lanes].astype(bf16)
        if z.rl > C * (D // 128):
            s.gl1[h, C * (D // 128) :, :] = jnp.zeros((z.rl - C * (D // 128), 128), bf16)
    shares((s.gl1, s.gl1r), 8)
    spread_done(s.ge2, s.ge2r, 3)
    s.ge3[me_b] = batch_sum(s.ge2[me_b], s.ge2r)
    spread(lambda peer: s.ge3.at[me_b], s.ge3.at[me_b], 4)

    slot = lax.broadcasted_iota(jnp.int32, (T, L), 1)
    d_row, d_col = grid_of(slot)
    picks = []
    for down_sign in (1, -1):
        for right_sign in (1, -1):
            r = rows_s + down_sign * d_row
            c = cols_s + right_sign * d_col
            good = (r >= 0) & (r < SIDE) & (c >= 0) & (c < SIDE) & (slot < length)
            if down_sign < 0:
                good = good & (d_row > 0)
            if right_sign < 0:
                good = good & (d_col > 0)
            picks.append((jnp.where(good, r * SIDE + c, 0), good))
    bias_rows = []
    for h in range(H):
        whole = s.dbias[h]
        high = whole.astype(bf16)
        rest = (whole - high.astype(f32)).astype(bf16)
        ordered = nn(high, s.onehot[...]) + nn(rest, s.onehot[...])
        line = jnp.zeros((T, L), f32)
        for index, good in picks:
            line = line + jnp.where(good, take(ordered[:, 0:128], ordered[:, 128:256], index), 0.0)
        bias_rows.append(total(line * s.rowmask[...]))
    start_sum(5, bias_rows)

    for i in range(1, n // GB):
        send_tokens(i)
    shares_done((s.gl1, s.gl1r), 8)
    s.gl2[...] = head_sum((s.gl1, s.gl1r)).reshape(B, z.rl // B, 128)
    spread(lambda peer: s.gl2.at[peer], s.gl2r.at[me_b], 5)
    for h, row in enumerate(finish_sum(5, L)):
        s.brow[h] = row
    spread_done(s.gl2, s.gl2r, 5)
    s.gl3[me_b] = batch_sum(s.gl2[me_b], s.gl2r)
    spread(lambda peer: s.gl3.at[me_b], s.gl3.at[me_b], 6)

    small_o[...] = jnp.zeros(small_o.shape, f32)
    small_o[0:1, :] = sum_gain_1
    small_o[1:2, :] = sum_shift_1
    small_o[2:3, :] = sum_gain_3
    small_o[3:4, :] = sum_shift_3
    small_o[4:5, 0:FH] = s.srow[0:1, own]
    small_o[5:6, 0:FH] = s.srow[1:2, own]
    small_o[6:7, :] = s.brow[me_h]

    spread_done(s.ge3, s.ge3, 4)
    early_o[...] = s.ge3[...].reshape(z.re, 128)
    spread_done(s.gl3, s.gl3, 6)
    late_o[...] = s.gl3[...].reshape(z.rl, 128)

    done(to_head(s.osend.at[some], out_o.at[pl.ds(0, n * (H - 1))], 5, 1))
    done(to_head(s.tsend.at[some], tg_o.at[pl.ds(0, n * (H - 1))], 6, 1))
    c_out.wait()
    pltpu.make_async_copy(s.tsend.at[me_h], tg_o.at[pl.ds(me_h * n, n)], s.loc.at[7]).wait()


def finish_kernel(z, out_i, tg_i, early, late, small, out, tg, qkv, bias, proj, g1, s1, up, g2, s2, down, g3, s3):
    at = lax.broadcasted_iota(jnp.int32, (128, 128), 0)
    to = lax.broadcasted_iota(jnp.int32, (128, 128), 1)
    turn = jnp.where(lax.bitwise_and(at, 7) * 16 + lax.shift_right_logical(at, 3) == to, 1.0, 0.0).astype(bf16)
    whole = z.share // 16 * 16
    for src, dst in ((out_i, out), (tg_i, tg)):
        for i in range(0, src.shape[0], 8):
            for k in range(0, whole, 16):
                rows = src[i : i + 8, k : k + 16, :].reshape(128, z.D)
                dst[k : k + 16, i : i + 8, :] = nn(turn, rows).reshape(16, 8, z.D)
            for k in range(whole, z.share):
                dst[k, i : i + 8, :] = src[i : i + 8, k, :].astype(f32)

    @pl.when(pl.program_id(0) == 0)
    def _():
        D, C, PH = z.D, z.C, z.D // z.H
        down[...] = early[0:D, :].T
        up[...] = early[D : 2 * D, :]
        for half in range(D // 128):
            lanes = slice(half * 128, (half + 1) * 128)
            proj[:, lanes] = early[2 * D + half * PH : 2 * D + (half + 1) * PH, :]
            qkv[0, :, lanes] = late[half * C : (half + 1) * C, :]
        g1[...] = small[0:1, :]
        s1[...] = small[1:2, :]
        g3[...] = small[2:3, :]
        s3[...] = small[3:4, :]
        g2[...] = small[4:5, 0 : z.F // z.H]
        s2[...] = small[5:6, 0 : z.F // z.H]
        bias[...] = small[6:7, 0 : z.length]


def on_device(H, B, tokens, image_count, token_place, qkv_weight, bias_table, proj_weight, attention_gain,
              attention_shift, up_weight, hidden_gain, hidden_shift, down_weight, output_gain, output_shift,
              cotangent):
    images, length, width = tokens.shape
    z = types.SimpleNamespace(
        n=images // H, T=round_up(length, 16), L=round_up(length, 128), D=width, F=up_weight.shape[1] * H,
        H=H, B=B, C=qkv_weight.shape[1], share=cotangent.shape[1], length=length)
    z.re = round_up(2 * z.D + z.D // H * (z.D // 128), 8 * max(B, 2))
    z.rl = round_up(z.C * (z.D // 128), 8 * max(B, 2))
    z.group = max(g for g in (1, 2, 3, 4) if z.n % g == 0)
    z.group_back = max(g for g in (1, 2, 3) if z.n % g == 0)
    z.direct = H == 4 and B <= 8
    z.sums = {}
    for k, r in enumerate((2 * z.D, 2 * z.F, 4 * z.D, 2 * z.F, 2 * z.D, H * z.L)):
        z.sums["sum%d" % k] = pltpu.VMEM((H * B if z.direct else H, r // 128, 128), f32)
        if not z.direct:
            z.sums["part%d" % (k % 2)] = pltpu.VMEM((B, 8, 128), f32)

    def bufs(s, k):
        first = getattr(s, "sum%d" % k)
        return first, None if z.direct else getattr(s, "part%d" % (k % 2)).at[:, 0 : first.shape[1]]

    z.bufs = bufs
    z.vectors = [(length, jnp.int32), (length, f32), (width, f32), (width, f32)]
    z.vectors += [(z.F // H, f32)] * 2 + [(width, f32)] * 2
    scratch = layout(z)
    hbm = pl.BlockSpec(memory_space=pl.ANY)
    vmem = pl.BlockSpec(memory_space=pltpu.VMEM)
    smem = pl.BlockSpec(memory_space=pltpu.SMEM)
    outs = pl.pallas_call(
        functools.partial(block_kernel, z, tuple(scratch)),
        out_shape=(
            jax.ShapeDtypeStruct((images, z.share, width), bf16),
            jax.ShapeDtypeStruct((images, z.share, width), bf16),
            jax.ShapeDtypeStruct((z.re, 128), f32),
            jax.ShapeDtypeStruct((z.rl, 128), f32),
            jax.ShapeDtypeStruct((8, width), f32),
        ),
        in_specs=[hbm, smem] + [hbm] * 13,
        out_specs=(hbm, hbm, vmem, vmem, vmem),
        scratch_shapes=list(scratch.values()),
        compiler_params=pltpu.CompilerParams(
            collective_id=0, has_side_effects=True, vmem_limit_bytes=127 * 512 * 1024
        ),
    )(
        tokens.transpose(1, 0, 2), image_count, token_place.reshape(1, -1), qkv_weight, bias_table, proj_weight,
        attention_gain.reshape(1, -1), attention_shift.reshape(1, -1), up_weight, hidden_gain.reshape(1, -1),
        hidden_shift.reshape(1, -1), down_weight, output_gain.reshape(1, -1), output_shift.reshape(1, -1),
        cotangent.transpose(1, 0, 2),
    )

    steps = 2
    block = pl.BlockSpec((images // steps, z.share, width), lambda i: (i, 0, 0))
    turned = pl.BlockSpec((z.share, images // steps, width), lambda i: (0, i, 0))

    def whole(*shape):
        return jax.ShapeDtypeStruct(shape, f32), pl.BlockSpec(shape, lambda i: (0,) * len(shape))

    fh = z.F // H
    small = [
        whole(1, z.C, width), whole(1, length), whole(width // H, width), whole(1, width), whole(1, width),
        whole(width, fh), whole(1, fh), whole(1, fh), whole(fh, width), whole(1, width), whole(1, width)]
    big = jax.ShapeDtypeStruct((z.share, images, width), f32)
    res = pl.pallas_call(
        functools.partial(finish_kernel, z),
        grid=(steps,),
        out_shape=[big, big] + [a for a, _ in small],
        in_specs=[block, block, whole(z.re, 128)[1], whole(z.rl, 128)[1], whole(8, width)[1]],
        out_specs=[turned, turned] + [b for _, b in small],
        compiler_params=pltpu.CompilerParams(vmem_limit_bytes=127 * 512 * 1024),
    )(*outs)
    res = [res[0].transpose(1, 0, 2), res[1].transpose(1, 0, 2), *res[2:]]
    for k in (5, 6, 8, 9, 11, 12):
        res[k] = res[k].reshape(-1)
    return tuple(res)


def solution(mesh):
    H, B = mesh.shape["head"], mesh.shape["batch"]
    placed = (
        P("batch", None, None),
        P("batch"),
        P(),
        P("head", None, None),
        P("head", None),
        P(),
        P(),
        P(),
        P(None, "head"),
        P("head"),
        P("head"),
        P("head", None),
        P(),
        P(),
        P("batch", "head", None),
    )
    return jax.shard_map(
        functools.partial(on_device, H, B),
        mesh=mesh,
        in_specs=placed,
        out_specs=(
            P("batch", "head", None),
            P("batch", "head", None),
            P("head", None, None),
            P("head", None),
            P("head", None),
            P(),
            P(),
            P(None, "head"),
            P("head"),
            P("head"),
            P("head", None),
            P(),
            P(),
        ),
        check_vma=False,
    )
```

```python
import functools
import types

import jax
import jax.numpy as jnp
from jax import lax
from jax.experimental import pallas as pl
from jax.experimental.pallas import tpu as pltpu
from jax.sharding import PartitionSpec as P

KEY = 32
VAL = 64
SIDE = 14
EPSILON = 1e-05
LOG2E = 1.4426950408889634
MESH = pl.DeviceIdType.MESH
f32 = jnp.float32
bf16 = jnp.bfloat16


def nn(left, right):
    return lax.dot_general(left, right, (((1,), (0,)), ((), ())), preferred_element_type=f32)


def nt(left, right):
    return lax.dot_general(left, right, (((1,), (1,)), ((), ())), preferred_element_type=f32)


def tn(left, right):
    return lax.dot_general(left, right, (((0,), (0,)), ((), ())), preferred_element_type=f32)


def among(block, at, total_rows):
    parts = []
    if at > 0:
        parts.append(jnp.zeros((at, block.shape[1]), block.dtype))
    parts.append(block)
    if at + block.shape[0] < total_rows:
        parts.append(jnp.zeros((total_rows - at - block.shape[0], block.shape[1]), block.dtype))
    return jnp.concatenate(parts, axis=0)


def spaced(value, heads):
    rows, columns = value.shape
    each = columns // heads
    lane = lax.broadcasted_iota(jnp.int32, (rows, columns), 1)
    return jnp.concatenate(
        [jnp.where((lane >= h * each) & (lane < (h + 1) * each), value, jnp.zeros_like(value)) for h in range(heads)],
        axis=0)


def round_up(value, step):
    return -(-value // step) * step


def sigmoid(value):
    return 0.5 * jnp.tanh(0.5 * value) + 0.5


def fold(value):
    rows, columns = value.shape
    return jnp.sum(value.reshape(rows // 8, 8, columns), axis=0)


def total(value):
    return jnp.sum(value, axis=0, keepdims=True)


def lookup(table, index):
    rows = index.shape[0]
    low = jnp.broadcast_to(table[:, 0:128], (rows, 128))
    high = jnp.broadcast_to(table[:, 128:256], (rows, 128))
    return take(low, high, index)


def take(low, high, index):
    parts = []
    for half in range(2):
        at = index[:, half * 128 : (half + 1) * 128]
        inside = lax.bitwise_and(at, 127)
        first = jnp.take_along_axis(low, inside, axis=1, mode="promise_in_bounds")
        second = jnp.take_along_axis(high, inside, axis=1, mode="promise_in_bounds")
        parts.append(jnp.where(at < 128, first, second))
    return jnp.concatenate(parts, axis=1)


def layout(z):
    n, T, L, D, F, H, B, C = z.n, z.T, z.L, z.D, z.F, z.H, z.B, z.C
    dma = pltpu.SemaphoreType.DMA
    vmem = pltpu.VMEM
    return {
        "xt": vmem((T, 16, D), bf16),
        "ct": vmem((T, 16, D), bf16),
        "cin": vmem((round_up(z.share, 4), H * n, D), bf16),
        "mix": vmem((n * 16, 256), bf16),
        "unmix": vmem((n * 16, n * 16), bf16),
        "deal": vmem((H * n * 4, H * n * 4), bf16),
        "qkvg": vmem((H, C, D), bf16),
        "downg": vmem((H, F // H, D), bf16),
        "smallg": vmem((H, 4, 128), f32),
        "w2": vmem((H * C, D), bf16),
        "upcat": vmem((D, F), bf16),
        "projw": vmem((D, D), bf16),
        "bias": vmem((H, T, L), f32),
        "dbias": vmem((H, T, L), f32),
        "rowmask": vmem((T, D), f32),
        "onehot": vmem((L, L), bf16),
        "xpad": vmem((n, L, D), bf16),
        "qt": vmem((n, H * KEY, L), bf16),
        "knat": vmem((n, T, H * KEY), bf16),
        "vnat": vmem((n, T, H * VAL), bf16),
        "tmp": vmem((z.group, T, D), f32),
        "p": vmem((n, H, T, L), bf16),
        "linv": vmem((n, H, 1, L), f32),
        "att": vmem((n, H * VAL, L), f32),
        "act": vmem((n, H * VAL, L), bf16),
        "proj": vmem((n, T, D), f32),
        "hid": vmem((n, T, F), f32),
        "slope": vmem((n, T, F), f32),
        "act2": vmem((n, T, F), bf16),
        "out": vmem((n, T, D), f32),
        "u": vmem((n, T, D), f32),
        "gproj": vmem((n, L, D), bf16),
        "osend": vmem((H, n, z.share, D), bf16),
        "tsend": vmem((H, n, z.share, D), bf16),
        "gdown": vmem((D, F), f32),
        "gup": vmem((D, F), f32),
        "gpr": vmem((D, D), f32),
        "gqkv": vmem((H * C, D), f32),
        "srow": vmem((2, F), f32),
        "brow": vmem((H, 1, L), f32),
        **z.sums,
        "cnt": vmem((B, 1, 128), f32),
        "ge1": vmem((H, z.re, 128), bf16),
        "ge1r": vmem((H, z.re, 128), bf16),
        "ge2": vmem((B, z.re // B, 128), f32),
        "ge2r": vmem((B, z.re // B, 128), f32),
        "ge3": vmem((B, z.re // B, 128), f32),
        "gl1": vmem((H, z.rl, 128), bf16),
        "gl1r": vmem((H, z.rl, 128), bf16),
        "gl2": vmem((B, z.rl // B, 128), f32),
        "gl2r": vmem((B, z.rl // B, 128), f32),
        "gl3": vmem((B, z.rl // B, 128), f32),
        **{"vector%d" % k: vmem((1, size), kind) for k, (size, kind) in enumerate(z.vectors)},
        "vec": dma((len(z.vectors),)),
        "loc": dma((8,)),
        "hs": dma((9,)),
        "hr": dma((9,)),
        "ass": dma((12,)),
        "asr": dma((12,)),
        "bs": dma((7,)),
        "br": dma((7,)),
        "ready": pltpu.SemaphoreType.REGULAR,
    }


def block_kernel(z, names, *refs):
    (tokens, count, place, qkv_w, table, proj_w, gain_1, shift_1, up_w, gain_2, shift_2, down_w,
     gain_3, shift_3, cot, out_o, tg_o, early_o, late_o, small_o) = refs[:20]
    s = types.SimpleNamespace(**dict(zip(names, refs[20:], strict=True)))
    n, T, L, D, F, H, B, C = z.n, z.T, z.L, z.D, z.F, z.H, z.B, z.C
    share, length = z.share, z.length
    me_h = lax.axis_index("head")
    me_b = lax.axis_index("batch")

    def local(src, dst, k):
        copy = pltpu.make_async_copy(src, dst, s.loc.at[k])
        copy.start()
        return copy

    def to_head(src, dst, k, j):
        return pltpu.make_async_remote_copy(
            src_ref=src, dst_ref=dst, send_sem=s.hs.at[k], recv_sem=s.hr.at[k],
            device_id={"head": head_peers[j]}, device_id_type=MESH)

    def to_batch(src, dst, k, peer):
        return pltpu.make_async_remote_copy(
            src_ref=src, dst_ref=dst, send_sem=s.bs.at[k], recv_sem=s.br.at[k],
            device_id={"batch": peer}, device_id_type=MESH)

    head_peers = [lax.rem(me_h + j, H) for j in range(H)]
    core = lax.rem(me_b, 2)
    sibling = me_b + 1 - 2 * core

    def done(copies):
        copies.wait()

    def around(size, step):
        if size <= 8:
            for j in range(1, size):
                step(j)
        else:
            lax.fori_loop(1, size, lambda j, c: (step(j), c)[1], 0)

    vectors = (place, table, gain_1, shift_1, gain_2, shift_2, gain_3, shift_3)
    kept = [getattr(s, "vector%d" % k) for k in range(len(vectors))]
    fetched = [pltpu.make_async_copy(src, dst, s.vec.at[k]) for k, (src, dst) in enumerate(zip(vectors, kept))]
    for copy in fetched:
        copy.start()
    place, table, gain_1, shift_1, gain_2, shift_2, gain_3, shift_3 = kept

    FH = F // H
    PH = D // H
    own = pl.ds(pl.multiple_of(me_h * FH, FH), FH)
    qkv_32, up_32, down_32 = s.gqkv.at[0:C], s.gup.at[:, 0:FH], s.gdown.at[0:FH, 0:D]
    c_qkv = local(qkv_w.at[0], qkv_32, 0)
    c_up = local(up_w, up_32, 1)
    c_down = local(down_w, down_32, 2)
    def window(slot):
        return pl.multiple_of(slot * n // 8 * 8, 8)

    c_tok = local(tokens.at[:, pl.ds(window(me_h), 16)], s.xt.at[pl.ds(0, length)], 3)
    c_proj = local(proj_w, s.gpr, 4)
    c_cot = local(cot, s.cin.at[pl.ds(0, share)], 6)

    def everyone():
        pairs = [(a, b) for a in range(H) for b in range(B) if a or b]
        return sorted(pairs, key=lambda p: -(p[0] % 2 + p[0] // 2 + (2 if p[1] > 1 else p[1] / 4)))

    def at_offset(a, b):
        x, y = lax.rem(me_h, 2), lax.div(me_h, 2)
        other = (y + a // 2 - 2 * y * (a // 2)) * 2 + x + a % 2 - 2 * x * (a % 2)
        return {"head": other, "batch": lax.rem(me_b + b, B)}

    barrier = pltpu.get_barrier_semaphore()
    def greet(semaphore):
        around(B, lambda j: pl.semaphore_signal(
            semaphore, inc=1, device_id={"batch": lax.rem(me_b + j, B)}, device_id_type=MESH))

    greet(barrier)
    for j in range(1, H):
        pl.semaphore_signal(barrier, inc=1, device_id={"head": head_peers[j]}, device_id_type=MESH)
    targets = [at_offset(*pair) for pair in everyone()] if z.direct else []

    for copy in fetched:
        copy.wait()
    s.smallg[me_h] = jnp.concatenate(
        [gain_2[...], shift_2[...], table[:, 0:128], jnp.concatenate(
            [table[:, 128:length], jnp.zeros((1, 256 - length), f32)], axis=1)], axis=0)
    c_qkv.wait()
    s.qkvg[me_h] = qkv_32[...].astype(bf16)
    up_rows = pl.ds(pl.multiple_of(core * (D // 2), D // 2), D // 2)
    down_rows = pl.ds(pl.multiple_of(core * (FH // 2), FH // 2), FH // 2)
    c_up.wait()
    s.upcat[up_rows, own] = s.gup[up_rows, 0:FH].astype(bf16)
    c_down.wait()
    s.downg[me_h, down_rows] = s.gdown[down_rows, 0:D].astype(bf16)

    s.cnt[me_b] = jnp.full((1, 128), count[0]).astype(f32)
    pl.semaphore_wait(barrier, H - 1 + B - 1)

    shared = (s.qkvg.at[me_h], s.smallg.at[me_h], s.upcat.at[up_rows, own], s.downg.at[me_h, down_rows])
    for k in (1, 0, 2, 3):
        for j in range(1, H):
            to_head(shared[k], shared[k], k, j).start()
    greet(s.ready)

    around(B, lambda j: to_batch(s.cnt.at[me_b], s.cnt.at[me_b], 0, lax.rem(me_b + j, B)).start())
    row_at = lax.broadcasted_iota(jnp.int32, (L, L), 0)
    lane_at = lax.broadcasted_iota(jnp.int32, (L, L), 1)
    s.rowmask[...] = jnp.where(row_at < length, 1.0, 0.0)[0:T]
    place_lane = jnp.broadcast_to(
        jnp.concatenate([place[...].astype(f32), jnp.zeros((1, L - length), f32)], axis=1), (L, L))
    place_row = place_lane.T
    s.onehot[...] = jnp.where((place_row == lane_at.astype(f32)) & (row_at < length), 1.0, 0.0).astype(bf16)

    def grid_of(at):
        at = at.astype(jnp.int32)
        row = lax.shift_right_logical(at * 4682, 16)
        return row, at - row * SIDE

    rows_t, cols_t = grid_of(place_lane[0:T])
    rows_s, cols_s = grid_of(place_row[0:T])
    offsets = jnp.abs(rows_s - rows_t) * SIDE + jnp.abs(cols_s - cols_t)
    for h in range(H):
        s.dbias[h] = jnp.zeros((T, L), f32)
    s.gdown[...] = jnp.zeros(s.gdown.shape, f32)
    s.gup[...] = jnp.zeros(s.gup.shape, f32)
    s.gqkv[...] = jnp.zeros(s.gqkv.shape, f32)

    def valid_of(i):
        return jnp.where(me_h * n + i < count[0], 1.0, 0.0)

    c_proj.wait()
    s.projw[...] = s.gpr[...].astype(bf16)
    s.gpr[...] = jnp.zeros(s.gpr.shape, f32)
    line_at = lax.broadcasted_iota(jnp.int32, (n * 16, 256), 0)
    pick_at = lax.broadcasted_iota(jnp.int32, (n * 16, 256), 1)
    image_at = lax.shift_right_logical(line_at, 4)
    s.mix[...] = jnp.where(
        (lax.bitwise_and(line_at, 15) == lax.shift_right_logical(pick_at, 4))
        & (lax.bitwise_and(pick_at, 15) == image_at + (me_h * n - window(me_h)))
        & (image_at + me_h * n < count[0]),
        1.0, 0.0).astype(bf16)
    s.xt[length:T] = jnp.zeros((T - length, 16, D), bf16)
    s.u[:, T - 16 : T, :] = jnp.zeros((n, 16, D), f32)
    s.xpad[:, T:L, :] = jnp.zeros((n, L - T, D), bf16)
    s.gproj[:, T:L, :] = jnp.zeros((n, L - T, D), bf16)
    c_tok.wait()

    def enter_tokens(k, carry):
        at = pl.ds(pl.multiple_of(k * 16, 16), 16)
        s.xpad[:, at, :] = nn(s.mix[...], s.xt[at].reshape(256, D)).astype(bf16).reshape(n, 16, D)
        return carry

    lax.fori_loop(0, T // 16, enter_tokens, 0)


    blocks = -(-share * n // 16)
    step = n * 4 // 16

    def over(value, divisor):
        return lax.shift_right_logical(value * (65536 // divisor + 1), 16)

    def square(size):
        return (lax.broadcasted_iota(jnp.int32, (size, size), 0),
                lax.broadcasted_iota(jnp.int32, (size, size), 1))

    to, at = square(n * 16)
    image_to = lax.shift_right_logical(to, 4)
    s.unmix[...] = jnp.where(
        (at == lax.bitwise_and(to, 15) * n + image_to) & (image_to + me_h * n < count[0]), 1.0, 0.0).astype(bf16)
    to, at = square(H * n * 4)
    owner = over(to, n * 4)
    inside = to - owner * (n * 4)
    token_to = over(inside, n)
    s.deal[...] = jnp.where(
        at == token_to * (H * n) + owner * n + inside - token_to * n, 1.0, 0.0).astype(bf16)
    s.cin[share:] = jnp.zeros((s.cin.shape[0] - share, H * n, D), bf16)
    c_cot.wait()

    def deal(k, wide):
        dealt = nn(s.deal[...], s.cin[pl.ds(k * 4, 4)].reshape(H * n * 4, D)).astype(bf16)
        for h in range(H):
            piece = dealt[h * n * 4 : h * n * 4 + wide * 16].reshape(wide, 16, D)
            s.xt[pl.ds(h * blocks + k * step, wide)] = piece

    lax.fori_loop(0, share // 4, lambda k, c: (deal(k, step), c)[1], 0)
    if share % 4:
        deal(share // 4, blocks - share // 4 * step)
    own_blocks = pl.ds(me_h * blocks, blocks)
    c_own = local(s.xt.at[own_blocks], s.ct.at[own_blocks], 5)

    def enter_cotangent(q):
        first = q * blocks
        for k in range(share // 16):
            rows = s.ct[first + k * n : first + (k + 1) * n].reshape(n * 16, D)
            at = q * share + k * 16
            s.u[:, at : at + 16, :] = nn(s.unmix[...], rows).reshape(n, 16, D)
        rest = s.ct[first + share // 16 * n].astype(f32)
        for i in range(n):
            at = q * share + share // 16 * 16
            s.u[i, at : at + 1, :] = rest[i : i + 1] * valid_of(i)

    cuts = (0, blocks * 6 // 10, blocks)

    def send_cotangent(piece):
        low, high = cuts[piece], cuts[piece + 1]
        for j in range(1, H):
            to_head(s.xt.at[pl.ds(head_peers[j] * blocks + low, high - low)],
                    s.ct.at[pl.ds(me_h * blocks + low, high - low)], 4, j).start()

    send_cotangent(0)

    some = pl.ds(0, H - 1)
    done(to_head(s.smallg.at[some], s.smallg.at[some], 1, 1))
    for h in range(H):
        line = jnp.concatenate([s.smallg[h, 2:3, :], s.smallg[h, 3:4, :]], axis=1)
        s.bias[h] = jnp.where(row_at[0:T] < length, lookup(line, offsets) * LOG2E, -1e30)
    done(to_head(s.qkvg.at[some], s.qkvg.at[some], 0, 1))
    for h in range(H):
        s.w2[h * KEY : (h + 1) * KEY] = s.qkvg[h, 0:KEY]
        s.w2[(H + h) * KEY : (H + h + 1) * KEY] = s.qkvg[h, KEY : 2 * KEY]
        at = 2 * H * KEY + h * VAL
        s.w2[at : at + VAL] = s.qkvg[h, 2 * KEY : C]

    scale = KEY**-0.5
    KH, VH = H * KEY, H * VAL

    def attend(i, carry):
        first, second = carry
        at = [i * z.group + u for u in range(z.group)]
        mixed, scores = [], []
        for j in at:
            x = s.xpad[j]
            mixed.append(nt(s.w2[...], x).astype(bf16))
            s.qt[j] = mixed[-1][0:KH]
            natural = nt(x[0:T], s.w2[KH : H * C]).astype(bf16)
            s.knat[j] = natural[:, 0:KH]
            s.vnat[j] = natural[:, KH:]
            scores.append(natural[:, 0:KH])
        for u in range(z.group):
            scores[u] = nn(spaced(scores[u], H), mixed[u][0:KH])
        for h in range(H):
            for u, j in enumerate(at):
                logits = scores[u][h * T : (h + 1) * T] * (scale * LOG2E) + s.bias[h]
                raised = jnp.exp2(logits - jnp.max(logits, axis=0, keepdims=True))
                inverse = 1.0 / total(raised)
                s.linv[j, h] = inverse
                low = raised.astype(bf16)
                s.p[j, h] = low
                values = mixed[u][2 * KH + h * VAL : 2 * KH + (h + 1) * VAL, 0:T]
                attended = nn(values, low) * inverse
                s.att[j, h * VAL : (h + 1) * VAL] = attended
                s.act[j, h * VAL : (h + 1) * VAL] = (attended * sigmoid(attended)).astype(bf16)
        for j in at:
            projected = tn(s.act[j], s.projw[...])[0:T] * s.rowmask[...]
            s.proj[j] = projected
            first, second = first + fold(projected), second + fold(projected * projected)
        return first, second

    def zeros(width):
        return jnp.zeros((8, width), f32)

    def port(k, src, dst, device):
        return pltpu.make_async_remote_copy(
            src_ref=src, dst_ref=dst, send_sem=s.ass.at[k], recv_sem=s.asr.at[k],
            device_id=device, device_id_type=MESH)

    def sum_slots(buf, size):
        if size <= 32:
            whole = buf[0]
            for b in range(1, size):
                whole = whole + buf[b]
            return whole
        return lax.fori_loop(1, size, lambda b, c: c + buf[b], buf[0])

    def start_sum(k, rows):
        buf = z.bufs(s, k)[0]
        me = me_h * B + me_b if z.direct else me_h
        r = 0
        for row in rows:
            for c in range(row.shape[1] // 128):
                buf[me, r : r + 1, :] = row[:, c * 128 : (c + 1) * 128]
                r += 1
        for target in targets if z.direct else [{"head": p} for p in head_peers[1:]]:
            port(k, buf.at[me], buf.at[me], target).start()

    def finish_sum(k, width):
        others = z.bufs(s, k)[0].at[pl.ds(0, H * B - 1 if z.direct else H - 1)]
        done(port(k, others, others, {"head": head_peers[1]}))
        bufs = z.bufs(s, k)
        if z.direct:
            whole = sum_slots(bufs[0], H * B)
        else:
            bufs[1][me_b] = sum_slots(bufs[0], H)
            mine = bufs[1].at[me_b]
            around(B, lambda j: port(k + 6, mine, mine, {"batch": lax.rem(me_b + j, B)}).start())
            others = bufs[1].at[pl.ds(0, B - 1)]
            done(port(k + 6, others, others, {"batch": lax.rem(me_b + 1, B)}))
            whole = sum_slots(bufs[1], B)
        step = width // 128
        return [
            jnp.concatenate([whole[r + c : r + c + 1] for c in range(step)], axis=1)
            for r in range(0, whole.shape[0], step)
        ]

    first, second = lax.fori_loop(0, n // z.group, attend, (zeros(D), zeros(D)))
    pl.semaphore_wait(s.ready, B - 1)
    start_sum(0, [total(first), total(second)])
    some_rows = pl.ds(0, D // 2)
    done(to_head(s.upcat.at[some_rows, pl.ds(0, FH * (H - 1))], s.upcat.at[some_rows, pl.ds(0, FH * (H - 1))], 2, 1))
    down_some = s.downg.at[some, pl.ds(0, FH // 2)]
    done(to_head(down_some, down_some, 3, 1))
    halves = (s.upcat.at[up_rows, :], s.downg.at[:, down_rows])
    for k in range(2):
        to_batch(halves[k], halves[k], k + 1, sibling).start()
    send_cotangent(1)
    for k in range(2):
        to_batch(halves[k], halves[k], k + 1, sibling).wait()
    down = s.downg[...].reshape(F, D)
    gain_2w = jnp.concatenate([s.smallg[h, 0:1, :] for h in range(H)], axis=1)
    shift_2w = jnp.concatenate([s.smallg[h, 1:2, :] for h in range(H)], axis=1)
    others = s.cnt.at[pl.ds(0, B - 1)]
    done(to_batch(others, others, 0, sibling))
    seen_part = sum_slots(s.cnt, B) * float(length)
    seen_row = jnp.concatenate([seen_part] * (D // 128), axis=1)
    sums = finish_sum(0, D)
    seen_wide = jnp.concatenate([seen_row] * (F // D), axis=1)

    def moments(first, second, seen):
        mean = first / seen
        return mean, lax.rsqrt(second / seen - mean * mean + EPSILON)

    mean_1, inverse_1 = moments(sums[0], sums[1], seen_row)
    a_1 = gain_1[...] * inverse_1
    b_1 = shift_1[...] - mean_1 * a_1

    G = z.group
    GT = G * T

    def group(ref, i):
        return ref[pl.ds(i * G, G), 0:T].reshape(GT, ref.shape[2])

    def put(ref, i, value):
        ref[pl.ds(i * G, G), 0:T] = value.reshape(G, T, value.shape[1])

    def mask_of(i):
        return jnp.concatenate([s.rowmask[...] * valid_of(i * G + u) for u in range(G)], axis=0)

    def residual_of(i):
        return group(s.xpad, i).astype(f32) + (group(s.proj, i) * a_1 + b_1 * mask_of(i))

    def enter(i, carry):
        first, second = carry
        residual = residual_of(i).astype(bf16)
        hidden = nn(residual, s.upcat[...])
        put(s.hid, i, hidden)
        return first + fold(hidden), second + fold(hidden * hidden)

    first, second = lax.fori_loop(0, n // G, enter, (zeros(F), zeros(F)))
    start_sum(1, [total(first), total(second)])
    others = s.ct.at[pl.ds(0, blocks * (H - 1))]
    done(to_head(others, others, 4, 1))
    c_own.wait()
    for q in range(H):
        enter_cotangent(q)
    sums = finish_sum(1, F)
    mean_2, inverse_2 = moments(sums[0], sums[1], seen_wide)
    a_2 = gain_2w * inverse_2
    b_2 = shift_2w - mean_2 * a_2

    def leave(i, carry):
        one, two, three, four = carry
        shaped = group(s.hid, i) * a_2 + b_2
        gate = sigmoid(shaped)
        active = shaped * gate
        low = active.astype(bf16)
        put(s.act2, i, low)
        outgoing = nn(low, down)
        put(s.out, i, outgoing)
        upstream = group(s.u, i)
        masked = outgoing * mask_of(i)
        return (one + fold(masked), two + fold(masked * outgoing), three + fold(upstream),
                four + fold(upstream * outgoing))

    sums = lax.fori_loop(0, n // G, leave, (zeros(D), zeros(D), zeros(D), zeros(D)))
    start_sum(2, [total(v) for v in sums])

    def slope(i, carry):
        shaped = group(s.hid, i) * a_2 + b_2
        gate = sigmoid(shaped)
        put(s.slope, i, gate + shaped * gate * (1.0 - gate))
        return carry

    lax.fori_loop(0, n // G, slope, 0)
    sums = finish_sum(2, D)
    mean_3, inverse_3 = moments(sums[0], sums[1], seen_row)
    a_3 = gain_3[...] * inverse_3
    b_3 = shift_3[...] - mean_3 * a_3
    sum_shift_3 = sums[2]
    sum_gain_3 = inverse_3 * (sums[3] - mean_3 * sum_shift_3)

    def back(gain, mean, inverse, sum_shift, sum_gain, seen):
        scaled = gain * inverse
        slope = -scaled * inverse * (sum_gain / seen)
        return scaled, slope, -scaled * (sum_shift / seen) - slope * mean

    s_3, v_3, r_3 = back(gain_3[...], mean_3, inverse_3, sum_shift_3, sum_gain_3, seen_row)

    def back_leave(i, carry):
        one, two = carry
        grad = (group(s.u, i) * s_3 + (group(s.out, i) * v_3 + r_3) * mask_of(i)).astype(bf16)
        put(s.gproj, i, grad)
        shaped = nt(grad, down) * group(s.slope, i)
        put(s.slope, i, shaped)
        return one + fold(shaped), two + fold(shaped * group(s.hid, i))

    def down_gradient(i, carry):
        s.gdown[...] += tn(group(s.gproj, i), group(s.act2, i))
        return carry

    def output(i):
        s.tmp[...] = ((residual_of(i) + (group(s.out, i) * a_3 + b_3)) * mask_of(i)).reshape(G, T, D)
        for u in range(G):
            for q in range(H):
                s.osend[q, i * G + u] = s.tmp[u, q * share : (q + 1) * share, :].astype(bf16)

    def early(at, parts):
        for h, part in enumerate(parts):
            s.ge1[h, at : at + part.shape[0], :] = part.astype(bf16)

    def send_early(low, high):
        rows = pl.ds(low, high - low)
        for j in range(1, H):
            to_head(s.ge1.at[head_peers[j], rows], s.ge1r.at[me_h, rows], 7, j).start()

    def send_output(low, high):
        low, high = low * n // 12, high * n // 12
        if high > low:
            to = out_o.at[pl.ds(me_h * n + low, high - low)]
            for j in range(1, H):
                to_head(s.osend.at[head_peers[j], pl.ds(low, high - low)], to, 5, j).start()

    first, second = lax.fori_loop(0, n // G, back_leave, (zeros(F), zeros(F)))
    start_sum(3, [total(first), total(second)])
    output(0)
    send_output(0, 4)
    lax.fori_loop(0, n // G, down_gradient, 0)
    for i in range(1, n // G):
        output(i)
    early(0, [s.gdown[:, h * FH : (h + 1) * FH] for h in range(H)])
    sums = finish_sum(3, F)

    sum_shift_2 = sums[0]
    sum_gain_2 = inverse_2 * (sums[1] - mean_2 * sum_shift_2)
    s_2, v_2, r_2 = back(gain_2w, mean_2, inverse_2, sum_shift_2, sum_gain_2, seen_wide)
    s.srow[0:1, :] = sum_gain_2
    s.srow[1:2, :] = sum_shift_2

    def back_enter(i, carry):
        one, two = carry
        mask = jnp.concatenate([mask_of(i)] * (F // D), axis=1)
        grad = (group(s.slope, i) * s_2 + group(s.hid, i) * v_2 + r_2 * mask).astype(bf16)
        put(s.act2, i, grad)
        upstream = group(s.u, i) + nt(grad, s.upcat[...])
        put(s.u, i, upstream)
        return one + fold(upstream), two + fold(upstream * group(s.proj, i))

    first, second = lax.fori_loop(0, n // G, back_enter, (zeros(D), zeros(D)))
    start_sum(4, [total(first), total(second)])
    send_early(0, D)

    def up_gradient(i, carry):
        s.gup[...] += tn(residual_of(i).astype(bf16), group(s.act2, i))
        return carry

    lax.fori_loop(0, n // G, up_gradient, 0)
    early(D, [s.gup[:, h * FH : (h + 1) * FH] for h in range(H)])
    send_early(D, 2 * D)
    sums = finish_sum(4, D)
    c_out = local(s.osend.at[me_h], out_o.at[pl.ds(me_h * n, n)], 6)
    sum_shift_1 = sums[0]
    sum_gain_1 = inverse_1 * (sums[1] - mean_1 * sum_shift_1)
    s_1, v_1, r_1 = back(gain_1[...], mean_1, inverse_1, sum_shift_1, sum_gain_1, seen_row)

    def back_project(i, carry):
        grad = (group(s.u, i) * s_1 + group(s.proj, i) * v_1 + r_1 * mask_of(i)).astype(bf16)
        put(s.gproj, i, grad)
        whole = s.gpr[...]
        for u in range(G):
            whole = whole + nn(s.act[i * G + u], s.gproj[i * G + u])
        s.gpr[...] = whole
        return carry

    lax.fori_loop(0, n // G, back_project, 0)

    def shares(buffer, k):
        for j in range(1, H):
            to_head(buffer[0].at[head_peers[j]], buffer[1].at[me_h], k, j).start()

    def shares_done(buffer, k):
        done(to_head(buffer[0].at[some], buffer[1].at[some], k, 1))

    def head_sum(buffer):
        whole = buffer[0][me_h].astype(f32)
        for j in range(1, H):
            whole = whole + buffer[1][head_peers[j]].astype(f32)
        return whole

    def spread(src, dst, k):
        around(B, lambda j: to_batch(src(lax.rem(me_b + j, B)), dst, k, lax.rem(me_b + j, B)).start())

    def spread_done(src, dst, k):
        others = pl.ds(0, B - 1)
        done(to_batch(src.at[others], dst.at[others], k, sibling))

    def batch_sum(own, received):
        if B <= 8:
            whole = own
            for j in range(1, B):
                whole = whole + received[lax.rem(me_b + j, B)]
            return whole
        return lax.fori_loop(1, B, lambda j, c: c + received[lax.rem(me_b + j, B)], own)

    for half in range(D // 128):
        lanes = slice(half * 128, (half + 1) * 128)
        early(2 * D + half * PH, [s.gpr[h * PH : (h + 1) * PH, lanes] for h in range(H)])
    filled = 2 * D + D // 128 * PH
    if z.re > filled:
        s.ge1[:, filled:, :] = jnp.zeros((H, z.re - filled, 128), bf16)
    send_early(2 * D, z.re)
    send_output(4, 12)

    GB = z.group_back

    def back_attend(i, carry):
        at = [i * GB + u for u in range(GB)]
        lows, deltas, products = [], [], []
        for j in at:
            att = s.att[j]
            gate = sigmoid(att)
            active = att * gate
            gact = nt(s.projw[...], s.gproj[j]) * (gate + active * (1.0 - gate))
            low, delta = [], []
            for h in range(H):
                rows = slice(h * VAL, (h + 1) * VAL)
                grad = gact[rows] * s.linv[j, h]
                low.append(grad.astype(bf16))
                delta.append(total(grad * att[rows]))
            lows.append(low)
            deltas.append(delta)
            products.append(nn(spaced(s.vnat[j], H), jnp.concatenate(low, axis=0)))
        grads = [[] for _ in at]
        for h in range(H):
            whole = None
            for u, j in enumerate(at):
                gscores = s.p[j, h].astype(f32) * (products[u][h * T : (h + 1) * T] - deltas[u][h])
                whole = gscores if whole is None else whole + gscores
                grads[u].append(gscores.astype(bf16))
            s.dbias[h] += whole
        mixes = []
        for u, j in enumerate(at):
            queries = s.qt[j]
            near = jnp.concatenate(
                [among(queries[h * KEY : (h + 1) * KEY], h * KEY, KH) for h in range(H)], axis=1)
            far = jnp.concatenate([among(lows[u][h], h * VAL, VH) for h in range(H)], axis=1)
            grad_k = nt(jnp.concatenate(grads[u], axis=1), near) * scale
            grad_v = nt(jnp.concatenate([s.p[j, h] for h in range(H)], axis=1), far)
            grad_q = tn(jnp.concatenate(grads[u], axis=0), spaced(s.knat[j], H))[0:T] * scale
            mixes.append(jnp.concatenate([v.astype(bf16) for v in (grad_q, grad_k, grad_v)], axis=1))
        whole = s.gqkv[...]
        for u, j in enumerate(at):
            whole = whole + tn(mixes[u], s.xpad[j, 0:T])
        s.gqkv[...] = whole
        terms = nn(jnp.concatenate(mixes, axis=0), s.w2[...])
        for u, j in enumerate(at):
            s.tmp[u] = s.u[j] + terms[u * T : (u + 1) * T]
            for q in range(H):
                s.tsend[q, j] = s.tmp[u, q * share : (q + 1) * share, :].astype(bf16)
        pl.when(i == 0)(lambda: send_tokens(0))

        @pl.when(i == 1)
        def _():
            shares_done((s.ge1, s.ge1r), 7)
            s.ge2[...] = head_sum((s.ge1, s.ge1r)).reshape(B, z.re // B, 128)
            spread(lambda peer: s.ge2.at[peer], s.ge2r.at[me_b], 3)

        return carry

    def send_tokens(i):
        to = tg_o.at[pl.ds(me_h * n + i * GB, GB)]
        for j in range(1, H):
            to_head(s.tsend.at[head_peers[j], pl.ds(i * GB, GB)], to, 6, j).start()
        pltpu.make_async_copy(s.tsend.at[me_h, pl.ds(i * GB, GB)], to, s.loc.at[7]).start()

    lax.fori_loop(0, n // GB, back_attend, 0)

    for h in range(H):
        for half in range(D // 128):
            lanes = slice(half * 128, (half + 1) * 128)
            at = half * C
            s.gl1[h, at : at + KEY, :] = s.gqkv[h * KEY : (h + 1) * KEY, lanes].astype(bf16)
            s.gl1[h, at + KEY : at + 2 * KEY, :] = s.gqkv[KH + h * KEY : KH + (h + 1) * KEY, lanes].astype(bf16)
            s.gl1[h, at + 2 * KEY : at + C, :] = s.gqkv[2 * KH + h * VAL : 2 * KH + (h + 1) * VAL, lanes].astype(bf16)
        if z.rl > C * (D // 128):
            s.gl1[h, C * (D // 128) :, :] = jnp.zeros((z.rl - C * (D // 128), 128), bf16)
    shares((s.gl1, s.gl1r), 8)
    spread_done(s.ge2, s.ge2r, 3)
    s.ge3[me_b] = batch_sum(s.ge2[me_b], s.ge2r)
    spread(lambda peer: s.ge3.at[me_b], s.ge3.at[me_b], 4)

    slot = lax.broadcasted_iota(jnp.int32, (T, L), 1)
    d_row, d_col = grid_of(slot)
    picks = []
    for down_sign in (1, -1):
        for right_sign in (1, -1):
            r = rows_s + down_sign * d_row
            c = cols_s + right_sign * d_col
            good = (r >= 0) & (r < SIDE) & (c >= 0) & (c < SIDE) & (slot < length)
            if down_sign < 0:
                good = good & (d_row > 0)
            if right_sign < 0:
                good = good & (d_col > 0)
            picks.append((jnp.where(good, r * SIDE + c, 0), good))
    bias_rows = []
    for h in range(H):
        whole = s.dbias[h]
        high = whole.astype(bf16)
        rest = (whole - high.astype(f32)).astype(bf16)
        ordered = nn(high, s.onehot[...]) + nn(rest, s.onehot[...])
        line = jnp.zeros((T, L), f32)
        for index, good in picks:
            line = line + jnp.where(good, take(ordered[:, 0:128], ordered[:, 128:256], index), 0.0)
        bias_rows.append(total(line * s.rowmask[...]))
    start_sum(5, bias_rows)

    for i in range(1, n // GB):
        send_tokens(i)
    shares_done((s.gl1, s.gl1r), 8)
    s.gl2[...] = head_sum((s.gl1, s.gl1r)).reshape(B, z.rl // B, 128)
    spread(lambda peer: s.gl2.at[peer], s.gl2r.at[me_b], 5)
    for h, row in enumerate(finish_sum(5, L)):
        s.brow[h] = row
    spread_done(s.gl2, s.gl2r, 5)
    s.gl3[me_b] = batch_sum(s.gl2[me_b], s.gl2r)
    spread(lambda peer: s.gl3.at[me_b], s.gl3.at[me_b], 6)

    small_o[...] = jnp.zeros(small_o.shape, f32)
    small_o[0:1, :] = sum_gain_1
    small_o[1:2, :] = sum_shift_1
    small_o[2:3, :] = sum_gain_3
    small_o[3:4, :] = sum_shift_3
    small_o[4:5, 0:FH] = s.srow[0:1, own]
    small_o[5:6, 0:FH] = s.srow[1:2, own]
    small_o[6:7, :] = s.brow[me_h]

    spread_done(s.ge3, s.ge3, 4)
    early_o[...] = s.ge3[...].reshape(z.re, 128)
    spread_done(s.gl3, s.gl3, 6)
    late_o[...] = s.gl3[...].reshape(z.rl, 128)

    done(to_head(s.osend.at[some], out_o.at[pl.ds(0, n * (H - 1))], 5, 1))
    done(to_head(s.tsend.at[some], tg_o.at[pl.ds(0, n * (H - 1))], 6, 1))
    c_out.wait()
    pltpu.make_async_copy(s.tsend.at[me_h], tg_o.at[pl.ds(me_h * n, n)], s.loc.at[7]).wait()


def finish_kernel(z, out_i, tg_i, early, late, small, out, tg, qkv, bias, proj, g1, s1, up, g2, s2, down, g3, s3):
    at = lax.broadcasted_iota(jnp.int32, (128, 128), 0)
    to = lax.broadcasted_iota(jnp.int32, (128, 128), 1)
    turn = jnp.where(lax.bitwise_and(at, 7) * 16 + lax.shift_right_logical(at, 3) == to, 1.0, 0.0).astype(bf16)
    whole = z.share // 16 * 16
    for src, dst in ((out_i, out), (tg_i, tg)):
        for i in range(0, src.shape[0], 8):
            for k in range(0, whole, 16):
                rows = src[i : i + 8, k : k + 16, :].reshape(128, z.D)
                dst[k : k + 16, i : i + 8, :] = nn(turn, rows).reshape(16, 8, z.D)
            for k in range(whole, z.share):
                dst[k, i : i + 8, :] = src[i : i + 8, k, :].astype(f32)

    @pl.when(pl.program_id(0) == 0)
    def _():
        D, C, PH = z.D, z.C, z.D // z.H
        down[...] = early[0:D, :].T
        up[...] = early[D : 2 * D, :]
        for half in range(D // 128):
            lanes = slice(half * 128, (half + 1) * 128)
            proj[:, lanes] = early[2 * D + half * PH : 2 * D + (half + 1) * PH, :]
            qkv[0, :, lanes] = late[half * C : (half + 1) * C, :]
        g1[...] = small[0:1, :]
        s1[...] = small[1:2, :]
        g3[...] = small[2:3, :]
        s3[...] = small[3:4, :]
        g2[...] = small[4:5, 0 : z.F // z.H]
        s2[...] = small[5:6, 0 : z.F // z.H]
        bias[...] = small[6:7, 0 : z.length]


def on_device(H, B, tokens, image_count, token_place, qkv_weight, bias_table, proj_weight, attention_gain,
              attention_shift, up_weight, hidden_gain, hidden_shift, down_weight, output_gain, output_shift,
              cotangent):
    images, length, width = tokens.shape
    z = types.SimpleNamespace(
        n=images // H, T=round_up(length, 16), L=round_up(length, 128), D=width, F=up_weight.shape[1] * H,
        H=H, B=B, C=qkv_weight.shape[1], share=cotangent.shape[1], length=length)
    z.re = round_up(2 * z.D + z.D // H * (z.D // 128), 8 * max(B, 2))
    z.rl = round_up(z.C * (z.D // 128), 8 * max(B, 2))
    z.group = max(g for g in (1, 2, 3, 4) if z.n % g == 0)
    z.group_back = max(g for g in (1, 2, 3) if z.n % g == 0)
    z.direct = H == 4 and B <= 8
    z.sums = {}
    for k, r in enumerate((2 * z.D, 2 * z.F, 4 * z.D, 2 * z.F, 2 * z.D, H * z.L)):
        z.sums["sum%d" % k] = pltpu.VMEM((H * B if z.direct else H, r // 128, 128), f32)
        if not z.direct:
            z.sums["part%d" % (k % 2)] = pltpu.VMEM((B, 8, 128), f32)

    def bufs(s, k):
        first = getattr(s, "sum%d" % k)
        return first, None if z.direct else getattr(s, "part%d" % (k % 2)).at[:, 0 : first.shape[1]]

    z.bufs = bufs
    z.vectors = [(length, jnp.int32), (length, f32), (width, f32), (width, f32)]
    z.vectors += [(z.F // H, f32)] * 2 + [(width, f32)] * 2
    scratch = layout(z)
    hbm = pl.BlockSpec(memory_space=pl.ANY)
    vmem = pl.BlockSpec(memory_space=pltpu.VMEM)
    smem = pl.BlockSpec(memory_space=pltpu.SMEM)
    outs = pl.pallas_call(
        functools.partial(block_kernel, z, tuple(scratch)),
        out_shape=(
            jax.ShapeDtypeStruct((images, z.share, width), bf16),
            jax.ShapeDtypeStruct((images, z.share, width), bf16),
            jax.ShapeDtypeStruct((z.re, 128), f32),
            jax.ShapeDtypeStruct((z.rl, 128), f32),
            jax.ShapeDtypeStruct((8, width), f32),
        ),
        in_specs=[hbm, smem] + [hbm] * 13,
        out_specs=(hbm, hbm, vmem, vmem, vmem),
        scratch_shapes=list(scratch.values()),
        compiler_params=pltpu.CompilerParams(
            collective_id=0, has_side_effects=True, vmem_limit_bytes=127 * 512 * 1024
        ),
    )(
        tokens.transpose(1, 0, 2), image_count, token_place.reshape(1, -1), qkv_weight, bias_table, proj_weight,
        attention_gain.reshape(1, -1), attention_shift.reshape(1, -1), up_weight, hidden_gain.reshape(1, -1),
        hidden_shift.reshape(1, -1), down_weight, output_gain.reshape(1, -1), output_shift.reshape(1, -1),
        cotangent.transpose(1, 0, 2),
    )

    steps = 2
    block = pl.BlockSpec((images // steps, z.share, width), lambda i: (i, 0, 0))
    turned = pl.BlockSpec((z.share, images // steps, width), lambda i: (0, i, 0))

    def whole(*shape):
        return jax.ShapeDtypeStruct(shape, f32), pl.BlockSpec(shape, lambda i: (0,) * len(shape))

    fh = z.F // H
    small = [
        whole(1, z.C, width), whole(1, length), whole(width // H, width), whole(1, width), whole(1, width),
        whole(width, fh), whole(1, fh), whole(1, fh), whole(fh, width), whole(1, width), whole(1, width)]
    big = jax.ShapeDtypeStruct((z.share, images, width), f32)
    res = pl.pallas_call(
        functools.partial(finish_kernel, z),
        grid=(steps,),
        out_shape=[big, big] + [a for a, _ in small],
        in_specs=[block, block, whole(z.re, 128)[1], whole(z.rl, 128)[1], whole(8, width)[1]],
        out_specs=[turned, turned] + [b for _, b in small],
        compiler_params=pltpu.CompilerParams(vmem_limit_bytes=127 * 512 * 1024),
    )(*outs)
    res = [res[0].transpose(1, 0, 2), res[1].transpose(1, 0, 2), *res[2:]]
    for k in (5, 6, 8, 9, 11, 12):
        res[k] = res[k].reshape(-1)
    return tuple(res)


def solution(mesh):
    H, B = mesh.shape["head"], mesh.shape["batch"]
    placed = (
        P("batch", None, None),
        P("batch"),
        P(),
        P("head", None, None),
        P("head", None),
        P(),
        P(),
        P(),
        P(None, "head"),
        P("head"),
        P("head"),
        P("head", None),
        P(),
        P(),
        P("batch", "head", None),
    )
    return jax.shard_map(
        functools.partial(on_device, H, B),
        mesh=mesh,
        in_specs=placed,
        out_specs=(
            P("batch", "head", None),
            P("batch", "head", None),
            P("head", None, None),
            P("head", None),
            P("head", None),
            P(),
            P(),
            P(None, "head"),
            P("head"),
            P("head"),
            P("head", None),
            P(),
            P(),
        ),
        check_vma=False,
    )
```
